128 devices in a mesh: grp: 4 (over z_lo, core), dev: 32 (over y, x, z_hi).
Axes of the slice: x: 4, y: 4, z: 4 (z_hi: 2, z_lo: 2; z = z_hi * 2 + z_lo), core: 2. Of those that a mesh axis runs over, the one named last changes fastest.
Arguments:
- embeds: bfloat16 [32768, 512], P(('grp', 'dev')), may hold values from -0.19921875 to 0.19921875
- partner: int32 [32768], P(('grp', 'dev')), may hold values from 0 to 32767, as said below
Outputs:
- loss: float32 [], replicated
- grad: float32 [32768, 512], P(('grp', 'dev'))
The draws below stay inside these ranges and needn't reach their ends.
Inputs may be any that keep to these rules, and one draw needn't show every extreme that they name: partner pairs the views: partner[partner[i]] == i and partner[i] != i for every view i, and partner[i] lies in the same aligned block of 256 views as i.
All inputs are finite; a program needn't handle non-finite values.
Results may differ from the reference program's by a relative error of at most 0.0031.
Values may be sent and summed in bfloat16 or wider, within the bound.
No kernel may reach another device: no remote copies, remote signals or barrier semaphores. Data moves between devices by JAX's collectives and lax.ppermute only.
A program may use at most 128 MiB of HBM per device.

```python
import math
import jax
import jax.numpy as jnp
from jax import lax

E = 512
VIEWS_DEV = 256
VIEWS = 32768


def pairing(key):
    key = jax.random.fold_in(key, 5)
    blocks = VIEWS // VIEWS_DEV
    keys = jax.random.split(key, blocks)
    local = jax.vmap(lambda k: jax.random.permutation(k, VIEWS_DEV))(keys)
    offsets = (jnp.arange(blocks, dtype=jnp.int32) * VIEWS_DEV)[:, None]
    order = (local.astype(jnp.int32) + offsets).reshape(-1)
    swapped = order.reshape(-1, 2)[:, ::-1].reshape(-1)
    return jnp.zeros((VIEWS,), jnp.int32).at[order].set(swapped)


def draw_partner(key, part):
    return pairing(key)


def draw_embeds(key, part):
    mates = pairing(key)
    key = jax.random.fold_in(key, 11)
    key_first, key_second, key_centre, key_tight, key_jitter, key_shared = jax.random.split(key, 6)
    cluster_a = jax.random.randint(key_first, (VIEWS,), 0, 64)
    cluster_b = jax.random.randint(key_second, (VIEWS,), 1, 65)
    member_of = cluster_a * cluster_b // 64
    centres = jax.random.normal(key_centre, (64, E), jnp.float32)
    pair_low = jnp.minimum(jnp.arange(VIEWS, dtype=jnp.int32), mates)
    ramp = pair_low.astype(jnp.float32) / VIEWS
    tightness = jax.random.uniform(key_tight, (64,), jnp.float32, 0.0, 0.9)
    jitter = jax.random.normal(key_jitter, (VIEWS, E), jnp.float32)
    pull = 0.1 + 0.88 * ramp
    shared = jax.random.normal(key_shared, (VIEWS, E), jnp.float32)[pair_low]
    pulled = tightness[member_of][:, None]
    blended = pulled * centres[member_of] + jnp.sqrt(1.0 - pulled * pulled) * jitter
    pull = pull[:, None]
    mixed = pull * shared + jnp.sqrt(1.0 - pull * pull) * blended
    return jnp.clip(0.03125 * mixed, -0.19921875, 0.19921875).astype(jnp.bfloat16)


def setup_inputs(seed: int = 0) -> dict:
    key_of = jax.random.split(jax.random.key(seed), 3)
    embeds = draw_embeds(jax.random.fold_in(key_of[2], 71), 0)
    partner = draw_partner(jax.random.fold_in(key_of[2], 71), 0)
    return dict(embeds=embeds, partner=partner)


INV_TAU = 10.0

def reference(embeds, partner):
    zf = embeds.astype(jnp.float32)
    recip = lax.rsqrt(lax.optimization_barrier(jnp.sum(zf * zf, axis=1, keepdims=True)) + 1e-06)
    unit = zf * recip
    unit_b = unit.astype(jnp.bfloat16)
    block = math.gcd(VIEWS, 1024)
    count = VIEWS // block
    starts = jnp.arange(count, dtype=jnp.int32) * block
    col_ids = jnp.arange(VIEWS, dtype=jnp.int32)

    def block_lse(start):
        rows = lax.dynamic_slice_in_dim(unit_b, start, block, 0)
        s = jnp.dot(rows, unit_b.T, preferred_element_type=jnp.float32) * INV_TAU
        row_ids = start + jnp.arange(block, dtype=jnp.int32)
        off = col_ids[None, :] != row_ids[:, None]
        total = lax.optimization_barrier(jnp.sum(jnp.where(off, jnp.exp(s - INV_TAU), 0.0), axis=1))
        return INV_TAU + jnp.log(total)
    lse = lax.map(block_lse, starts).reshape(VIEWS)
    mates = unit_b[partner].astype(jnp.float32)
    positive = lax.optimization_barrier(jnp.sum(unit_b.astype(jnp.float32) * mates, axis=1)) * INV_TAU
    loss = jnp.mean(lse - positive)

    def block_grad(start):
        rows = lax.dynamic_slice_in_dim(unit_b, start, block, 0)
        row_lse = lax.dynamic_slice_in_dim(lse, start, block, 0)
        s = jnp.dot(rows, unit_b.T, preferred_element_type=jnp.float32) * INV_TAU
        row_ids = start + jnp.arange(block, dtype=jnp.int32)
        off = col_ids[None, :] != row_ids[:, None]
        w = jnp.where(off, jnp.exp(s - row_lse[:, None]) + jnp.exp(s - lse[None, :]), 0.0).astype(jnp.bfloat16)
        return jnp.dot(w, unit_b, preferred_element_type=jnp.float32)
    acc = lax.map(block_grad, starts).reshape(VIEWS, E)
    grad_unit = INV_TAU * (acc - 2.0 * mates)
    grad = recip * (grad_unit - unit * lax.optimization_barrier(jnp.sum(unit * grad_unit, axis=1, keepdims=True)))
    return (loss, grad)
```

```python
import functools
import math

import jax
import jax.numpy as jnp
from jax import lax
from jax.experimental import pallas as pl
from jax.experimental.pallas import tpu as pltpu
from jax.sharding import Mesh, PartitionSpec as P

INV_TAU = 10.0
EXP_SCALE = INV_TAU * math.log2(math.e)
AXES = ("zlo", "core", "y", "x", "zhi")
SIZES = (2, 2, 4, 4, 2)
OFFSETS = (0, -1, 1, 2)
Z_OFFSETS = (0, 1, 3, 2)
NT = (((1,), (1,)), ((), ()))
NN = (((1,), (0,)), ((), ()))
ROWS = 256
ALL_ROWS = 2048
COLS = 4096
TILE = 512
NEAR_ROWS = 768
MIB = 1024 * 1024
E = 512
BF16 = jnp.bfloat16
F32 = jnp.float32


def place(x, y, z, core):
    return ((((z % 2) * 2 + core) * 4 + y) * 4 + x) * 2 + z // 2


def get(value, z=0, core=0, first=0, second=0, z_own=0):
    pairs = []
    for px in range(4):
        for py in range(4):
            for pz in range(4):
                for pc in range(2):
                    x, y = (first, second) if pc == 0 else (second, first)
                    away = z + (z_own if pc == 0 else -z_own)
                    source = place((px + x) % 4, (py + y) % 4, (pz + away) % 4, pc ^ core)
                    pairs.append((source, place(px, py, pz, pc)))
    return lax.ppermute(value, AXES, pairs)


def ring_sum(own, before, after, far):
    return (own + far) + (before + after)


def after(value, *others):
    return lax.optimization_barrier((value, *others))[0]


def vmem():
    return pl.BlockSpec(memory_space=pltpu.VMEM)


def smem():
    return pl.BlockSpec(memory_space=pltpu.SMEM)


def hbm():
    return pl.BlockSpec(memory_space=pltpu.HBM)


def params(mib):
    return pltpu.CompilerParams(vmem_limit_bytes=mib * MIB)


def block_of(z, core):
    return ((z & 1) * 2 + core) * 2 + lax.shift_right_logical(z, 1)


def unit_kernel(z_ref, unit_ref):
    zf = z_ref[...].astype(F32)
    recip = lax.rsqrt(jnp.sum(zf * zf, axis=1, keepdims=True) + 1e-06)
    unit_ref[...] = (zf * recip).astype(BF16)


def make_unit(embeds):
    return pl.pallas_call(
        unit_kernel,
        out_shape=jax.ShapeDtypeStruct((ROWS, E), BF16),
        in_specs=[vmem()],
        out_specs=vmem(),
        compiler_params=params(4),
        name="unit",
    )(embeds)


def mates_kernel(unit_ref, partner_ref, mates_ref, positive_ref):
    unit = unit_ref[...]
    ids = lax.broadcasted_iota(jnp.int32, (ROWS, ROWS), 0)
    pick = (ids == (partner_ref[...] & (ROWS - 1))).astype(F32).astype(BF16)
    mates = lax.dot_general(pick, unit, NN, preferred_element_type=F32)
    mates_ref[...] = mates.astype(BF16)
    products = jnp.sum(unit.astype(F32) * mates, axis=0, keepdims=True)
    total = jnp.sum(products, axis=1, keepdims=True) * INV_TAU
    positive_ref[...] = jnp.broadcast_to(total, (1, 128))


def make_mates(unit, partner):
    return pl.pallas_call(
        mates_kernel,
        out_shape=(
            jax.ShapeDtypeStruct((ROWS, E), BF16),
            jax.ShapeDtypeStruct((1, 128), F32),
        ),
        in_specs=[vmem(), vmem()],
        out_specs=(vmem(), vmem()),
        compiler_params=params(4),
        name="mates",
    )(unit, partner.reshape(1, ROWS))


def exps_kernel(places, olds, first, last, *refs):
    count = len(places)
    near, far = ((0, NEAR_ROWS), (1024, 1024 + NEAR_ROWS)), ((NEAR_ROWS, 1024), (1024 + NEAR_ROWS, 2048))
    info_ref, refs = refs[0], refs[1:]
    row_refs, refs = (refs[:2], refs[2:]) if first else (refs[:4], refs[4:])
    col_refs, refs = refs[:count], refs[count:]
    if not first:
        before_ref, refs = refs[0], refs[3:]
    if last:
        positive_ref, refs = refs[0], refs[1:]
    sums_ref, exps_ref, unit_ref, rows, sums, line = refs
    for ref, (start, stop) in zip(row_refs, near + far):
        rows[start:stop] = ref[...]
    sums[...] = jnp.zeros_like(sums) if first else before_ref[...]
    for n, col_ref in enumerate(col_refs):
        if n in olds:
            ranges = far
        else:
            ranges = near if first else ((0, 1024), (1024, 2048))
            start = places[n] * TILE
            unit_ref[start : start + col_ref.shape[0]] = col_ref[...]

        @pl.loop(0, col_ref.shape[0] // ROWS)
        def _(m):
            here = pl.ds(pl.multiple_of(places[n] * TILE + m * ROWS, ROWS), ROWS)
            cols = col_ref[pl.ds(pl.multiple_of(m * ROWS, ROWS), ROWS), :]
            for start, stop in ranges:
                s = lax.dot_general(rows[start:stop], cols, NT, preferred_element_type=F32)
                e = jnp.exp2(s * EXP_SCALE)
                if first and start == 0:
                    i = lax.broadcasted_iota(jnp.int32, (ROWS, ROWS), 0)
                    j = lax.broadcasted_iota(jnp.int32, (ROWS, ROWS), 1)
                    own = jnp.where(i == j + m * ROWS, 0.0, e[:ROWS])
                    e = jnp.concatenate([own, e[ROWS:]], axis=0)
                exps_ref[start:stop, here] = e.astype(BF16)
                sums[start:stop] += e[:, :128] + e[:, 128:]

    if last:
        totals = jnp.sum(sums[...].T, axis=0, keepdims=True)
        line[...] = jnp.zeros_like(line)
        for c in range(2):
            for k in range(4):
                n = c * 4 + k
                at = block_of((info_ref[2] + Z_OFFSETS[k]) & 3, info_ref[3] ^ c)
                line[pl.ds(at, 1), :] = totals[:, n * ROWS : (n + 1) * ROWS]
        line[8:9, 0:128] = positive_ref[...]
        sums_ref[...] = line[...]
    else:
        sums_ref[...] = sums[...]


def make_exps(info, rows, cols, places, olds, chain, positive, name):
    first, last = chain is None, positive is not None
    count = len(cols)
    tiles = sum(c.shape[0] for c in cols) // TILE
    sums_shape = (16, ROWS) if last else (ALL_ROWS, 128)
    operands = [info, *rows, *cols] + ([] if first else list(chain)) + ([positive] if last else [])
    return pl.pallas_call(
        functools.partial(exps_kernel, places, olds, first, last),
        out_shape=(
            jax.ShapeDtypeStruct(sums_shape, F32),
            pltpu.VMEM((ALL_ROWS, COLS), BF16),
            pltpu.VMEM((COLS, E), BF16),
        ),
        in_specs=[smem()] + [vmem()] * (len(operands) - 1),
        out_specs=(vmem(), vmem(), vmem()),
        input_output_aliases={} if first else {6 + count: 1, 7 + count: 2},
        scratch_shapes=[
            pltpu.VMEM((ALL_ROWS, E), BF16),
            pltpu.VMEM((ALL_ROWS, 128), F32),
            pltpu.VMEM((16, ROWS), F32),
        ],
        compiler_params=params(12),
        cost_estimate=pl.CostEstimate(
            flops=2 * ALL_ROWS * tiles * TILE * E,
            bytes_accessed=tiles * TILE * E * 2,
            transcendentals=ALL_ROWS * tiles * TILE,
        ),
        name=name,
    )(*operands)


def totals_kernel(info_ref, own_ref, before_ref, after_ref, far_ref, arow_ref, message_ref, recips):
    both = ring_sum(own_ref[...], before_ref[...], after_ref[...], far_ref[...])
    total = both[:8]
    recips[...] = 1.0 / total
    logs = jnp.sum(jnp.sum(jnp.log(total), axis=0, keepdims=True), axis=1, keepdims=True)
    loss = jnp.broadcast_to(logs, (1, 128)) - both[8:9, :128]
    for c in range(2):
        for k in range(4):
            n = c * 4 + k
            at = block_of((info_ref[2] + Z_OFFSETS[k]) & 3, info_ref[3] ^ c)
            line = recips[pl.ds(at, 1), :]
            arow_ref[n * ROWS : (n + 1) * ROWS] = jnp.broadcast_to(line, (128, ROWS)).T.astype(BF16)
    own = recips[pl.ds(block_of(info_ref[2], info_ref[3]), 1), :]
    zeros = jnp.zeros((5, 128), F32)
    message_ref[...] = jnp.concatenate([own[:, :128], own[:, 128:], loss, zeros], axis=0)


def make_totals(info, own, before, after, far):
    return pl.pallas_call(
        totals_kernel,
        out_shape=(
            jax.ShapeDtypeStruct((ALL_ROWS, 128), BF16),
            jax.ShapeDtypeStruct((8, 128), F32),
        ),
        in_specs=[smem()] + [vmem()] * 4,
        out_specs=(vmem(), vmem()),
        scratch_shapes=[pltpu.VMEM((8, ROWS), F32)],
        compiler_params=params(4),
        name="totals",
    )(info, own, before, after, far)


def grads_kernel(first, count, adds, info_ref, plane_ref, arow_ref, exps_ref, unit_ref, *refs):
    if adds:
        add_ref, refs = refs[0], refs[1:]
    (out_ref,) = refs
    size = min(count, 512)
    cols = [plane_ref[8 * (g // 2) + g % 2 : 8 * (g // 2) + g % 2 + 1].astype(BF16) for g in range(COLS // 128)]

    @pl.loop(0, count // size)
    def _(r):
        here = pl.ds(pl.multiple_of(first + r * size, ROWS), size)
        a = arow_ref[here]
        w = exps_ref[here] * jnp.concatenate([a + col for col in cols], axis=1)
        product = lax.dot_general(w, unit_ref[...], NN, preferred_element_type=F32)
        if adds:
            product += add_ref[here].astype(F32)
        out_ref[pl.ds(pl.multiple_of(r * size, size), size)] = product.astype(out_ref.dtype)


def make_grads(first, count, dtype, info, plane, arow, exps, unit, add, name):
    adds = add is not None
    exps = pltpu.with_memory_space_constraint(exps, pltpu.VMEM)
    unit = pltpu.with_memory_space_constraint(unit, pltpu.VMEM)
    return pl.pallas_call(
        functools.partial(grads_kernel, first, count, adds),
        out_shape=jax.ShapeDtypeStruct((count, E), dtype),
        in_specs=[smem()] + [vmem()] * (5 if adds else 4),
        out_specs=vmem(),
        compiler_params=params(16),
        cost_estimate=pl.CostEstimate(
            flops=2 * count * COLS * E,
            bytes_accessed=COLS * (count + E) * 2,
            transcendentals=0,
        ),
        name=name,
    )(info, plane, arow, exps, unit, *([add] if adds else []))


def far_kernel(raw_ref, core_ref, out_ref):
    out_ref[...] = (raw_ref[...] + core_ref[NEAR_ROWS:].astype(F32)).astype(BF16)


def make_far(raw, core):
    return pl.pallas_call(
        far_kernel,
        out_shape=jax.ShapeDtypeStruct((ROWS, E), BF16),
        in_specs=[vmem(), vmem()],
        out_specs=vmem(),
        compiler_params=params(4),
        name="far",
    )(raw, core)


def near_kernel(info_ref, raw_ref, far_ref, up_ref, down_ref):
    far = far_ref[...].astype(F32)
    zero = jnp.zeros_like(far)
    up_ref[...] = (raw_ref[:ROWS] + jnp.where(info_ref[3] == 0, far, zero)).astype(BF16)
    down_ref[...] = (raw_ref[ROWS:] + jnp.where(info_ref[3] == 0, zero, far)).astype(BF16)


def make_near(info, raw, far):
    return pl.pallas_call(
        near_kernel,
        out_shape=(jax.ShapeDtypeStruct((ROWS, E), BF16), jax.ShapeDtypeStruct((ROWS, E), BF16)),
        in_specs=[smem(), vmem(), vmem()],
        out_specs=(vmem(), vmem()),
        compiler_params=params(4),
        name="near",
    )(info, raw, far)


def final_kernel(info_ref, z_ref, mates_ref, own_ref, below_ref, above_ref, plane_ref, grad_ref, loss_ref):
    zf = z_ref[...].astype(F32)
    recip = lax.rsqrt(jnp.sum(zf * zf, axis=1, keepdims=True) + 1e-06)
    unit = zf * recip
    acc = own_ref[...] + below_ref[...].astype(F32) + above_ref[...].astype(F32)
    grad_unit = INV_TAU * (acc - 2.0 * mates_ref[...].astype(F32))
    along = jnp.sum(unit * grad_unit, axis=1, keepdims=True)
    grad_ref[...] = recip * (grad_unit - unit * along)
    parts = [[plane_ref[8 * n + 2 : 8 * n + 3] for n in range(4 * m, 4 * m + 4)] for m in range(4)]
    x_first = ring_sum(*[ring_sum(*line) for line in parts])
    y_first = ring_sum(*[ring_sum(*line) for line in zip(*parts)])
    loss = jnp.where(info_ref[3] == 0, x_first, y_first)
    loss_ref[...] = loss[:, :1] / (ROWS * 128)


def make_final(info, embeds, mates, own, below, above, plane):
    return pl.pallas_call(
        final_kernel,
        out_shape=(jax.ShapeDtypeStruct((ROWS, E), F32), jax.ShapeDtypeStruct((1, 1), F32)),
        in_specs=[smem()] + [vmem()] * 6,
        out_specs=(vmem(), vmem()),
        compiler_params=params(4),
        name="final",
    )(info, embeds, mates, own, below, above, plane)


def per_device(embeds, partner):
    unit = make_unit(embeds)
    core_id = lax.axis_index("core")
    z = lax.axis_index("zhi") * 2 + lax.axis_index("zlo")
    info = jnp.stack([lax.axis_index("x"), lax.axis_index("y"), z, core_id]).astype(jnp.int32)

    before, next_ = get(unit, first=-1), get(unit, first=1)
    z_before, z_after = get(unit, z=-1), get(unit, z=1)
    before, next_ = lax.optimization_barrier((before, next_))
    far = get(before, first=-1)
    line = jnp.concatenate([unit, before, next_, far], axis=0)
    line_before, line_after = get(line, second=-1), get(line, second=1)
    near = jnp.concatenate([after(unit, far), z_after, z_before], axis=0)
    near = [near, get(near, core=1)]
    z_far = get(jnp.where(core_id == 0, after(z_before, line), after(z_after, line)), z_own=-1)

    mates, positive = make_mates(unit, partner)
    chain = make_exps(info, near, [line], (0,), (), None, None, "exps0")
    far0 = get(after(line_before, line_after, chain[0])[: 2 * ROWS], second=-1)
    far1 = get(after(line_after, line_before, chain[0])[2 * ROWS :], second=1)
    rows = near + [z_far, get(after(z_far, chain[0]), core=1)]
    chain = make_exps(info, rows, [line, line_before, line_after], (0, 2, 4), (0,), chain, None, "exps1")
    sums, exps, units = make_exps(info, rows, [far0, far1], (6, 7), (), chain, positive, "exps2")

    sums = sums + get(sums, core=1)
    arow, plane = make_totals(info, sums, get(sums, z=-1), get(sums, z=1), get(sums, z=2))
    plane = jnp.concatenate([plane] + [get(plane, first=k) for k in OFFSETS[1:]], axis=0)
    plane = jnp.concatenate([plane] + [get(plane, second=k) for k in OFFSETS[1:]], axis=0)

    theirs = make_grads(1024, 1024, BF16, info, plane, arow, exps, units, None, "grads_core")
    core = get(theirs, core=1)
    raw = make_grads(NEAR_ROWS, ROWS, F32, after(info, theirs), plane, arow, exps, units, None, "grads_far")
    far = make_far(raw, core)
    passed = get(far, z_own=-1)
    raw = make_grads(ROWS, 2 * ROWS, F32, after(info, far), plane, arow, exps, units, core, "grads_near")
    up, down = make_near(info, raw, passed)
    below, above = get(up, z=-1), get(down, z=1)
    own = make_grads(0, ROWS, F32, after(info, up), plane, arow, exps, units, core, "grads_own")
    grad, loss = make_final(info, embeds, mates, own, below, above, plane)
    return (loss[0, 0], grad)


def solution(mesh):
    torus = Mesh(mesh.devices.reshape(SIZES), AXES)
    return jax.shard_map(
        per_device,
        mesh=torus,
        in_specs=(P(AXES, None), P(AXES)),
        out_specs=(P(), P(AXES, None)),
        check_vma=False,
    )
```

```python
import functools
import math

import jax
import jax.numpy as jnp
from jax import lax
from jax.experimental import pallas as pl
from jax.experimental.pallas import tpu as pltpu
from jax.sharding import Mesh, PartitionSpec as P

INV_TAU = 10.0
EXP_SCALE = INV_TAU * math.log2(math.e)
AXES = ("zlo", "core", "y", "x", "zhi")
SIZES = (2, 2, 4, 4, 2)
OFFSETS = (0, -1, 1, 2)
Z_OFFSETS = (0, 1, 3, 2)
NT = (((1,), (1,)), ((), ()))
NN = (((1,), (0,)), ((), ()))
ROWS = 256
ALL_ROWS = 2048
COLS = 4096
TILE = 512
NEAR_ROWS = 768
MIB = 1024 * 1024
E = 512
BF16 = jnp.bfloat16
F32 = jnp.float32


def place(x, y, z, core):
    return ((((z % 2) * 2 + core) * 4 + y) * 4 + x) * 2 + z // 2


def get(value, z=0, core=0, first=0, second=0, z_own=0):
    pairs = []
    for px in range(4):
        for py in range(4):
            for pz in range(4):
                for pc in range(2):
                    x, y = (first, second) if pc == 0 else (second, first)
                    away = z + (z_own if pc == 0 else -z_own)
                    source = place((px + x) % 4, (py + y) % 4, (pz + away) % 4, pc ^ core)
                    pairs.append((source, place(px, py, pz, pc)))
    return lax.ppermute(value, AXES, pairs)


def ring_sum(own, before, after, far):
    return (own + far) + (before + after)


def after(value, *others):
    return lax.optimization_barrier((value, *others))[0]


def vmem():
    return pl.BlockSpec(memory_space=pltpu.VMEM)


def smem():
    return pl.BlockSpec(memory_space=pltpu.SMEM)


def hbm():
    return pl.BlockSpec(memory_space=pltpu.HBM)


def params(mib):
    return pltpu.CompilerParams(vmem_limit_bytes=mib * MIB)


def block_of(z, core):
    return ((z & 1) * 2 + core) * 2 + lax.shift_right_logical(z, 1)


def unit_kernel(z_ref, unit_ref):
    zf = z_ref[...].astype(F32)
    recip = lax.rsqrt(jnp.sum(zf * zf, axis=1, keepdims=True) + 1e-06)
    unit_ref[...] = (zf * recip).astype(BF16)


def make_unit(embeds):
    return pl.pallas_call(
        unit_kernel,
        out_shape=jax.ShapeDtypeStruct((ROWS, E), BF16),
        in_specs=[vmem()],
        out_specs=vmem(),
        compiler_params=params(4),
        name="unit",
    )(embeds)


def mates_kernel(unit_ref, partner_ref, mates_ref, positive_ref):
    unit = unit_ref[...]
    ids = lax.broadcasted_iota(jnp.int32, (ROWS, ROWS), 0)
    pick = (ids == (partner_ref[...] & (ROWS - 1))).astype(F32).astype(BF16)
    mates = lax.dot_general(pick, unit, NN, preferred_element_type=F32)
    mates_ref[...] = mates.astype(BF16)
    products = jnp.sum(unit.astype(F32) * mates, axis=0, keepdims=True)
    total = jnp.sum(products, axis=1, keepdims=True) * INV_TAU
    positive_ref[...] = jnp.broadcast_to(total, (1, 128))


def make_mates(unit, partner):
    return pl.pallas_call(
        mates_kernel,
        out_shape=(
            jax.ShapeDtypeStruct((ROWS, E), BF16),
            jax.ShapeDtypeStruct((1, 128), F32),
        ),
        in_specs=[vmem(), vmem()],
        out_specs=(vmem(), vmem()),
        compiler_params=params(4),
        name="mates",
    )(unit, partner.reshape(1, ROWS))


def exps_kernel(places, olds, first, last, *refs):
    count = len(places)
    near, far = ((0, NEAR_ROWS), (1024, 1024 + NEAR_ROWS)), ((NEAR_ROWS, 1024), (1024 + NEAR_ROWS, 2048))
    info_ref, refs = refs[0], refs[1:]
    row_refs, refs = (refs[:2], refs[2:]) if first else (refs[:4], refs[4:])
    col_refs, refs = refs[:count], refs[count:]
    if not first:
        before_ref, refs = refs[0], refs[3:]
    if last:
        positive_ref, refs = refs[0], refs[1:]
    sums_ref, exps_ref, unit_ref, rows, sums, line = refs
    for ref, (start, stop) in zip(row_refs, near + far):
        rows[start:stop] = ref[...]
    sums[...] = jnp.zeros_like(sums) if first else before_ref[...]
    for n, col_ref in enumerate(col_refs):
        if n in olds:
            ranges = far
        else:
            ranges = near if first else ((0, 1024), (1024, 2048))
            start = places[n] * TILE
            unit_ref[start : start + col_ref.shape[0]] = col_ref[...]

        @pl.loop(0, col_ref.shape[0] // ROWS)
        def _(m):
            here = pl.ds(pl.multiple_of(places[n] * TILE + m * ROWS, ROWS), ROWS)
            cols = col_ref[pl.ds(pl.multiple_of(m * ROWS, ROWS), ROWS), :]
            for start, stop in ranges:
                s = lax.dot_general(rows[start:stop], cols, NT, preferred_element_type=F32)
                e = jnp.exp2(s * EXP_SCALE)
                if first and n == 0 and start == 0:
                    i = lax.broadcasted_iota(jnp.int32, (ROWS, ROWS), 0)
                    j = lax.broadcasted_iota(jnp.int32, (ROWS, ROWS), 1)
                    own = jnp.where(i == j + m * ROWS, 0.0, e[:ROWS])
                    e = jnp.concatenate([own, e[ROWS:]], axis=0)
                exps_ref[start:stop, here] = e.astype(BF16)
                sums[start:stop] += e[:, :128] + e[:, 128:]

    if last:
        totals = jnp.sum(sums[...].T, axis=0, keepdims=True)
        line[...] = jnp.zeros_like(line)
        for c in range(2):
            for k in range(4):
                n = c * 4 + k
                at = block_of((info_ref[2] + Z_OFFSETS[k]) & 3, info_ref[3] ^ c)
                line[pl.ds(at, 1), :] = totals[:, n * ROWS : (n + 1) * ROWS]
        line[8:9, 0:128] = positive_ref[...]
        sums_ref[...] = line[...]
    else:
        sums_ref[...] = sums[...]


def make_exps(info, rows, cols, places, olds, chain, positive, name):
    first, last = chain is None, positive is not None
    count = len(cols)
    tiles = sum(c.shape[0] for c in cols) // TILE
    sums_shape = (16, ROWS) if last else (ALL_ROWS, 128)
    operands = [info, *rows, *cols] + ([] if first else list(chain)) + ([positive] if last else [])
    return pl.pallas_call(
        functools.partial(exps_kernel, places, olds, first, last),
        out_shape=(
            jax.ShapeDtypeStruct(sums_shape, F32),
            pltpu.VMEM((ALL_ROWS, COLS), BF16),
            pltpu.VMEM((COLS, E), BF16),
        ),
        in_specs=[smem()] + [vmem()] * (len(operands) - 1),
        out_specs=(vmem(), vmem(), vmem()),
        input_output_aliases={} if first else {6 + count: 1, 7 + count: 2},
        scratch_shapes=[
            pltpu.VMEM((ALL_ROWS, E), BF16),
            pltpu.VMEM((ALL_ROWS, 128), F32),
            pltpu.VMEM((16, ROWS), F32),
        ],
        compiler_params=params(12),
        cost_estimate=pl.CostEstimate(
            flops=2 * ALL_ROWS * tiles * TILE * E,
            bytes_accessed=tiles * TILE * E * 2,
            transcendentals=ALL_ROWS * tiles * TILE,
        ),
        name=name,
    )(*operands)


def totals_kernel(info_ref, own_ref, before_ref, after_ref, far_ref, arow_ref, message_ref, recips):
    both = ring_sum(own_ref[...], before_ref[...], after_ref[...], far_ref[...])
    total = both[:8]
    recips[...] = 1.0 / total
    logs = jnp.sum(jnp.sum(jnp.log(total), axis=0, keepdims=True), axis=1, keepdims=True)
    loss = jnp.broadcast_to(logs, (1, 128)) - both[8:9, :128]
    for c in range(2):
        for k in range(4):
            n = c * 4 + k
            at = block_of((info_ref[2] + Z_OFFSETS[k]) & 3, info_ref[3] ^ c)
            line = recips[pl.ds(at, 1), :]
            arow_ref[n * ROWS : (n + 1) * ROWS] = jnp.broadcast_to(line, (128, ROWS)).T.astype(BF16)
    own = recips[pl.ds(block_of(info_ref[2], info_ref[3]), 1), :]
    zeros = jnp.zeros((5, 128), F32)
    message_ref[...] = jnp.concatenate([own[:, :128], own[:, 128:], loss, zeros], axis=0)


def make_totals(info, own, before, after, far):
    return pl.pallas_call(
        totals_kernel,
        out_shape=(
            jax.ShapeDtypeStruct((ALL_ROWS, 128), BF16),
            jax.ShapeDtypeStruct((8, 128), F32),
        ),
        in_specs=[smem()] + [vmem()] * 4,
        out_specs=(vmem(), vmem()),
        scratch_shapes=[pltpu.VMEM((8, ROWS), F32)],
        compiler_params=params(4),
        name="totals",
    )(info, own, before, after, far)


def grads_kernel(first, count, adds, info_ref, plane_ref, arow_ref, exps_ref, unit_ref, *refs):
    if adds:
        add_ref, refs = refs[0], refs[1:]
    (out_ref,) = refs
    size = min(count, 512)
    cols = [plane_ref[8 * (g // 2) + g % 2 : 8 * (g // 2) + g % 2 + 1].astype(BF16) for g in range(COLS // 128)]

    @pl.loop(0, count // size)
    def _(r):
        here = pl.ds(pl.multiple_of(first + r * size, ROWS), size)
        a = arow_ref[here]
        w = exps_ref[here] * jnp.concatenate([a + col for col in cols], axis=1)
        product = lax.dot_general(w, unit_ref[...], NN, preferred_element_type=F32)
        if adds:
            product += add_ref[here].astype(F32)
        out_ref[pl.ds(pl.multiple_of(r * size, size), size)] = product.astype(out_ref.dtype)


def make_grads(first, count, dtype, info, plane, arow, exps, unit, add, name):
    adds = add is not None
    exps = pltpu.with_memory_space_constraint(exps, pltpu.VMEM)
    unit = pltpu.with_memory_space_constraint(unit, pltpu.VMEM)
    return pl.pallas_call(
        functools.partial(grads_kernel, first, count, adds),
        out_shape=jax.ShapeDtypeStruct((count, E), dtype),
        in_specs=[smem()] + [vmem()] * (5 if adds else 4),
        out_specs=vmem(),
        compiler_params=params(16),
        cost_estimate=pl.CostEstimate(
            flops=2 * count * COLS * E,
            bytes_accessed=COLS * (count + E) * 2,
            transcendentals=0,
        ),
        name=name,
    )(info, plane, arow, exps, unit, *([add] if adds else []))


def far_kernel(raw_ref, core_ref, out_ref):
    out_ref[...] = (raw_ref[...] + core_ref[NEAR_ROWS:].astype(F32)).astype(BF16)


def make_far(raw, core):
    return pl.pallas_call(
        far_kernel,
        out_shape=jax.ShapeDtypeStruct((ROWS, E), BF16),
        in_specs=[vmem(), vmem()],
        out_specs=vmem(),
        compiler_params=params(4),
        name="far",
    )(raw, core)


def pick_kernel(info_ref, raw_ref, free_ref, held_ref):
    up, down = raw_ref[:ROWS], raw_ref[ROWS:]
    free_ref[...] = jnp.where(info_ref[3] == 0, down, up).astype(BF16)
    held_ref[...] = jnp.where(info_ref[3] == 0, up, down)


def make_pick(info, raw):
    return pl.pallas_call(
        pick_kernel,
        out_shape=(jax.ShapeDtypeStruct((ROWS, E), BF16), jax.ShapeDtypeStruct((ROWS, E), F32)),
        in_specs=[smem(), vmem()],
        out_specs=(vmem(), vmem()),
        compiler_params=params(4),
        name="pick",
    )(info, raw)


def pass_kernel(held_ref, far_ref, out_ref):
    out_ref[...] = (held_ref[...] + far_ref[...].astype(F32)).astype(BF16)


def make_pass(held, far):
    return pl.pallas_call(
        pass_kernel,
        out_shape=jax.ShapeDtypeStruct((ROWS, E), BF16),
        in_specs=[vmem(), vmem()],
        out_specs=vmem(),
        compiler_params=params(4),
        name="pass",
    )(held, far)


def final_kernel(info_ref, z_ref, mates_ref, own_ref, below_ref, above_ref, plane_ref, grad_ref, loss_ref):
    zf = z_ref[...].astype(F32)
    recip = lax.rsqrt(jnp.sum(zf * zf, axis=1, keepdims=True) + 1e-06)
    unit = zf * recip
    acc = own_ref[...] + below_ref[...].astype(F32) + above_ref[...].astype(F32)
    grad_unit = INV_TAU * (acc - 2.0 * mates_ref[...].astype(F32))
    along = jnp.sum(unit * grad_unit, axis=1, keepdims=True)
    grad_ref[...] = recip * (grad_unit - unit * along)
    parts = [[plane_ref[8 * n + 2 : 8 * n + 3] for n in range(4 * m, 4 * m + 4)] for m in range(4)]
    x_first = ring_sum(*[ring_sum(*line) for line in parts])
    y_first = ring_sum(*[ring_sum(*line) for line in zip(*parts)])
    loss = jnp.where(info_ref[3] == 0, x_first, y_first)
    loss_ref[...] = loss[:, :1] / (ROWS * 128)


def make_final(info, embeds, mates, own, below, above, plane):
    return pl.pallas_call(
        final_kernel,
        out_shape=(jax.ShapeDtypeStruct((ROWS, E), F32), jax.ShapeDtypeStruct((1, 1), F32)),
        in_specs=[smem()] + [vmem()] * 6,
        out_specs=(vmem(), vmem()),
        compiler_params=params(4),
        name="final",
    )(info, embeds, mates, own, below, above, plane)


def per_device(embeds, partner):
    unit = make_unit(embeds)
    core_id = lax.axis_index("core")
    z = lax.axis_index("zhi") * 2 + lax.axis_index("zlo")
    info = jnp.stack([lax.axis_index("x"), lax.axis_index("y"), z, core_id]).astype(jnp.int32)

    before, next_ = get(unit, first=-1), get(unit, first=1)
    z_before, z_after = get(unit, z=-1), get(unit, z=1)
    before, next_ = lax.optimization_barrier((before, next_))
    far = get(before, first=-1)
    near = jnp.concatenate([unit, z_after, z_before], axis=0)
    line0 = jnp.concatenate([after(unit, near), before], axis=0)
    line1 = jnp.concatenate([after(next_, near), far], axis=0)
    before0, after0 = get(line0, second=-1), get(line0, second=1)
    before1, after1 = get(line1, second=-1), get(line1, second=1)
    near = [near, get(near, core=1)]
    z_far = get(jnp.where(core_id == 0, after(z_before, line1), after(z_after, line1)), z_own=-1)

    mates, positive = make_mates(unit, partner)
    chain = make_exps(info, near, [line0, line1], (0, 1), (), None, None, "exps0")
    far0 = get(after(before0, chain[0]), second=-1)
    far1 = get(after(after1, chain[0]), second=1)
    rows = near + [z_far, get(after(z_far, chain[0]), core=1)]
    cols = [line0, line1, before0, after0, before1, after1]
    chain = make_exps(info, rows, cols, (0, 1, 2, 4, 3, 5), (0, 1), chain, None, "exps1")
    sums, exps, units = make_exps(info, rows, [far0, far1], (6, 7), (), chain, positive, "exps2")

    sums = sums + get(sums, core=1)
    arow, plane = make_totals(info, sums, get(sums, z=-1), get(sums, z=1), get(sums, z=2))
    plane = jnp.concatenate([plane] + [get(plane, first=k) for k in OFFSETS[1:]], axis=0)
    plane = jnp.concatenate([plane] + [get(plane, second=k) for k in OFFSETS[1:]], axis=0)

    theirs = make_grads(1024, 1024, BF16, info, plane, arow, exps, units, None, "grads_core")
    core = get(theirs, core=1)
    raw = make_grads(NEAR_ROWS, ROWS, F32, after(info, theirs), plane, arow, exps, units, None, "grads_far")
    far = make_far(raw, core)
    passed = get(far, z_own=-1)
    raw = make_grads(ROWS, 2 * ROWS, F32, after(info, far), plane, arow, exps, units, core, "grads_near")
    free, held = make_pick(info, raw)
    one = get(free, z_own=1)
    held = make_pass(held, passed)
    other = get(held, z_own=-1)
    own = make_grads(0, ROWS, F32, after(info, held), plane, arow, exps, units, core, "grads_own")
    grad, loss = make_final(info, embeds, mates, own, one, other, plane)
    return (loss[0, 0], grad)


def solution(mesh):
    torus = Mesh(mesh.devices.reshape(SIZES), AXES)
    return jax.shard_map(
        per_device,
        mesh=torus,
        in_specs=(P(AXES, None), P(AXES)),
        out_specs=(P(), P(AXES, None)),
        check_vma=False,
    )
```

```python
import functools
import math

import jax
import jax.numpy as jnp
from jax import lax
from jax.experimental import pallas as pl
from jax.experimental.pallas import tpu as pltpu
from jax.sharding import Mesh, PartitionSpec as P

INV_TAU = 10.0
EXP_SCALE = INV_TAU * math.log2(math.e)
AXES = ("zlo", "core", "y", "x", "zhi")
SIZES = (2, 2, 4, 4, 2)
OFFSETS = (0, -1, 1, 2)
NT = (((1,), (1,)), ((), ()))
NN = (((1,), (0,)), ((), ()))
ROWS = 256
ALL_ROWS = 2048
COLS = 4096
TILE = 512
MIB = 1024 * 1024
E = 512
BF16 = jnp.bfloat16
F32 = jnp.float32


def place(x, y, z, core):
    return ((((z % 2) * 2 + core) * 4 + y) * 4 + x) * 2 + z // 2


def get(value, z=0, core=0, first=0, second=0, z_own=0):
    pairs = []
    for px in range(4):
        for py in range(4):
            for pz in range(4):
                for pc in range(2):
                    x, y = (first, second) if pc == 0 else (second, first)
                    away = z + (z_own if pc == 0 else -z_own)
                    source = place((px + x) % 4, (py + y) % 4, (pz + away) % 4, pc ^ core)
                    pairs.append((source, place(px, py, pz, pc)))
    return lax.ppermute(value, AXES, pairs)


def ring_sum(own, before, after, far):
    return (own + far) + (before + after)


def after(value, *others):
    return lax.optimization_barrier((value, *others))[0]


def vmem():
    return pl.BlockSpec(memory_space=pltpu.VMEM)


def smem():
    return pl.BlockSpec(memory_space=pltpu.SMEM)


def hbm():
    return pl.BlockSpec(memory_space=pltpu.HBM)


def params(mib):
    return pltpu.CompilerParams(vmem_limit_bytes=mib * MIB)


def block_of(z, core):
    return ((z & 1) * 2 + core) * 2 + lax.shift_right_logical(z, 1)


def row_blocks(info_ref):
    for c in range(2):
        core = info_ref[3] ^ c
        up = 1 - 2 * core
        for k, away in enumerate((0, -up, up, 2)):
            yield (k // 2) * 1024 + c * 512 + (k % 2) * ROWS, block_of((info_ref[2] + away) & 3, core)


def unit_kernel(z_ref, unit_ref):
    zf = z_ref[...].astype(F32)
    recip = lax.rsqrt(jnp.sum(zf * zf, axis=1, keepdims=True) + 1e-06)
    unit_ref[...] = (zf * recip).astype(BF16)


def make_unit(embeds):
    return pl.pallas_call(
        unit_kernel,
        out_shape=jax.ShapeDtypeStruct((ROWS, E), BF16),
        in_specs=[vmem()],
        out_specs=vmem(),
        compiler_params=params(4),
        name="unit",
    )(embeds)


def mates_kernel(unit_ref, partner_ref, mates_ref, positive_ref):
    unit = unit_ref[...]
    ids = lax.broadcasted_iota(jnp.int32, (ROWS, ROWS), 0)
    pick = (ids == (partner_ref[...] & (ROWS - 1))).astype(F32).astype(BF16)
    mates = lax.dot_general(pick, unit, NN, preferred_element_type=F32)
    mates_ref[...] = mates.astype(BF16)
    products = jnp.sum(unit.astype(F32) * mates, axis=0, keepdims=True)
    total = jnp.sum(products, axis=1, keepdims=True) * INV_TAU
    positive_ref[...] = jnp.broadcast_to(total, (1, 128))


def make_mates(unit, partner):
    return pl.pallas_call(
        mates_kernel,
        out_shape=(
            jax.ShapeDtypeStruct((ROWS, E), BF16),
            jax.ShapeDtypeStruct((1, 128), F32),
        ),
        in_specs=[vmem(), vmem()],
        out_specs=(vmem(), vmem()),
        compiler_params=params(4),
        name="mates",
    )(unit, partner.reshape(1, ROWS))


def exps_kernel(places, rows_here, first, last, *refs):
    count = len(places)
    halves = len(rows_here)
    info_ref, refs = refs[0], refs[1:]
    row_refs, col_refs, refs = refs[: 2 * halves], refs[2 * halves : 2 * halves + count], refs[2 * halves + count :]
    if not first:
        before_ref, refs = refs[0], refs[3:]
    if last:
        positive_ref, refs = refs[0], refs[1:]
    sums_ref, exps_ref, unit_ref, rows, sums, line = refs
    for n, ref in enumerate(row_refs):
        start = rows_here[n // 2] * 1024 + (n % 2) * 512
        rows[start : start + 512] = ref[...]
    sums[...] = jnp.zeros_like(sums) if first else before_ref[...]
    part = slice(rows_here[0] * 1024, rows_here[-1] * 1024 + 1024)
    for n, col_ref in enumerate(col_refs):
        if 0 in rows_here:
            start = places[n] * TILE
            unit_ref[start : start + col_ref.shape[0]] = col_ref[...]

        @pl.loop(0, col_ref.shape[0] // ROWS)
        def _(m):
            here = pl.ds(pl.multiple_of(places[n] * TILE + m * ROWS, ROWS), ROWS)
            cols = col_ref[pl.ds(pl.multiple_of(m * ROWS, ROWS), ROWS), :]
            for start in range(part.start, part.stop, ROWS):
                piece = slice(start, start + ROWS)
                s = lax.dot_general(rows[piece], cols, NT, preferred_element_type=F32)
                e = jnp.exp2(s * EXP_SCALE)
                if first and n == 0 and start == 0:
                    i = lax.broadcasted_iota(jnp.int32, (ROWS, ROWS), 0)
                    j = lax.broadcasted_iota(jnp.int32, (ROWS, ROWS), 1)
                    e = jnp.where(i == j + m * ROWS, 0.0, e)
                exps_ref[piece, here] = e.astype(BF16)
                sums[piece] += e[:, :128] + e[:, 128:]

    if last:
        totals = jnp.sum(sums[...].T, axis=0, keepdims=True)
        line[...] = jnp.zeros_like(line)
        for start, at in row_blocks(info_ref):
            line[pl.ds(at, 1), :] = totals[:, start : start + ROWS]
        line[8:9, 0:128] = positive_ref[...]
        sums_ref[...] = line[...]
    else:
        sums_ref[...] = sums[...]


def make_exps(info, rows, rows_here, cols, places, chain, positive, name):
    first, last = chain is None, positive is not None
    count = len(cols)
    tiles = sum(c.shape[0] for c in cols) // TILE
    sums_shape = (16, ROWS) if last else (ALL_ROWS, 128)
    operands = [info, *rows, *cols] + ([] if first else list(chain)) + ([positive] if last else [])
    return pl.pallas_call(
        functools.partial(exps_kernel, places, rows_here, first, last),
        out_shape=(
            jax.ShapeDtypeStruct(sums_shape, F32),
            pltpu.VMEM((ALL_ROWS, COLS), BF16),
            pltpu.VMEM((COLS, E), BF16),
        ),
        in_specs=[smem()] + [vmem()] * (len(operands) - 1),
        out_specs=(vmem(), vmem(), vmem()),
        input_output_aliases={} if first else {2 + len(rows) + count: 1, 3 + len(rows) + count: 2},
        scratch_shapes=[
            pltpu.VMEM((ALL_ROWS, E), BF16),
            pltpu.VMEM((ALL_ROWS, 128), F32),
            pltpu.VMEM((16, ROWS), F32),
        ],
        compiler_params=params(12),
        cost_estimate=pl.CostEstimate(
            flops=2 * len(rows) * 512 * tiles * TILE * E * (8 if len(rows) == 2 else 4),
            bytes_accessed=tiles * TILE * E * 2,
            transcendentals=len(rows) * 512 * tiles * TILE,
        ),
        name=name,
    )(*operands)


def totals_kernel(info_ref, own_ref, before_ref, after_ref, far_ref, arow_ref, message_ref, recips):
    both = ring_sum(own_ref[...], before_ref[...], after_ref[...], far_ref[...])
    total = both[:8]
    recips[...] = 1.0 / total
    logs = jnp.sum(jnp.sum(jnp.log(total), axis=0, keepdims=True), axis=1, keepdims=True)
    loss = jnp.broadcast_to(logs, (1, 128)) - both[8:9, :128]
    for start, at in row_blocks(info_ref):
        line = recips[pl.ds(at, 1), :]
        arow_ref[start : start + ROWS] = jnp.broadcast_to(line, (128, ROWS)).T.astype(BF16)
    own = recips[pl.ds(block_of(info_ref[2], info_ref[3]), 1), :]
    zeros = jnp.zeros((5, 128), F32)
    message_ref[...] = jnp.concatenate([own[:, :128], own[:, 128:], loss, zeros], axis=0)


def make_totals(info, own, before, after, far):
    return pl.pallas_call(
        totals_kernel,
        out_shape=(
            jax.ShapeDtypeStruct((ALL_ROWS, 128), BF16),
            jax.ShapeDtypeStruct((8, 128), F32),
        ),
        in_specs=[smem()] + [vmem()] * 4,
        out_specs=(vmem(), vmem()),
        scratch_shapes=[pltpu.VMEM((8, ROWS), F32)],
        compiler_params=params(4),
        name="totals",
    )(info, own, before, after, far)


def grads_kernel(pieces, adds, info_ref, plane_ref, arow_ref, exps_ref, unit_ref, *refs):
    if adds is not None:
        add_ref, refs = refs[0], refs[1:]
    cols = [plane_ref[8 * (g // 2) + g % 2 : 8 * (g // 2) + g % 2 + 1].astype(BF16) for g in range(COLS // 128)]

    def weights(here):
        a = arow_ref[here]
        return exps_ref[here] * jnp.concatenate([a + col for col in cols], axis=1)

    if adds is None:
        size = pieces[0][1]
        step = pieces[-1][0] - pieces[0][0]

        @pl.loop(0, len(pieces))
        def _(n):
            w = weights(pl.ds(pl.multiple_of(pieces[0][0] + n * step, size), size))
            product = lax.dot_general(w, unit_ref[...], NN, preferred_element_type=F32)
            refs[0][pl.ds(pl.multiple_of(n * size, size), size)] = product.astype(refs[0].dtype)

    else:
        w = jnp.concatenate([weights(slice(start, start + size)) for start, size in pieces], axis=0)
        product = lax.dot_general(w, unit_ref[...], NN, preferred_element_type=F32)
        start = 0
        for (_, size), add, ref in zip(pieces, adds, refs):
            ref[...] = (product[start : start + size] + add_ref[add : add + size].astype(F32)).astype(ref.dtype)
            start += size


def make_grads(pieces, adds, dtypes, info, plane, arow, exps, unit, add, name):
    count = sum(size for _, size in pieces)
    sizes = [count] if adds is None else [size for _, size in pieces]
    exps = pltpu.with_memory_space_constraint(exps, pltpu.VMEM)
    unit = pltpu.with_memory_space_constraint(unit, pltpu.VMEM)
    return pl.pallas_call(
        functools.partial(grads_kernel, pieces, adds),
        out_shape=tuple(jax.ShapeDtypeStruct((size, E), dtype) for size, dtype in zip(sizes, dtypes)),
        in_specs=[smem()] + [vmem()] * (4 if adds is None else 5),
        out_specs=(vmem(),) * len(sizes),
        compiler_params=params(16),
        cost_estimate=pl.CostEstimate(
            flops=2 * count * COLS * E,
            bytes_accessed=COLS * (count + E) * 2,
            transcendentals=0,
        ),
        name=name,
    )(info, plane, arow, exps, unit, *([] if adds is None else [add]))


def pass_kernel(start, held_ref, far_ref, out_ref):
    out_ref[...] = (held_ref[...] + far_ref[start : start + ROWS].astype(F32)).astype(BF16)


def make_pass(held, far, start, name):
    return pl.pallas_call(
        functools.partial(pass_kernel, start),
        out_shape=jax.ShapeDtypeStruct((ROWS, E), BF16),
        in_specs=[vmem(), vmem()],
        out_specs=vmem(),
        compiler_params=params(4),
        name=name,
    )(held, far)


def final_kernel(info_ref, z_ref, mates_ref, own_ref, below_ref, above_ref, plane_ref, grad_ref, loss_ref):
    zf = z_ref[...].astype(F32)
    recip = lax.rsqrt(jnp.sum(zf * zf, axis=1, keepdims=True) + 1e-06)
    unit = zf * recip
    acc = own_ref[...] + below_ref[...].astype(F32) + above_ref[...].astype(F32)
    grad_unit = INV_TAU * (acc - 2.0 * mates_ref[...].astype(F32))
    along = jnp.sum(unit * grad_unit, axis=1, keepdims=True)
    grad_ref[...] = recip * (grad_unit - unit * along)
    parts = [[plane_ref[8 * n + 2 : 8 * n + 3] for n in range(4 * m, 4 * m + 4)] for m in range(4)]
    x_first = ring_sum(*[ring_sum(*line) for line in parts])
    y_first = ring_sum(*[ring_sum(*line) for line in zip(*parts)])
    loss = jnp.where(info_ref[3] == 0, x_first, y_first)
    loss_ref[...] = loss[:, :1] / (ROWS * 128)


def make_final(info, embeds, mates, own, below, above, plane):
    return pl.pallas_call(
        final_kernel,
        out_shape=(jax.ShapeDtypeStruct((ROWS, E), F32), jax.ShapeDtypeStruct((1, 1), F32)),
        in_specs=[smem()] + [vmem()] * 6,
        out_specs=(vmem(), vmem()),
        compiler_params=params(4),
        name="final",
    )(info, embeds, mates, own, below, above, plane)


def per_device(embeds, partner):
    unit = make_unit(embeds)
    core_id = lax.axis_index("core")
    z = lax.axis_index("zhi") * 2 + lax.axis_index("zlo")
    info = jnp.stack([lax.axis_index("x"), lax.axis_index("y"), z, core_id]).astype(jnp.int32)

    z_one = get(unit, z_own=-1)
    before, next_ = get(unit, first=-1), get(unit, first=1)
    before, next_ = lax.optimization_barrier((before, next_))
    far = get(unit, first=2)
    near = jnp.concatenate([unit, z_one], axis=0)
    line0 = jnp.concatenate([after(unit, near), before], axis=0)
    line1 = jnp.concatenate([next_, far], axis=0)
    before0, after0 = get(line0, second=-1), get(line0, second=1)
    before1, after1 = get(line1, second=-1), get(line1, second=1)
    z_two = get(unit, z_own=1)
    z_far = get(z_one, z_own=-1)
    near = [near, get(near, core=1)]

    mates, positive = make_mates(unit, partner)
    chain = make_exps(info, near, (0,), [line0, line1], (0, 1), None, None, "exps0")
    rest = jnp.concatenate([z_two, z_far], axis=0)
    rest = [rest, get(rest, core=1)]
    chain = make_exps(info, rest, (1,), [line0, line1], (0, 1), chain, None, "exps1")
    far0 = get(after(before0, after0, chain[0]), second=-1)
    far1 = get(after(after1, before1, chain[0]), second=1)
    rows = near + rest
    cols = [before0, after0, before1, after1]
    chain = make_exps(info, rows, (0, 1), cols, (2, 4, 3, 5), chain, None, "exps2")
    sums, exps, units = make_exps(info, rows, (0, 1), [far0, far1], (6, 7), chain, positive, "exps3")

    sums = sums + get(sums, core=1)
    arow, plane = make_totals(info, sums, get(sums, z=-1), get(sums, z=1), get(sums, z=2))
    plane = jnp.concatenate([plane] + [get(plane, first=k) for k in OFFSETS[1:]], axis=0)
    plane = jnp.concatenate([plane] + [get(plane, second=k) for k in OFFSETS[1:]], axis=0)

    (theirs,) = make_grads(((512, 512), (1536, 512)), None, (BF16,), info, plane, arow, exps, units, None, "grads_core")
    core = get(theirs, core=1)
    (far,) = make_grads(((1280, ROWS),), None, (F32,), after(info, theirs), plane, arow, exps, units, None, "grads_far")
    far = make_pass(far, core, 768, "pass_far")
    passed = get(far, z_own=-1)
    free, held = make_grads(
        ((256, ROWS), (1024, ROWS)), (256, 512), (BF16, F32), after(info, far), plane, arow, exps, units, core, "grads_near"
    )
    one = get(free, z_own=1)
    held = make_pass(held, passed, 0, "pass_two")
    two = get(held, z_own=-1)
    (own,) = make_grads(((0, ROWS),), (0,), (F32,), after(info, held), plane, arow, exps, units, core, "grads_own")
    grad, loss = make_final(info, embeds, mates, own, one, two, plane)
    return (loss[0, 0], grad)


def solution(mesh):
    torus = Mesh(mesh.devices.reshape(SIZES), AXES)
    return jax.shard_map(
        per_device,
        mesh=torus,
        in_specs=(P(AXES, None), P(AXES)),
        out_specs=(P(), P(AXES, None)),
        check_vma=False,
    )
```

```python
import functools
import math

import jax
import jax.numpy as jnp
from jax import lax
from jax.experimental import pallas as pl
from jax.experimental.pallas import tpu as pltpu
from jax.sharding import Mesh, PartitionSpec as P

INV_TAU = 10.0
EXP_SCALE = INV_TAU * math.log2(math.e)
AXES = ("zlo", "core", "y", "x", "zhi")
SIZES = (2, 2, 4, 4, 2)
OFFSETS = (0, -1, 1, 2)
NT = (((1,), (1,)), ((), ()))
NN = (((1,), (0,)), ((), ()))
ROWS = 256
ALL_ROWS = 2048
COLS = 4096
TILE = 512
MIB = 1024 * 1024
E = 512
BF16 = jnp.bfloat16
F32 = jnp.float32


def place(x, y, z, core):
    return ((((z % 2) * 2 + core) * 4 + y) * 4 + x) * 2 + z // 2


def get(value, z=0, core=0, first=0, second=0, z_own=0):
    pairs = []
    for px in range(4):
        for py in range(4):
            for pz in range(4):
                for pc in range(2):
                    x, y = (first, second) if pc == 0 else (second, first)
                    away = z + (z_own if pc == 0 else -z_own)
                    source = place((px + x) % 4, (py + y) % 4, (pz + away) % 4, pc ^ core)
                    pairs.append((source, place(px, py, pz, pc)))
    return lax.ppermute(value, AXES, pairs)


def ring_sum(own, before, after, far):
    return (own + far) + (before + after)


def after(value, *others):
    return lax.optimization_barrier((value, *others))[0]


def vmem():
    return pl.BlockSpec(memory_space=pltpu.VMEM)


def smem():
    return pl.BlockSpec(memory_space=pltpu.SMEM)


def hbm():
    return pl.BlockSpec(memory_space=pltpu.HBM)


def params(mib):
    return pltpu.CompilerParams(vmem_limit_bytes=mib * MIB)


def block_of(z, core):
    return ((z & 1) * 2 + core) * 2 + lax.shift_right_logical(z, 1)


def row_blocks(info_ref):
    for c in range(2):
        core = info_ref[3] ^ c
        up = 1 - 2 * core
        for k, away in enumerate((0, -up, up, 2)):
            yield (k // 2) * 1024 + c * 512 + (k % 2) * ROWS, block_of((info_ref[2] + away) & 3, core)


def col_blocks(info_ref):
    for two in OFFSETS:
        for one in OFFSETS:
            x = info_ref[0] + jnp.where(info_ref[3] == 0, one, two)
            y = info_ref[1] + jnp.where(info_ref[3] == 0, two, one)
            yield (y & 3) * 4 + (x & 3)


def in_parts(value):
    high = value.astype(BF16)
    rest = value - high.astype(F32)
    middle = rest.astype(BF16)
    low = (rest - middle.astype(F32)).astype(BF16)
    rows = [high.astype(F32), middle.astype(F32), low.astype(F32), jnp.zeros((13, value.shape[1]), F32)]
    return jnp.concatenate(rows, axis=0).astype(BF16)


def of_parts(block):
    rows = block.astype(F32)
    return rows[0:1] + (rows[1:2] + rows[2:3])


def unit_kernel(z_ref, unit_ref):
    zf = z_ref[...].astype(F32)
    recip = lax.rsqrt(jnp.sum(zf * zf, axis=1, keepdims=True) + 1e-06)
    unit_ref[...] = (zf * recip).astype(BF16)


def make_unit(embeds):
    return pl.pallas_call(
        unit_kernel,
        out_shape=jax.ShapeDtypeStruct((ROWS, E), BF16),
        in_specs=[vmem()],
        out_specs=vmem(),
        compiler_params=params(4),
        name="unit",
    )(embeds)


def mates_kernel(unit_ref, partner_ref, mates_ref, positive_ref):
    unit = unit_ref[...]
    ids = lax.broadcasted_iota(jnp.int32, (ROWS, ROWS), 0)
    pick = (ids == (partner_ref[...] & (ROWS - 1))).astype(F32).astype(BF16)
    mates = lax.dot_general(pick, unit, NN, preferred_element_type=F32)
    mates_ref[...] = mates.astype(BF16)
    products = jnp.sum(unit.astype(F32) * mates, axis=0, keepdims=True)
    total = jnp.sum(products, axis=1, keepdims=True) * INV_TAU
    positive_ref[...] = jnp.broadcast_to(total, (1, 128))


def make_mates(unit, partner):
    return pl.pallas_call(
        mates_kernel,
        out_shape=(
            jax.ShapeDtypeStruct((ROWS, E), BF16),
            jax.ShapeDtypeStruct((1, 128), F32),
        ),
        in_specs=[vmem(), vmem()],
        out_specs=(vmem(), vmem()),
        compiler_params=params(4),
        name="mates",
    )(unit, partner.reshape(1, ROWS))


def exps_kernel(places, rows_here, first, last, *refs):
    count = len(places)
    halves = len(rows_here)
    info_ref, refs = refs[0], refs[1:]
    row_refs, col_refs, refs = refs[: 2 * halves], refs[2 * halves : 2 * halves + count], refs[2 * halves + count :]
    if not first:
        before_ref, col_before_ref, refs = refs[0], refs[1], refs[4:]
    if last:
        positive_ref, refs = refs[0], refs[1:]
    sums_ref, col_sums_ref, exps_ref, unit_ref, rows, sums, col_sums, line, col_line = refs
    for n, ref in enumerate(row_refs):
        start = rows_here[n // 2] * 1024 + (n % 2) * 512
        rows[start : start + 512] = ref[...]
    sums[...] = jnp.zeros_like(sums) if first else before_ref[...]
    col_sums[...] = jnp.zeros_like(col_sums) if first else col_before_ref[...]
    part = slice(rows_here[0] * 1024, rows_here[-1] * 1024 + 1024)
    for n, col_ref in enumerate(col_refs):
        if 0 in rows_here:
            start = places[n] * TILE
            unit_ref[start : start + col_ref.shape[0]] = col_ref[...]

        @pl.loop(0, col_ref.shape[0] // ROWS)
        def _(m):
            here = pl.ds(pl.multiple_of(places[n] * TILE + m * ROWS, ROWS), ROWS)
            cols = col_ref[pl.ds(pl.multiple_of(m * ROWS, ROWS), ROWS), :]
            s = lax.dot_general(rows[part], cols, NT, preferred_element_type=F32)
            e = jnp.exp2(s * EXP_SCALE)
            if first and n == 0:
                i = lax.broadcasted_iota(jnp.int32, (ROWS, ROWS), 0)
                j = lax.broadcasted_iota(jnp.int32, (ROWS, ROWS), 1)
                own = jnp.where(i == j + m * ROWS, 0.0, e[:ROWS])
                e = jnp.concatenate([own, e[ROWS:]], axis=0)
            exps_ref[part, here] = e.astype(BF16)
            sums[part] += e[:, :128] + e[:, 128:]
            col_sums[:, here] += jnp.sum(e.reshape(-1, 8, ROWS), axis=0)

    if last:
        totals = jnp.sum(sums[...].T, axis=0, keepdims=True)
        for start, at in row_blocks(info_ref):
            line[pl.ds(at, 1), :] = totals[:, start : start + ROWS]
        sums_ref[...] = line[...]
        totals = jnp.sum(col_sums[...], axis=0, keepdims=True)
        col_line[...] = jnp.zeros_like(col_line)
        for n, at in enumerate(col_blocks(info_ref)):
            col_line[pl.ds(at, 1), :] = totals[:, n * ROWS : (n + 1) * ROWS]
        col_line[16:17, 0:128] = positive_ref[...]
        col_sums_ref[...] = col_line[...]
    else:
        sums_ref[...] = sums[...]
        col_sums_ref[...] = col_sums[...]


def make_exps(info, rows, rows_here, cols, places, chain, positive, name):
    first, last = chain is None, positive is not None
    count = len(cols)
    tiles = sum(c.shape[0] for c in cols) // TILE
    sums_shape = (8, ROWS) if last else (ALL_ROWS, 128)
    col_sums_shape = (24, ROWS) if last else (8, COLS)
    operands = [info, *rows, *cols] + ([] if first else list(chain)) + ([positive] if last else [])
    return pl.pallas_call(
        functools.partial(exps_kernel, places, rows_here, first, last),
        out_shape=(
            jax.ShapeDtypeStruct(sums_shape, F32),
            jax.ShapeDtypeStruct(col_sums_shape, F32),
            pltpu.VMEM((ALL_ROWS, COLS), BF16),
            pltpu.VMEM((COLS, E), BF16),
        ),
        in_specs=[smem()] + [vmem()] * (len(operands) - 1),
        out_specs=(vmem(), vmem(), vmem(), vmem()),
        input_output_aliases={} if first else {3 + len(rows) + count: 2, 4 + len(rows) + count: 3},
        scratch_shapes=[
            pltpu.VMEM((ALL_ROWS, E), BF16),
            pltpu.VMEM((ALL_ROWS, 128), F32),
            pltpu.VMEM((8, COLS), F32),
            pltpu.VMEM((8, ROWS), F32),
            pltpu.VMEM((24, ROWS), F32),
        ],
        compiler_params=params(12),
        cost_estimate=pl.CostEstimate(
            flops=2 * len(rows) * 512 * tiles * TILE * E * (8 if len(rows) == 2 else 4),
            bytes_accessed=tiles * TILE * E * 2,
            transcendentals=len(rows) * 512 * tiles * TILE,
        ),
        name=name,
    )(*operands)


def totals_kernel(info_ref, *refs):
    row_refs, col_refs, (arow_ref, acol_ref, loss_ref, recips, col_recips) = refs[:4], refs[4:8], refs[8:]
    recips[...] = 1.0 / ring_sum(*[ref[...] for ref in row_refs])
    both = ring_sum(*[ref[...] for ref in col_refs])
    totals = both[:16]
    col_recips[...] = 1.0 / totals
    logs = jnp.sum(jnp.sum(jnp.log(totals), axis=0, keepdims=True), axis=1, keepdims=True)
    loss = jnp.broadcast_to(logs, (1, 128)) - both[16:17, :128]
    loss_ref[...] = in_parts(jnp.concatenate([loss] * (E // 128), axis=1))
    for start, at in row_blocks(info_ref):
        line = recips[pl.ds(at, 1), :]
        arow_ref[start : start + ROWS] = jnp.broadcast_to(line, (128, ROWS)).T.astype(BF16)
    for n, at in enumerate(col_blocks(info_ref)):
        line = col_recips[pl.ds(at, 1), :]
        acol_ref[2 * n : 2 * n + 1] = line[:, :128]
        acol_ref[2 * n + 1 : 2 * n + 2] = line[:, 128:]


def make_totals(info, by_row, by_col):
    return pl.pallas_call(
        totals_kernel,
        out_shape=(
            jax.ShapeDtypeStruct((ALL_ROWS, 128), BF16),
            jax.ShapeDtypeStruct((32, 128), F32),
            jax.ShapeDtypeStruct((16, E), BF16),
        ),
        in_specs=[smem()] + [vmem()] * 8,
        out_specs=(vmem(), vmem(), vmem()),
        scratch_shapes=[pltpu.VMEM((8, ROWS), F32), pltpu.VMEM((16, ROWS), F32)],
        compiler_params=params(4),
        name="totals",
    )(info, *by_row, *by_col)


def grads_kernel(pieces, adds, carries, acol_ref, arow_ref, exps_ref, unit_ref, *refs):
    if adds is not None:
        add_ref, refs = refs[0], refs[1:]
    if carries:
        carry_ref, refs = refs[0], refs[1:]
        end = refs[0].shape[0]
        refs[0][end - 16 : end] = carry_ref[carry_ref.shape[0] - 16 : carry_ref.shape[0]]
    cols = [acol_ref[g : g + 1].astype(BF16) for g in range(COLS // 128)]

    def weights(here):
        a = arow_ref[here]
        return exps_ref[here] * jnp.concatenate([a + col for col in cols], axis=1)

    if adds is None:
        size = pieces[0][1]
        step = pieces[-1][0] - pieces[0][0]

        @pl.loop(0, len(pieces))
        def _(n):
            w = weights(pl.ds(pl.multiple_of(pieces[0][0] + n * step, size), size))
            product = lax.dot_general(w, unit_ref[...], NN, preferred_element_type=F32)
            refs[0][pl.ds(pl.multiple_of(n * size, size), size)] = product.astype(refs[0].dtype)

    else:
        w = jnp.concatenate([weights(slice(start, start + size)) for start, size in pieces], axis=0)
        product = lax.dot_general(w, unit_ref[...], NN, preferred_element_type=F32)
        start = 0
        for (_, size), add, ref in zip(pieces, adds, refs):
            ref[:size] = (product[start : start + size] + add_ref[add : add + size].astype(F32)).astype(ref.dtype)
            start += size


def make_grads(pieces, adds, dtypes, token, acol, arow, exps, unit, add, carry, name):
    count = sum(size for _, size in pieces)
    sizes = [count] if adds is None else [size for _, size in pieces]
    if carry is not None:
        sizes[0] += 16
    exps = pltpu.with_memory_space_constraint(exps, pltpu.VMEM)
    unit = pltpu.with_memory_space_constraint(unit, pltpu.VMEM)
    operands = [after(acol, token), arow, exps, unit]
    operands += [] if adds is None else [add]
    operands += [] if carry is None else [carry]
    return pl.pallas_call(
        functools.partial(grads_kernel, pieces, adds, carry is not None),
        out_shape=tuple(jax.ShapeDtypeStruct((size, E), dtype) for size, dtype in zip(sizes, dtypes)),
        in_specs=[vmem()] * len(operands),
        out_specs=(vmem(),) * len(sizes),
        compiler_params=params(16),
        cost_estimate=pl.CostEstimate(
            flops=2 * count * COLS * E,
            bytes_accessed=COLS * (count + E) * 2,
            transcendentals=0,
        ),
        name=name,
    )(*operands)


def far_kernel(raw_ref, core_ref, loss_ref, out_ref):
    out_ref[:ROWS] = (raw_ref[...] + core_ref[768:1024].astype(F32)).astype(BF16)
    out_ref[ROWS:] = in_parts(of_parts(loss_ref[...]) + of_parts(core_ref[1024:]))


def two_kernel(held_ref, far_ref, out_ref):
    out_ref[:ROWS] = (held_ref[...] + far_ref[:ROWS].astype(F32)).astype(BF16)
    out_ref[ROWS:] = far_ref[ROWS:]


def make_sum(kernel, operands, name):
    return pl.pallas_call(
        kernel,
        out_shape=jax.ShapeDtypeStruct((ROWS + 16, E), BF16),
        in_specs=[vmem()] * len(operands),
        out_specs=vmem(),
        compiler_params=params(4),
        name=name,
    )(*operands)


def final_kernel(z_ref, mates_ref, own_ref, one_ref, two_ref, here_ref, passed_ref, grad_ref, loss_ref):
    zf = z_ref[...].astype(F32)
    recip = lax.rsqrt(jnp.sum(zf * zf, axis=1, keepdims=True) + 1e-06)
    unit = zf * recip
    acc = own_ref[...] + one_ref[:ROWS].astype(F32) + two_ref[:ROWS].astype(F32)
    grad_unit = INV_TAU * (acc - 2.0 * mates_ref[...].astype(F32))
    along = jnp.sum(unit * grad_unit, axis=1, keepdims=True)
    grad_ref[...] = recip * (grad_unit - unit * along)
    loss = ring_sum(*[of_parts(ref[ROWS:]) for ref in (here_ref, passed_ref, one_ref, two_ref)])
    loss_ref[...] = loss[:, :1] / (ROWS * 128)


def make_final(operands):
    return pl.pallas_call(
        final_kernel,
        out_shape=(jax.ShapeDtypeStruct((ROWS, E), F32), jax.ShapeDtypeStruct((1, 1), F32)),
        in_specs=[vmem()] * len(operands),
        out_specs=(vmem(), vmem()),
        compiler_params=params(4),
        name="final",
    )(*operands)


def per_device(embeds, partner):
    unit = make_unit(embeds)
    core_id = lax.axis_index("core")
    z = lax.axis_index("zhi") * 2 + lax.axis_index("zlo")
    info = jnp.stack([lax.axis_index("x"), lax.axis_index("y"), z, core_id]).astype(jnp.int32)

    z_one = get(unit, z_own=-1)
    before, next_ = get(unit, first=-1), get(unit, first=1)
    before, next_ = lax.optimization_barrier((before, next_))
    far = get(unit, first=2)
    near = jnp.concatenate([unit, z_one], axis=0)
    line0 = jnp.concatenate([after(unit, near), before], axis=0)
    line1 = jnp.concatenate([next_, far], axis=0)
    before0, after0 = get(line0, second=-1), get(line0, second=1)
    before1, after1 = get(line1, second=-1), get(line1, second=1)
    z_two = get(unit, z_own=1)
    z_far = get(z_one, z_own=-1)
    near = [near, get(near, core=1)]

    mates, positive = make_mates(unit, partner)
    chain = make_exps(info, near, (0,), [line0, line1], (0, 1), None, None, "exps0")
    rest = jnp.concatenate([z_two, z_far], axis=0)
    rest = [rest, get(rest, core=1)]
    chain = make_exps(info, rest, (1,), [line0, line1], (0, 1), chain, None, "exps1")
    far0 = get(after(before0, after0, chain[0]), second=-1)
    far1 = get(after(after1, before1, chain[0]), second=1)
    rows = near + rest
    cols = [before0, after0, before1, after1]
    chain = make_exps(info, rows, (0, 1), cols, (2, 4, 3, 5), chain, None, "exps2")
    sums, col_sums, exps, units = make_exps(info, rows, (0, 1), [far0, far1], (6, 7), chain, positive, "exps3")

    by_row = sums + get(sums, core=1)
    by_row = [by_row] + [get(by_row, z=k) for k in OFFSETS[1:]]
    by_col = ring_sum(col_sums, *[get(col_sums, first=k) for k in OFFSETS[1:]])
    by_col = [by_col] + [get(by_col, second=k) for k in OFFSETS[1:]]
    arow, acol, loss = make_totals(info, by_row, by_col)

    given = (acol, arow, exps, units)
    (theirs,) = make_grads(((512, 512), (1536, 512)), None, (BF16,), info, *given, None, loss, "grads_core")
    core = get(theirs, core=1)
    (far,) = make_grads(((1280, ROWS),), None, (F32,), theirs, *given, None, None, "grads_far")
    far = make_sum(far_kernel, (far, core, loss), "sum_far")
    passed = get(far, z_own=-1)
    free, held = make_grads(
        ((256, ROWS), (1024, ROWS)), (256, 512), (BF16, F32), info, *given, core, far, "grads_near"
    )
    one = get(free, z_own=1)
    two = make_sum(two_kernel, (held, passed), "sum_two")
    own_token = two
    two = get(two, z_own=-1)
    (own,) = make_grads(((0, ROWS),), (0,), (F32,), own_token, *given, core, None, "grads_own")
    grad, loss = make_final((embeds, mates, own, one, two, far, passed))
    return (loss[0, 0], grad)


def solution(mesh):
    torus = Mesh(mesh.devices.reshape(SIZES), AXES)
    return jax.shard_map(
        per_device,
        mesh=torus,
        in_specs=(P(AXES, None), P(AXES)),
        out_specs=(P(), P(AXES, None)),
        check_vma=False,
    )
```

```python
import functools
import math

import jax
import jax.numpy as jnp
from jax import lax
from jax.experimental import pallas as pl
from jax.experimental.pallas import tpu as pltpu
from jax.sharding import Mesh, PartitionSpec as P

INV_TAU = 10.0
EXP_SCALE = INV_TAU * math.log2(math.e)
AXES = ("zlo", "core", "y", "x", "zhi")
SIZES = (2, 2, 4, 4, 2)
OFFSETS = (0, -1, 1, 2)
NT = (((1,), (1,)), ((), ()))
NN = (((1,), (0,)), ((), ()))
ROWS = 256
ALL_ROWS = 2048
COLS = 4096
TILE = 512
MIB = 1024 * 1024
E = 512
BF16 = jnp.bfloat16
F32 = jnp.float32


def place(x, y, z, core):
    return ((((z % 2) * 2 + core) * 4 + y) * 4 + x) * 2 + z // 2


def get(value, z=0, core=0, first=0, second=0, z_own=0):
    pairs = []
    for px in range(4):
        for py in range(4):
            for pz in range(4):
                for pc in range(2):
                    x, y = (first, second) if pc == 0 else (second, first)
                    away = z + (z_own if pc == 0 else -z_own)
                    source = place((px + x) % 4, (py + y) % 4, (pz + away) % 4, pc ^ core)
                    pairs.append((source, place(px, py, pz, pc)))
    return lax.ppermute(value, AXES, pairs)


def swap(value, way, step):
    pairs = []
    for px in range(4):
        for py in range(4):
            for pz in range(4):
                for pc in range(2):
                    at = [px, py, pz]
                    axis = {"z": 2, "first": pc, "second": 1 - pc}[way]
                    at[axis] = at[axis] ^ 1 if step == 0 else 3 - at[axis]
                    pairs.append((place(*at, pc), place(px, py, pz, pc)))
    return lax.ppermute(value, AXES, pairs)


def ring_sum(own, before, after, far):
    return (own + far) + (before + after)


def after(value, *others):
    return lax.optimization_barrier((value, *others))[0]


def vmem():
    return pl.BlockSpec(memory_space=pltpu.VMEM)


def smem():
    return pl.BlockSpec(memory_space=pltpu.SMEM)


def hbm():
    return pl.BlockSpec(memory_space=pltpu.HBM)


def params(mib):
    return pltpu.CompilerParams(vmem_limit_bytes=mib * MIB)


def block_of(z, core):
    return ((z & 1) * 2 + core) * 2 + lax.shift_right_logical(z, 1)


def row_blocks(info_ref):
    for c in range(2):
        core = info_ref[3] ^ c
        up = 1 - 2 * core
        for k, away in enumerate((0, -up, up, 2)):
            yield (k // 2) * 1024 + c * 512 + (k % 2) * ROWS, block_of((info_ref[2] + away) & 3, core)


def col_blocks(info_ref):
    for two in OFFSETS:
        for one in OFFSETS:
            x = info_ref[0] + jnp.where(info_ref[3] == 0, one, two)
            y = info_ref[1] + jnp.where(info_ref[3] == 0, two, one)
            yield (y & 3) * 4 + (x & 3)


def in_parts(value):
    high = value.astype(BF16)
    rest = value - high.astype(F32)
    middle = rest.astype(BF16)
    low = (rest - middle.astype(F32)).astype(BF16)
    rows = [high.astype(F32), middle.astype(F32), low.astype(F32), jnp.zeros((13, value.shape[1]), F32)]
    return jnp.concatenate(rows, axis=0).astype(BF16)


def of_parts(block):
    rows = block.astype(F32)
    return rows[0:1] + (rows[1:2] + rows[2:3])


def unit_kernel(z_ref, unit_ref):
    zf = z_ref[...].astype(F32)
    recip = lax.rsqrt(jnp.sum(zf * zf, axis=1, keepdims=True) + 1e-06)
    unit_ref[...] = (zf * recip).astype(BF16)


def make_unit(embeds):
    return pl.pallas_call(
        unit_kernel,
        out_shape=jax.ShapeDtypeStruct((ROWS, E), BF16),
        in_specs=[vmem()],
        out_specs=vmem(),
        compiler_params=params(4),
        name="unit",
    )(embeds)


def mates_kernel(unit_ref, partner_ref, mates_ref, positive_ref):
    unit = unit_ref[...]
    ids = lax.broadcasted_iota(jnp.int32, (ROWS, ROWS), 0)
    pick = (ids == (partner_ref[...] & (ROWS - 1))).astype(F32).astype(BF16)
    mates = lax.dot_general(pick, unit, NN, preferred_element_type=F32)
    mates_ref[...] = mates.astype(BF16)
    products = jnp.sum(unit.astype(F32) * mates, axis=0, keepdims=True)
    total = jnp.sum(products, axis=1, keepdims=True) * INV_TAU
    positive_ref[...] = jnp.broadcast_to(total, (1, 128))


def make_mates(unit, partner):
    return pl.pallas_call(
        mates_kernel,
        out_shape=(
            jax.ShapeDtypeStruct((ROWS, E), BF16),
            jax.ShapeDtypeStruct((1, 128), F32),
        ),
        in_specs=[vmem(), vmem()],
        out_specs=(vmem(), vmem()),
        compiler_params=params(4),
        name="mates",
    )(unit, partner.reshape(1, ROWS))


def exps_kernel(places, rows_here, first, last, *refs):
    count = len(places)
    halves = len(rows_here)
    info_ref, refs = refs[0], refs[1:]
    row_refs, col_refs, refs = refs[: 2 * halves], refs[2 * halves : 2 * halves + count], refs[2 * halves + count :]
    if not first:
        before_ref, col_before_ref, refs = refs[0], refs[1], refs[4:]
    if last:
        positive_ref, refs = refs[0], refs[1:]
    sums_ref, col_sums_ref, exps_ref, unit_ref, rows, sums, col_sums, line, col_line = refs
    for n, ref in enumerate(row_refs):
        start = rows_here[n // 2] * 1024 + (n % 2) * 512
        rows[start : start + 512] = ref[...]
    sums[...] = jnp.zeros_like(sums) if first else before_ref[...]
    col_sums[...] = jnp.zeros_like(col_sums) if first else col_before_ref[...]
    part = slice(rows_here[0] * 1024, rows_here[-1] * 1024 + 1024)
    for n, col_ref in enumerate(col_refs):
        if 0 in rows_here:
            start = places[n] * TILE
            unit_ref[start : start + col_ref.shape[0]] = col_ref[...]

        @pl.loop(0, col_ref.shape[0] // ROWS)
        def _(m):
            here = pl.ds(pl.multiple_of(places[n] * TILE + m * ROWS, ROWS), ROWS)
            cols = col_ref[pl.ds(pl.multiple_of(m * ROWS, ROWS), ROWS), :]
            s = lax.dot_general(rows[part], cols, NT, preferred_element_type=F32)
            e = jnp.exp2(s * EXP_SCALE)
            if first and n == 0:
                i = lax.broadcasted_iota(jnp.int32, (ROWS, ROWS), 0)
                j = lax.broadcasted_iota(jnp.int32, (ROWS, ROWS), 1)
                own = jnp.where(i == j + m * ROWS, 0.0, e[:ROWS])
                e = jnp.concatenate([own, e[ROWS:]], axis=0)
            exps_ref[part, here] = e.astype(BF16)
            sums[part] += e[:, :128] + e[:, 128:]
            col_sums[:, here] += jnp.sum(e.reshape(-1, 8, ROWS), axis=0)

    if last:
        totals = jnp.sum(sums[...].T, axis=0, keepdims=True)
        for start, at in row_blocks(info_ref):
            line[pl.ds(at, 1), :] = totals[:, start : start + ROWS]
        sums_ref[...] = line[...]
        totals = jnp.sum(col_sums[...], axis=0, keepdims=True)
        col_line[...] = jnp.zeros_like(col_line)
        for n, at in enumerate(col_blocks(info_ref)):
            col_line[pl.ds(at, 1), :] = totals[:, n * ROWS : (n + 1) * ROWS]
        col_line[16:17, 0:128] = positive_ref[...]
        col_sums_ref[...] = col_line[...]
    else:
        sums_ref[...] = sums[...]
        col_sums_ref[...] = col_sums[...]


def make_exps(info, rows, rows_here, cols, places, chain, positive, name):
    first, last = chain is None, positive is not None
    count = len(cols)
    tiles = sum(c.shape[0] for c in cols) // TILE
    sums_shape = (8, ROWS) if last else (ALL_ROWS, 128)
    col_sums_shape = (24, ROWS) if last else (8, COLS)
    operands = [info, *rows, *cols] + ([] if first else list(chain)) + ([positive] if last else [])
    return pl.pallas_call(
        functools.partial(exps_kernel, places, rows_here, first, last),
        out_shape=(
            jax.ShapeDtypeStruct(sums_shape, F32),
            jax.ShapeDtypeStruct(col_sums_shape, F32),
            pltpu.VMEM((ALL_ROWS, COLS), BF16),
            pltpu.VMEM((COLS, E), BF16),
        ),
        in_specs=[smem()] + [vmem()] * (len(operands) - 1),
        out_specs=(vmem(), vmem(), vmem(), vmem()),
        input_output_aliases={} if first else {3 + len(rows) + count: 2, 4 + len(rows) + count: 3},
        scratch_shapes=[
            pltpu.VMEM((ALL_ROWS, E), BF16),
            pltpu.VMEM((ALL_ROWS, 128), F32),
            pltpu.VMEM((8, COLS), F32),
            pltpu.VMEM((8, ROWS), F32),
            pltpu.VMEM((24, ROWS), F32),
        ],
        compiler_params=params(12),
        cost_estimate=pl.CostEstimate(
            flops=2 * len(rows) * 512 * tiles * TILE * E * (8 if len(rows) == 2 else 4),
            bytes_accessed=tiles * TILE * E * 2,
            transcendentals=len(rows) * 512 * tiles * TILE,
        ),
        name=name,
    )(*operands)


def totals_kernel(info_ref, *refs):
    row_refs, col_refs, (arow_ref, acol_ref, loss_ref, recips, col_recips) = refs[:2], refs[2:4], refs[4:]
    recips[...] = 1.0 / (row_refs[0][...] + row_refs[1][...])
    both = col_refs[0][...] + col_refs[1][...]
    totals = both[:16]
    col_recips[...] = 1.0 / totals
    logs = jnp.sum(jnp.sum(jnp.log(totals), axis=0, keepdims=True), axis=1, keepdims=True)
    loss = jnp.broadcast_to(logs, (1, 128)) - both[16:17, :128]
    loss_ref[...] = in_parts(jnp.concatenate([loss] * (E // 128), axis=1))
    for start, at in row_blocks(info_ref):
        line = recips[pl.ds(at, 1), :]
        arow_ref[start : start + ROWS] = jnp.broadcast_to(line, (128, ROWS)).T.astype(BF16)
    for n, at in enumerate(col_blocks(info_ref)):
        line = col_recips[pl.ds(at, 1), :]
        acol_ref[2 * n : 2 * n + 1] = line[:, :128]
        acol_ref[2 * n + 1 : 2 * n + 2] = line[:, 128:]


def make_totals(info, by_row, by_col):
    return pl.pallas_call(
        totals_kernel,
        out_shape=(
            jax.ShapeDtypeStruct((ALL_ROWS, 128), BF16),
            jax.ShapeDtypeStruct((32, 128), F32),
            jax.ShapeDtypeStruct((16, E), BF16),
        ),
        in_specs=[smem()] + [vmem()] * 4,
        out_specs=(vmem(), vmem(), vmem()),
        scratch_shapes=[pltpu.VMEM((8, ROWS), F32), pltpu.VMEM((16, ROWS), F32)],
        compiler_params=params(4),
        name="totals",
    )(info, *by_row, *by_col)


def grads_kernel(pieces, adds, carries, acol_ref, arow_ref, exps_ref, unit_ref, *refs):
    if adds is not None:
        add_ref, refs = refs[0], refs[1:]
    if carries:
        carry_ref, refs = refs[0], refs[1:]
        end = refs[0].shape[0]
        refs[0][end - 16 : end] = carry_ref[carry_ref.shape[0] - 16 : carry_ref.shape[0]]
    cols = [acol_ref[g : g + 1].astype(BF16) for g in range(COLS // 128)]

    def weights(here):
        a = arow_ref[here]
        return exps_ref[here] * jnp.concatenate([a + col for col in cols], axis=1)

    if adds is None:
        size = pieces[0][1]
        step = pieces[-1][0] - pieces[0][0]

        @pl.loop(0, len(pieces))
        def _(n):
            w = weights(pl.ds(pl.multiple_of(pieces[0][0] + n * step, size), size))
            product = lax.dot_general(w, unit_ref[...], NN, preferred_element_type=F32)
            refs[0][pl.ds(pl.multiple_of(n * size, size), size)] = product.astype(refs[0].dtype)

    else:
        w = jnp.concatenate([weights(slice(start, start + size)) for start, size in pieces], axis=0)
        product = lax.dot_general(w, unit_ref[...], NN, preferred_element_type=F32)
        start = 0
        for (_, size), add, ref in zip(pieces, adds, refs):
            ref[:size] = (product[start : start + size] + add_ref[add : add + size].astype(F32)).astype(ref.dtype)
            start += size


def make_grads(pieces, adds, dtypes, token, acol, arow, exps, unit, add, carry, name):
    count = sum(size for _, size in pieces)
    sizes = [count] if adds is None else [size for _, size in pieces]
    if carry is not None:
        sizes[0] += 16
    exps = pltpu.with_memory_space_constraint(exps, pltpu.VMEM)
    unit = pltpu.with_memory_space_constraint(unit, pltpu.VMEM)
    operands = [after(acol, token), arow, exps, unit]
    operands += [] if adds is None else [add]
    operands += [] if carry is None else [carry]
    return pl.pallas_call(
        functools.partial(grads_kernel, pieces, adds, carry is not None),
        out_shape=tuple(jax.ShapeDtypeStruct((size, E), dtype) for size, dtype in zip(sizes, dtypes)),
        in_specs=[vmem()] * len(operands),
        out_specs=(vmem(),) * len(sizes),
        compiler_params=params(16),
        cost_estimate=pl.CostEstimate(
            flops=2 * count * COLS * E,
            bytes_accessed=COLS * (count + E) * 2,
            transcendentals=0,
        ),
        name=name,
    )(*operands)


def far_kernel(raw_ref, core_ref, loss_ref, out_ref):
    out_ref[:ROWS] = (raw_ref[...] + core_ref[768:1024].astype(F32)).astype(BF16)
    out_ref[ROWS:] = in_parts(of_parts(loss_ref[...]) + of_parts(core_ref[1024:]))


def two_kernel(held_ref, far_ref, out_ref):
    out_ref[:ROWS] = (held_ref[...] + far_ref[:ROWS].astype(F32)).astype(BF16)
    out_ref[ROWS:] = far_ref[ROWS:]


def make_sum(kernel, operands, name):
    return pl.pallas_call(
        kernel,
        out_shape=jax.ShapeDtypeStruct((ROWS + 16, E), BF16),
        in_specs=[vmem()] * len(operands),
        out_specs=vmem(),
        compiler_params=params(4),
        name=name,
    )(*operands)


def final_kernel(z_ref, mates_ref, own_ref, one_ref, two_ref, here_ref, passed_ref, grad_ref, loss_ref):
    zf = z_ref[...].astype(F32)
    recip = lax.rsqrt(jnp.sum(zf * zf, axis=1, keepdims=True) + 1e-06)
    unit = zf * recip
    acc = own_ref[...] + one_ref[:ROWS].astype(F32) + two_ref[:ROWS].astype(F32)
    grad_unit = INV_TAU * (acc - 2.0 * mates_ref[...].astype(F32))
    along = jnp.sum(unit * grad_unit, axis=1, keepdims=True)
    grad_ref[...] = recip * (grad_unit - unit * along)
    loss = ring_sum(*[of_parts(ref[ROWS:]) for ref in (here_ref, passed_ref, one_ref, two_ref)])
    loss_ref[...] = loss[:, :1] / (ROWS * 128)


def make_final(operands):
    return pl.pallas_call(
        final_kernel,
        out_shape=(jax.ShapeDtypeStruct((ROWS, E), F32), jax.ShapeDtypeStruct((1, 1), F32)),
        in_specs=[vmem()] * len(operands),
        out_specs=(vmem(), vmem()),
        compiler_params=params(4),
        name="final",
    )(*operands)


def per_device(embeds, partner):
    unit = make_unit(embeds)
    core_id = lax.axis_index("core")
    z = lax.axis_index("zhi") * 2 + lax.axis_index("zlo")
    info = jnp.stack([lax.axis_index("x"), lax.axis_index("y"), z, core_id]).astype(jnp.int32)

    z_one = get(unit, z_own=-1)
    before, next_ = get(unit, first=-1), get(unit, first=1)
    before, next_ = lax.optimization_barrier((before, next_))
    far = get(unit, first=2)
    near = jnp.concatenate([unit, z_one], axis=0)
    line0 = jnp.concatenate([after(unit, near), before], axis=0)
    line1 = jnp.concatenate([next_, far], axis=0)
    before0, after0 = get(line0, second=-1), get(line0, second=1)
    before1, after1 = get(line1, second=-1), get(line1, second=1)
    z_two = get(unit, z_own=1)
    z_far = get(z_one, z_own=-1)
    near = [near, get(near, core=1)]

    mates, positive = make_mates(unit, partner)
    chain = make_exps(info, near, (0,), [line0, line1], (0, 1), None, None, "exps0")
    rest = jnp.concatenate([z_two, z_far], axis=0)
    rest = [rest, get(rest, core=1)]
    chain = make_exps(info, rest, (1,), [line0, line1], (0, 1), chain, None, "exps1")
    far0 = get(after(before0, after0, chain[0]), second=-1)
    rows = near + rest
    chain = make_exps(info, rows, (0, 1), [before0, after0], (2, 4), chain, None, "exps2")
    far1 = get(after(after1, before1, chain[0]), second=1)
    chain = make_exps(info, rows, (0, 1), [before1, after1, far0], (3, 5, 6), chain, None, "exps3")
    sums, col_sums, exps, units = make_exps(info, rows, (0, 1), [far1], (7,), chain, positive, "exps4")

    by_row = sums + get(sums, core=1)
    by_col = col_sums + swap(col_sums, "first", 0)
    by_col = by_col + swap(after(by_col, by_row), "first", 1)
    by_row = by_row + swap(by_row, "z", 0)
    by_col = by_col + swap(by_col, "second", 0)
    by_col = after(by_col, by_row)
    by_row = [by_row, swap(by_row, "z", 1)]
    by_col = [by_col, swap(by_col, "second", 1)]
    arow, acol, loss = make_totals(info, by_row, by_col)

    given = (acol, arow, exps, units)
    (theirs,) = make_grads(((512, 512), (1536, 512)), None, (BF16,), info, *given, None, loss, "grads_core")
    core = get(theirs, core=1)
    (far,) = make_grads(((1280, ROWS),), None, (F32,), theirs, *given, None, None, "grads_far")
    far = make_sum(far_kernel, (far, core, loss), "sum_far")
    passed = get(far, z_own=-1)
    free, held = make_grads(
        ((256, ROWS), (1024, ROWS)), (256, 512), (BF16, F32), info, *given, core, far, "grads_near"
    )
    one = get(free, z_own=1)
    two = make_sum(two_kernel, (held, passed), "sum_two")
    own_token = two
    two = get(two, z_own=-1)
    (own,) = make_grads(((0, ROWS),), (0,), (F32,), own_token, *given, core, None, "grads_own")
    grad, loss = make_final((embeds, mates, own, one, two, far, passed))
    return (loss[0, 0], grad)


def solution(mesh):
    torus = Mesh(mesh.devices.reshape(SIZES), AXES)
    return jax.shard_map(
        per_device,
        mesh=torus,
        in_specs=(P(AXES, None), P(AXES)),
        out_specs=(P(), P(AXES, None)),
        check_vma=False,
    )
```

```python
import functools
import math

import jax
import jax.numpy as jnp
from jax import lax
from jax.experimental import pallas as pl
from jax.experimental.pallas import tpu as pltpu
from jax.sharding import Mesh, PartitionSpec as P

INV_TAU = 10.0
EXP_SCALE = INV_TAU * math.log2(math.e)
AXES = ("zlo", "core", "y", "x", "zhi")
SIZES = (2, 2, 4, 4, 2)
OFFSETS = (0, -1, 1, 2)
NT = (((1,), (1,)), ((), ()))
NN = (((1,), (0,)), ((), ()))
ROWS = 256
ALL_ROWS = 2048
COLS = 4096
TILE = 512
MIB = 1024 * 1024
E = 512
BF16 = jnp.bfloat16
F32 = jnp.float32


def place(x, y, z, core):
    return ((((z % 2) * 2 + core) * 4 + y) * 4 + x) * 2 + z // 2


def get(value, z=0, core=0, first=0, second=0, z_own=0):
    pairs = []
    for px in range(4):
        for py in range(4):
            for pz in range(4):
                for pc in range(2):
                    x, y = (first, second) if pc == 0 else (second, first)
                    away = z + (z_own if pc == 0 else -z_own)
                    source = place((px + x) % 4, (py + y) % 4, (pz + away) % 4, pc ^ core)
                    pairs.append((source, place(px, py, pz, pc)))
    return lax.ppermute(value, AXES, pairs)


def swap(value, way, step):
    pairs = []
    for px in range(4):
        for py in range(4):
            for pz in range(4):
                for pc in range(2):
                    at = [px, py, pz]
                    axis = {"z": 2, "first": pc, "second": 1 - pc}[way]
                    at[axis] = at[axis] ^ 1 if step == 0 else 3 - at[axis]
                    pairs.append((place(*at, pc), place(px, py, pz, pc)))
    return lax.ppermute(value, AXES, pairs)


def ring_sum(own, before, after, far):
    return (own + far) + (before + after)


def after(value, *others):
    return lax.optimization_barrier((value, *others))[0]


def vmem():
    return pl.BlockSpec(memory_space=pltpu.VMEM)


def smem():
    return pl.BlockSpec(memory_space=pltpu.SMEM)


def hbm():
    return pl.BlockSpec(memory_space=pltpu.HBM)


def params(mib):
    return pltpu.CompilerParams(vmem_limit_bytes=mib * MIB)


def block_of(z, core):
    return ((z & 1) * 2 + core) * 2 + lax.shift_right_logical(z, 1)


def row_blocks(info_ref):
    for c in range(2):
        core = info_ref[3] ^ c
        up = 1 - 2 * core
        for k, away in enumerate((0, -up, up, 2)):
            yield (k // 2) * 1024 + c * 512 + (k % 2) * ROWS, block_of((info_ref[2] + away) & 3, core)


def col_blocks(info_ref):
    for two in OFFSETS:
        for one in OFFSETS:
            x = info_ref[0] + jnp.where(info_ref[3] == 0, one, two)
            y = info_ref[1] + jnp.where(info_ref[3] == 0, two, one)
            yield (y & 3) * 4 + (x & 3)


def in_parts(value):
    high = value.astype(BF16)
    rest = value - high.astype(F32)
    middle = rest.astype(BF16)
    low = (rest - middle.astype(F32)).astype(BF16)
    rows = [high.astype(F32), middle.astype(F32), low.astype(F32), jnp.zeros((13, value.shape[1]), F32)]
    return jnp.concatenate(rows, axis=0).astype(BF16)


def of_parts(block):
    rows = block.astype(F32)
    return rows[0:1] + (rows[1:2] + rows[2:3])


def unit_kernel(z_ref, unit_ref):
    zf = z_ref[...].astype(F32)
    recip = lax.rsqrt(jnp.sum(zf * zf, axis=1, keepdims=True) + 1e-06)
    unit_ref[...] = (zf * recip).astype(BF16)


def make_unit(embeds):
    return pl.pallas_call(
        unit_kernel,
        out_shape=jax.ShapeDtypeStruct((ROWS, E), BF16),
        in_specs=[vmem()],
        out_specs=vmem(),
        compiler_params=params(4),
        name="unit",
    )(embeds)


def mates_kernel(unit_ref, partner_ref, mates_ref, positive_ref):
    unit = unit_ref[...]
    ids = lax.broadcasted_iota(jnp.int32, (ROWS, ROWS), 0)
    pick = (ids == (partner_ref[...] & (ROWS - 1))).astype(F32).astype(BF16)
    mates = lax.dot_general(pick, unit, NN, preferred_element_type=F32)
    mates_ref[...] = mates.astype(BF16)
    products = jnp.sum(unit.astype(F32) * mates, axis=0, keepdims=True)
    total = jnp.sum(products, axis=1, keepdims=True) * INV_TAU
    positive_ref[...] = jnp.broadcast_to(total, (1, 128))


def make_mates(unit, partner):
    return pl.pallas_call(
        mates_kernel,
        out_shape=(
            jax.ShapeDtypeStruct((ROWS, E), BF16),
            jax.ShapeDtypeStruct((1, 128), F32),
        ),
        in_specs=[vmem(), vmem()],
        out_specs=(vmem(), vmem()),
        compiler_params=params(4),
        name="mates",
    )(unit, partner.reshape(1, ROWS))


def exps_kernel(places, rows_here, first, last, *refs):
    count = len(places)
    info_ref, refs = refs[0], refs[1:]
    row_refs, refs = refs[: 2 * len(rows_here)], refs[2 * len(rows_here) :]
    col_refs, refs = refs[:count], refs[count:]
    if not first:
        refs = refs[4:]
    if last:
        positive_ref, refs = refs[0], refs[1:]
    sums_ref, col_sums_ref, exps_ref, unit_ref = refs[:4]
    if first:
        sums_ref[...] = jnp.zeros_like(sums_ref)
        col_sums_ref[...] = jnp.zeros_like(col_sums_ref)
    for n, col_ref in enumerate(col_refs):
        if 0 in rows_here:
            start = places[n] * TILE
            unit_ref[start : start + col_ref.shape[0]] = col_ref[...]

        @pl.loop(0, col_ref.shape[0] // ROWS)
        def _(m):
            here = pl.ds(pl.multiple_of(places[n] * TILE + m * ROWS, ROWS), ROWS)
            cols = col_ref[pl.ds(pl.multiple_of(m * ROWS, ROWS), ROWS), :]
            by_col = col_sums_ref[:, here]
            for k, ref in enumerate(row_refs):
                start = rows_here[k // 2] * 1024 + (k % 2) * 512
                part = slice(start, start + 512)
                s = lax.dot_general(ref[...], cols, NT, preferred_element_type=F32)
                e = jnp.exp2(s * EXP_SCALE)
                if first and n == 0 and k == 0:
                    i = lax.broadcasted_iota(jnp.int32, (ROWS, ROWS), 0)
                    j = lax.broadcasted_iota(jnp.int32, (ROWS, ROWS), 1)
                    own = jnp.where(i == j + m * ROWS, 0.0, e[:ROWS])
                    e = jnp.concatenate([own, e[ROWS:]], axis=0)
                exps_ref[part, here] = e.astype(BF16)
                sums_ref[part] += e[:, :128] + e[:, 128:]
                by_col += jnp.sum(e.reshape(-1, 8, ROWS), axis=0)
            col_sums_ref[:, here] = by_col

    if last:
        line_ref, col_line_ref = refs[4:]
        totals = jnp.sum(sums_ref[...].T, axis=0, keepdims=True)
        for start, at in row_blocks(info_ref):
            line_ref[pl.ds(at, 1), :] = totals[:, start : start + ROWS]
        totals = jnp.sum(col_sums_ref[...], axis=0, keepdims=True)
        col_line_ref[...] = jnp.zeros_like(col_line_ref)
        for n, at in enumerate(col_blocks(info_ref)):
            col_line_ref[pl.ds(at, 1), :] = totals[:, n * ROWS : (n + 1) * ROWS]
        col_line_ref[16:17, 0:128] = positive_ref[...]


def make_exps(info, rows, rows_here, cols, places, chain, positive, name):
    first, last = chain is None, positive is not None
    count = len(cols)
    tiles = sum(c.shape[0] for c in cols) // TILE
    operands = [info, *rows, *cols] + ([] if first else list(chain[:4])) + ([positive] if last else [])
    out_shape = (
        pltpu.VMEM((ALL_ROWS, 128), F32),
        pltpu.VMEM((8, COLS), F32),
        pltpu.VMEM((ALL_ROWS, COLS), BF16),
        pltpu.VMEM((COLS, E), BF16),
    )
    if last:
        out_shape += (jax.ShapeDtypeStruct((8, ROWS), F32), jax.ShapeDtypeStruct((24, ROWS), F32))
    start = 1 + len(rows) + count
    return pl.pallas_call(
        functools.partial(exps_kernel, places, rows_here, first, last),
        out_shape=out_shape,
        in_specs=[smem()] + [vmem()] * (len(operands) - 1),
        out_specs=(vmem(),) * len(out_shape),
        input_output_aliases={} if first else {start + n: n for n in range(4)},
        compiler_params=params(12),
        cost_estimate=pl.CostEstimate(
            flops=2 * len(rows) * 512 * tiles * TILE * E * (8 if len(rows) == 2 else 4),
            bytes_accessed=tiles * TILE * E * 2,
            transcendentals=len(rows) * 512 * tiles * TILE,
        ),
        name=name,
    )(*operands)


def totals_kernel(info_ref, *refs):
    row_refs, col_refs, (arow_ref, acol_ref, loss_ref, recips, col_recips) = refs[:2], refs[2:4], refs[4:]
    recips[...] = 1.0 / (row_refs[0][...] + row_refs[1][...])
    both = col_refs[0][...] + col_refs[1][...]
    totals = both[:16]
    col_recips[...] = 1.0 / totals
    logs = jnp.sum(jnp.sum(jnp.log(totals), axis=0, keepdims=True), axis=1, keepdims=True)
    loss = jnp.broadcast_to(logs, (1, 128)) - both[16:17, :128]
    loss_ref[...] = in_parts(jnp.concatenate([loss] * (E // 128), axis=1))
    for start, at in row_blocks(info_ref):
        line = recips[pl.ds(at, 1), :]
        arow_ref[start : start + ROWS] = jnp.broadcast_to(line, (128, ROWS)).T.astype(BF16)
    for n, at in enumerate(col_blocks(info_ref)):
        line = col_recips[pl.ds(at, 1), :]
        acol_ref[2 * n : 2 * n + 1] = line[:, :128]
        acol_ref[2 * n + 1 : 2 * n + 2] = line[:, 128:]


def make_totals(info, by_row, by_col):
    return pl.pallas_call(
        totals_kernel,
        out_shape=(
            jax.ShapeDtypeStruct((ALL_ROWS, 128), BF16),
            jax.ShapeDtypeStruct((32, 128), F32),
            jax.ShapeDtypeStruct((16, E), BF16),
        ),
        in_specs=[smem()] + [vmem()] * 4,
        out_specs=(vmem(), vmem(), vmem()),
        scratch_shapes=[pltpu.VMEM((8, ROWS), F32), pltpu.VMEM((16, ROWS), F32)],
        compiler_params=params(4),
        name="totals",
    )(info, *by_row, *by_col)


def grads_kernel(pieces, adds, carries, acol_ref, arow_ref, exps_ref, unit_ref, *refs):
    if adds is not None:
        add_ref, refs = refs[0], refs[1:]
    if carries:
        carry_ref, refs = refs[0], refs[1:]
        end = refs[0].shape[0]
        refs[0][end - 16 : end] = carry_ref[carry_ref.shape[0] - 16 : carry_ref.shape[0]]
    cols = [acol_ref[g : g + 1].astype(BF16) for g in range(COLS // 128)]

    def weights(here):
        a = arow_ref[here]
        return exps_ref[here] * jnp.concatenate([a + col for col in cols], axis=1)

    if adds is None:
        to = 0
        for start, size in pieces:
            w = weights(slice(start, start + size))
            product = lax.dot_general(w, unit_ref[...], NN, preferred_element_type=F32)
            refs[0][to : to + size] = product.astype(refs[0].dtype)
            to += size

    else:
        w = jnp.concatenate([weights(slice(start, start + size)) for start, size in pieces], axis=0)
        product = lax.dot_general(w, unit_ref[...], NN, preferred_element_type=F32)
        start = 0
        for (_, size), add, ref in zip(pieces, adds, refs):
            ref[:size] = (product[start : start + size] + add_ref[add : add + size].astype(F32)).astype(ref.dtype)
            start += size


def make_grads(pieces, adds, dtypes, token, acol, arow, exps, unit, add, carry, name):
    count = sum(size for _, size in pieces)
    sizes = [count] if adds is None else [size for _, size in pieces]
    if carry is not None:
        sizes[0] += 16
    exps = pltpu.with_memory_space_constraint(exps, pltpu.VMEM)
    unit = pltpu.with_memory_space_constraint(unit, pltpu.VMEM)
    operands = [after(acol, token), arow, exps, unit]
    operands += [] if adds is None else [add]
    operands += [] if carry is None else [carry]
    return pl.pallas_call(
        functools.partial(grads_kernel, pieces, adds, carry is not None),
        out_shape=tuple(jax.ShapeDtypeStruct((size, E), dtype) for size, dtype in zip(sizes, dtypes)),
        in_specs=[vmem()] * len(operands),
        out_specs=(vmem(),) * len(sizes),
        compiler_params=params(16),
        cost_estimate=pl.CostEstimate(
            flops=2 * count * COLS * E,
            bytes_accessed=COLS * (count + E) * 2,
            transcendentals=0,
        ),
        name=name,
    )(*operands)


def far_kernel(raw_ref, core_ref, loss_ref, out_ref):
    out_ref[:ROWS] = (raw_ref[...] + core_ref[256:512].astype(F32)).astype(BF16)
    out_ref[ROWS:] = in_parts(of_parts(loss_ref[...]) + of_parts(core_ref[768:]))


def two_kernel(held_ref, far_ref, out_ref):
    out_ref[:ROWS] = (held_ref[...] + far_ref[:ROWS].astype(F32)).astype(BF16)
    out_ref[ROWS:] = far_ref[ROWS:]


def make_sum(kernel, operands, name):
    return pl.pallas_call(
        kernel,
        out_shape=jax.ShapeDtypeStruct((ROWS + 16, E), BF16),
        in_specs=[vmem()] * len(operands),
        out_specs=vmem(),
        compiler_params=params(4),
        name=name,
    )(*operands)


def final_kernel(z_ref, mates_ref, own_ref, one_ref, two_ref, here_ref, passed_ref, grad_ref, loss_ref):
    zf = z_ref[...].astype(F32)
    recip = lax.rsqrt(jnp.sum(zf * zf, axis=1, keepdims=True) + 1e-06)
    unit = zf * recip
    acc = own_ref[...] + one_ref[:ROWS].astype(F32) + two_ref[:ROWS].astype(F32)
    grad_unit = INV_TAU * (acc - 2.0 * mates_ref[...].astype(F32))
    along = jnp.sum(unit * grad_unit, axis=1, keepdims=True)
    grad_ref[...] = recip * (grad_unit - unit * along)
    loss = ring_sum(*[of_parts(ref[ROWS:]) for ref in (here_ref, passed_ref, one_ref, two_ref)])
    loss_ref[...] = loss[:, :1] / (ROWS * 128)


def make_final(operands):
    return pl.pallas_call(
        final_kernel,
        out_shape=(jax.ShapeDtypeStruct((ROWS, E), F32), jax.ShapeDtypeStruct((1, 1), F32)),
        in_specs=[vmem()] * len(operands),
        out_specs=(vmem(), vmem()),
        compiler_params=params(4),
        name="final",
    )(*operands)


def per_device(embeds, partner):
    unit = make_unit(embeds)
    core_id = lax.axis_index("core")
    z = lax.axis_index("zhi") * 2 + lax.axis_index("zlo")
    info = jnp.stack([lax.axis_index("x"), lax.axis_index("y"), z, core_id]).astype(jnp.int32)

    z_one = get(unit, z_own=-1)
    before, next_ = get(unit, first=-1), get(unit, first=1)
    before, next_ = lax.optimization_barrier((before, next_))
    far = get(unit, first=2)
    near = jnp.concatenate([unit, z_one], axis=0)
    line0 = jnp.concatenate([after(unit, near), before], axis=0)
    line1 = jnp.concatenate([next_, far], axis=0)
    before0, after0 = get(line0, second=-1), get(line0, second=1)
    before1, after1 = get(line1, second=-1), get(line1, second=1)
    z_two = get(unit, z_own=1)
    z_far = get(z_one, z_own=-1)
    near = [near, get(near, core=1)]

    mates, positive = make_mates(unit, partner)
    chain = make_exps(info, near, (0,), [line0, line1], (0, 1), None, None, "exps0")
    rest = jnp.concatenate([z_two, z_far], axis=0)
    rest = [rest, get(rest, core=1)]
    chain = make_exps(info, rest, (1,), [line0, line1], (0, 1), chain, None, "exps1")
    far0 = get(after(before0, after0, chain[0]), second=-1)
    rows = near + rest
    chain = make_exps(info, rows, (0, 1), [before0, after0], (2, 4), chain, None, "exps2")
    far1 = get(after(after1, before1, chain[0]), second=1)
    chain = make_exps(info, rows, (0, 1), [before1, after1, far0], (3, 5, 6), chain, None, "exps3")
    chain = make_exps(info, rows, (0, 1), [far1], (7,), chain, positive, "exps4")
    _, _, exps, units, sums, col_sums = chain

    by_row = sums + get(sums, core=1)
    by_col = col_sums + swap(col_sums, "first", 0)
    by_col = by_col + swap(after(by_col, by_row), "first", 1)
    by_row = by_row + swap(by_row, "z", 0)
    by_col = by_col + swap(by_col, "second", 0)
    by_col = after(by_col, by_row)
    by_row = [by_row, swap(by_row, "z", 1)]
    by_col = [by_col, swap(by_col, "second", 1)]
    arow, acol, loss = make_totals(info, by_row, by_col)

    given = (acol, arow, exps, units)
    (theirs,) = make_grads(((1536, 512), (768, ROWS)), None, (BF16,), info, *given, None, loss, "grads_core")
    core = get(theirs, core=1)
    (far,) = make_grads(((1280, ROWS),), None, (F32,), theirs, *given, None, None, "grads_far")
    far = make_sum(far_kernel, (far, core, loss), "sum_far")
    passed = get(far, z_own=-1)
    free, held = make_grads(
        ((256, ROWS), (1024, ROWS)), (512, 0), (BF16, F32), info, *given, core, far, "grads_near"
    )
    one = get(free, z_own=1)
    (theirs,) = make_grads(((512, ROWS),), None, (BF16,), held, *given, None, None, "grads_core_own")
    core = get(theirs, core=1)
    two = make_sum(two_kernel, (held, passed), "sum_two")
    token = two
    two = get(two, z_own=-1)
    (own,) = make_grads(((0, ROWS),), (0,), (F32,), token, *given, core, None, "grads_own")
    grad, loss = make_final((embeds, mates, own, one, two, far, passed))
    return (loss[0, 0], grad)


def solution(mesh):
    torus = Mesh(mesh.devices.reshape(SIZES), AXES)
    return jax.shard_map(
        per_device,
        mesh=torus,
        in_specs=(P(AXES, None), P(AXES)),
        out_specs=(P(), P(AXES, None)),
        check_vma=False,
    )
```

```python
import functools
import math

import jax
import jax.numpy as jnp
from jax import lax
from jax.experimental import pallas as pl
from jax.experimental.pallas import tpu as pltpu
from jax.sharding import Mesh, PartitionSpec as P

INV_TAU = 10.0
EXP_SCALE = INV_TAU * math.log2(math.e)
AXES = ("zlo", "core", "y", "x", "zhi")
SIZES = (2, 2, 4, 4, 2)
OFFSETS = (0, -1, 1, 2)
NT = (((1,), (1,)), ((), ()))
NN = (((1,), (0,)), ((), ()))
ROWS = 256
ALL_ROWS = 2048
COLS = 4096
TILE = 512
MIB = 1024 * 1024
E = 512
BF16 = jnp.bfloat16
F32 = jnp.float32


def place(x, y, z, core):
    return ((((z % 2) * 2 + core) * 4 + y) * 4 + x) * 2 + z // 2


def get(value, z=0, core=0, first=0, second=0, z_own=0):
    pairs = []
    for px in range(4):
        for py in range(4):
            for pz in range(4):
                for pc in range(2):
                    x, y = (first, second) if pc == 0 else (second, first)
                    away = z + (z_own if pc == 0 else -z_own)
                    source = place((px + x) % 4, (py + y) % 4, (pz + away) % 4, pc ^ core)
                    pairs.append((source, place(px, py, pz, pc)))
    return lax.ppermute(value, AXES, pairs)


def swap(value, way, step):
    pairs = []
    for px in range(4):
        for py in range(4):
            for pz in range(4):
                for pc in range(2):
                    at = [px, py, pz]
                    axis = {"z": 2, "first": pc, "second": 1 - pc}[way]
                    at[axis] = at[axis] ^ 1 if step == 0 else 3 - at[axis]
                    pairs.append((place(*at, pc), place(px, py, pz, pc)))
    return lax.ppermute(value, AXES, pairs)


def ring_sum(own, before, after, far):
    return (own + far) + (before + after)


def after(value, *others):
    return lax.optimization_barrier((value, *others))[0]


def vmem():
    return pl.BlockSpec(memory_space=pltpu.VMEM)


def smem():
    return pl.BlockSpec(memory_space=pltpu.SMEM)


def hbm():
    return pl.BlockSpec(memory_space=pltpu.HBM)


def params(mib):
    return pltpu.CompilerParams(vmem_limit_bytes=mib * MIB)


def block_of(z, core):
    return ((z & 1) * 2 + core) * 2 + lax.shift_right_logical(z, 1)


def row_blocks(info_ref):
    for c in range(2):
        core = info_ref[3] ^ c
        up = 1 - 2 * core
        for k, away in enumerate((0, -up, up, 2)):
            yield (k // 2) * 1024 + c * 512 + (k % 2) * ROWS, block_of((info_ref[2] + away) & 3, core)


def col_blocks(info_ref):
    for two in OFFSETS:
        for one in OFFSETS:
            x = info_ref[0] + jnp.where(info_ref[3] == 0, one, two)
            y = info_ref[1] + jnp.where(info_ref[3] == 0, two, one)
            yield (y & 3) * 4 + (x & 3)


def in_parts(value):
    high = value.astype(BF16)
    rest = value - high.astype(F32)
    middle = rest.astype(BF16)
    low = (rest - middle.astype(F32)).astype(BF16)
    rows = [high.astype(F32), middle.astype(F32), low.astype(F32), jnp.zeros((13, value.shape[1]), F32)]
    return jnp.concatenate(rows, axis=0).astype(BF16)


def of_parts(block):
    rows = block.astype(F32)
    return rows[0:1] + (rows[1:2] + rows[2:3])


def unit_kernel(z_ref, unit_ref):
    zf = z_ref[...].astype(F32)
    recip = lax.rsqrt(jnp.sum(zf * zf, axis=1, keepdims=True) + 1e-06)
    unit_ref[...] = (zf * recip).astype(BF16)


def make_unit(embeds):
    return pl.pallas_call(
        unit_kernel,
        out_shape=jax.ShapeDtypeStruct((ROWS, E), BF16),
        in_specs=[vmem()],
        out_specs=vmem(),
        compiler_params=params(4),
        name="unit",
    )(embeds)


def mates_kernel(unit_ref, partner_ref, mates_ref, positive_ref):
    unit = unit_ref[...]
    ids = lax.broadcasted_iota(jnp.int32, (ROWS, ROWS), 0)
    pick = (ids == (partner_ref[...] & (ROWS - 1))).astype(F32).astype(BF16)
    mates = lax.dot_general(pick, unit, NN, preferred_element_type=F32)
    mates_ref[...] = mates.astype(BF16)
    products = jnp.sum(unit.astype(F32) * mates, axis=0, keepdims=True)
    total = jnp.sum(products, axis=1, keepdims=True) * INV_TAU
    positive_ref[...] = jnp.broadcast_to(total, (1, 128))


def make_mates(unit, partner):
    return pl.pallas_call(
        mates_kernel,
        out_shape=(
            jax.ShapeDtypeStruct((ROWS, E), BF16),
            jax.ShapeDtypeStruct((1, 128), F32),
        ),
        in_specs=[vmem(), vmem()],
        out_specs=(vmem(), vmem()),
        compiler_params=params(4),
        name="mates",
    )(unit, partner.reshape(1, ROWS))


def exps_kernel(places, rows_here, first, last, *refs):
    count = len(places)
    info_ref, refs = refs[0], refs[1:]
    row_refs, refs = refs[: 2 * len(rows_here)], refs[2 * len(rows_here) :]
    col_refs, refs = refs[:count], refs[count:]
    if not first:
        refs = refs[4:]
    if last:
        positive_ref, refs = refs[0], refs[1:]
    sums_ref, col_sums_ref, exps_ref, unit_ref = refs[:4]
    if first:
        sums_ref[...] = jnp.zeros_like(sums_ref)
        col_sums_ref[...] = jnp.zeros_like(col_sums_ref)
    for n, col_ref in enumerate(col_refs):
        if 0 in rows_here:
            start = places[n] * TILE
            unit_ref[start : start + col_ref.shape[0]] = col_ref[...]

        @pl.loop(0, col_ref.shape[0] // ROWS)
        def _(m):
            here = pl.ds(pl.multiple_of(places[n] * TILE + m * ROWS, ROWS), ROWS)
            cols = col_ref[pl.ds(pl.multiple_of(m * ROWS, ROWS), ROWS), :]
            by_col = col_sums_ref[:, here]
            for k, ref in enumerate(row_refs):
                start = rows_here[k // 2] * 1024 + (k % 2) * 512
                part = slice(start, start + 512)
                s = lax.dot_general(ref[...], cols, NT, preferred_element_type=F32)
                e = jnp.exp2(s * EXP_SCALE)
                if first and n == 0 and k == 0:
                    i = lax.broadcasted_iota(jnp.int32, (ROWS, ROWS), 0)
                    j = lax.broadcasted_iota(jnp.int32, (ROWS, ROWS), 1)
                    own = jnp.where(i == j + m * ROWS, 0.0, e[:ROWS])
                    e = jnp.concatenate([own, e[ROWS:]], axis=0)
                exps_ref[part, here] = e.astype(BF16)
                sums_ref[part] += e[:, :128] + e[:, 128:]
                by_col += jnp.sum(e.reshape(-1, 8, ROWS), axis=0)
            col_sums_ref[:, here] = by_col

    if last:
        line_ref, col_line_ref = refs[4:]
        totals = jnp.sum(sums_ref[...].T, axis=0, keepdims=True)
        for start, at in row_blocks(info_ref):
            line_ref[pl.ds(at, 1), :] = totals[:, start : start + ROWS]
        totals = jnp.sum(col_sums_ref[...], axis=0, keepdims=True)
        col_line_ref[...] = jnp.zeros_like(col_line_ref)
        for n, at in enumerate(col_blocks(info_ref)):
            col_line_ref[pl.ds(at, 1), :] = totals[:, n * ROWS : (n + 1) * ROWS]
        col_line_ref[16:17, 0:128] = positive_ref[...]


def make_exps(info, rows, rows_here, cols, places, chain, positive, weight, name):
    first, last = chain is None, positive is not None
    count = len(cols)
    tiles = sum(c.shape[0] for c in cols) // TILE
    operands = [info, *rows, *cols] + ([] if first else list(chain[:4])) + ([positive] if last else [])
    out_shape = (
        pltpu.VMEM((ALL_ROWS, 128), F32),
        pltpu.VMEM((8, COLS), F32),
        pltpu.VMEM((ALL_ROWS, COLS), BF16),
        pltpu.VMEM((COLS, E), BF16),
    )
    if last:
        out_shape += (jax.ShapeDtypeStruct((8, ROWS), F32), jax.ShapeDtypeStruct((24, ROWS), F32))
    start = 1 + len(rows) + count
    return pl.pallas_call(
        functools.partial(exps_kernel, places, rows_here, first, last),
        out_shape=out_shape,
        in_specs=[smem()] + [vmem()] * (len(operands) - 1),
        out_specs=(vmem(),) * len(out_shape),
        input_output_aliases={} if first else {start + n: n for n in range(4)},
        compiler_params=params(12),
        cost_estimate=pl.CostEstimate(
            flops=2 * len(rows) * 512 * tiles * TILE * E * weight,
            bytes_accessed=tiles * TILE * E * 2 * weight,
            transcendentals=len(rows) * 512 * tiles * TILE * weight,
        ),
        name=name,
    )(*operands)


def totals_kernel(info_ref, *refs):
    row_refs, col_refs, (arow_ref, acol_ref, loss_ref, recips, col_recips) = refs[:2], refs[2:4], refs[4:]
    recips[...] = 1.0 / (row_refs[0][...] + row_refs[1][...])
    both = col_refs[0][...] + col_refs[1][...]
    totals = both[:16]
    col_recips[...] = 1.0 / totals
    logs = jnp.sum(jnp.sum(jnp.log(totals), axis=0, keepdims=True), axis=1, keepdims=True)
    loss = jnp.broadcast_to(logs, (1, 128)) - both[16:17, :128]
    loss_ref[...] = in_parts(jnp.concatenate([loss] * (E // 128), axis=1))
    for start, at in row_blocks(info_ref):
        line = recips[pl.ds(at, 1), :]
        arow_ref[start : start + ROWS] = jnp.broadcast_to(line, (128, ROWS)).T.astype(BF16)
    for n, at in enumerate(col_blocks(info_ref)):
        line = col_recips[pl.ds(at, 1), :]
        acol_ref[2 * n : 2 * n + 1] = line[:, :128]
        acol_ref[2 * n + 1 : 2 * n + 2] = line[:, 128:]


def make_totals(info, by_row, by_col):
    return pl.pallas_call(
        totals_kernel,
        out_shape=(
            jax.ShapeDtypeStruct((ALL_ROWS, 128), BF16),
            jax.ShapeDtypeStruct((32, 128), F32),
            jax.ShapeDtypeStruct((16, E), BF16),
        ),
        in_specs=[smem()] + [vmem()] * 4,
        out_specs=(vmem(), vmem(), vmem()),
        scratch_shapes=[pltpu.VMEM((8, ROWS), F32), pltpu.VMEM((16, ROWS), F32)],
        compiler_params=params(4),
        name="totals",
    )(info, *by_row, *by_col)


def grads_kernel(pieces, adds, carries, acol_ref, arow_ref, exps_ref, unit_ref, *refs):
    if adds is not None:
        add_ref, refs = refs[0], refs[1:]
    if carries:
        carry_ref, refs = refs[0], refs[1:]
        end = refs[0].shape[0]
        refs[0][end - 16 : end] = carry_ref[carry_ref.shape[0] - 16 : carry_ref.shape[0]]
    cols = [acol_ref[g : g + 1].astype(BF16) for g in range(COLS // 128)]

    def weights(here):
        a = arow_ref[here]
        return exps_ref[here] * jnp.concatenate([a + col for col in cols], axis=1)

    if adds is None:
        to = 0
        for start, size in pieces:
            w = weights(slice(start, start + size))
            product = lax.dot_general(w, unit_ref[...], NN, preferred_element_type=F32)
            refs[0][to : to + size] = product.astype(refs[0].dtype)
            to += size

    else:
        w = jnp.concatenate([weights(slice(start, start + size)) for start, size in pieces], axis=0)
        product = lax.dot_general(w, unit_ref[...], NN, preferred_element_type=F32)
        start = 0
        for (_, size), add, ref in zip(pieces, adds, refs):
            ref[:size] = (product[start : start + size] + add_ref[add : add + size].astype(F32)).astype(ref.dtype)
            start += size


def make_grads(pieces, adds, dtypes, token, acol, arow, exps, unit, add, carry, name):
    count = sum(size for _, size in pieces)
    sizes = [count] if adds is None else [size for _, size in pieces]
    if carry is not None:
        sizes[0] += 16
    exps = pltpu.with_memory_space_constraint(exps, pltpu.VMEM)
    unit = pltpu.with_memory_space_constraint(unit, pltpu.VMEM)
    operands = [after(acol, token), arow, exps, unit]
    operands += [] if adds is None else [add]
    operands += [] if carry is None else [carry]
    return pl.pallas_call(
        functools.partial(grads_kernel, pieces, adds, carry is not None),
        out_shape=tuple(jax.ShapeDtypeStruct((size, E), dtype) for size, dtype in zip(sizes, dtypes)),
        in_specs=[vmem()] * len(operands),
        out_specs=(vmem(),) * len(sizes),
        compiler_params=params(16),
        cost_estimate=pl.CostEstimate(
            flops=2 * count * COLS * E,
            bytes_accessed=COLS * (count + E) * 2,
            transcendentals=0,
        ),
        name=name,
    )(*operands)


def far_kernel(raw_ref, core_ref, loss_ref, out_ref):
    out_ref[:ROWS] = (raw_ref[...] + core_ref[256:512].astype(F32)).astype(BF16)
    out_ref[ROWS:] = in_parts(of_parts(loss_ref[...]) + of_parts(core_ref[768:]))


def two_kernel(held_ref, far_ref, out_ref):
    out_ref[:ROWS] = (held_ref[...] + far_ref[:ROWS].astype(F32)).astype(BF16)
    out_ref[ROWS:] = far_ref[ROWS:]


def make_sum(kernel, operands, name):
    return pl.pallas_call(
        kernel,
        out_shape=jax.ShapeDtypeStruct((ROWS + 16, E), BF16),
        in_specs=[vmem()] * len(operands),
        out_specs=vmem(),
        compiler_params=params(4),
        name=name,
    )(*operands)


def final_kernel(z_ref, mates_ref, own_ref, one_ref, two_ref, here_ref, passed_ref, grad_ref, loss_ref):
    zf = z_ref[...].astype(F32)
    recip = lax.rsqrt(jnp.sum(zf * zf, axis=1, keepdims=True) + 1e-06)
    unit = zf * recip
    acc = own_ref[...] + one_ref[:ROWS].astype(F32) + two_ref[:ROWS].astype(F32)
    grad_unit = INV_TAU * (acc - 2.0 * mates_ref[...].astype(F32))
    along = jnp.sum(unit * grad_unit, axis=1, keepdims=True)
    grad_ref[...] = recip * (grad_unit - unit * along)
    loss = ring_sum(*[of_parts(ref[ROWS:]) for ref in (here_ref, passed_ref, one_ref, two_ref)])
    loss_ref[...] = loss[:, :1] / (ROWS * 128)


def make_final(operands):
    return pl.pallas_call(
        final_kernel,
        out_shape=(jax.ShapeDtypeStruct((ROWS, E), F32), jax.ShapeDtypeStruct((1, 1), F32)),
        in_specs=[vmem()] * len(operands),
        out_specs=(vmem(), vmem()),
        compiler_params=params(4),
        name="final",
    )(*operands)


def per_device(embeds, partner):
    unit = make_unit(embeds)
    core_id = lax.axis_index("core")
    z = lax.axis_index("zhi") * 2 + lax.axis_index("zlo")
    info = jnp.stack([lax.axis_index("x"), lax.axis_index("y"), z, core_id]).astype(jnp.int32)

    z_one = get(unit, z_own=-1)
    before, next_ = get(unit, first=-1), get(unit, first=1)
    before, next_ = lax.optimization_barrier((before, next_))
    far = get(unit, first=2)
    near = jnp.concatenate([unit, z_one], axis=0)
    line0 = jnp.concatenate([after(unit, near), before], axis=0)
    line1 = jnp.concatenate([next_, far], axis=0)
    before0, after0 = get(line0, second=-1), get(line0, second=1)
    before1, after1 = get(line1, second=-1), get(line1, second=1)
    z_two = get(unit, z_own=1)
    z_far = get(z_one, z_own=-1)
    near = [near, get(near, core=1)]

    mates, positive = make_mates(unit, partner)
    chain = make_exps(info, near, (0,), [line0, line1], (0, 1), None, None, 8, "exps0")
    rest = jnp.concatenate([z_two, z_far], axis=0)
    rest = [rest, get(rest, core=1)]
    chain = make_exps(info, rest, (1,), [line0, line1], (0, 1), chain, None, 8, "exps1")
    far0 = get(after(before0, after0, chain[0]), second=-1)
    rows = near + rest
    chain = make_exps(info, rows, (0, 1), [before0], (2,), chain, None, 4, "exps2")
    far1 = get(after(after1, before1, chain[0]), second=1)
    chain = make_exps(info, rows, (0, 1), [after0, before1, after1], (4, 3, 5), chain, None, 0, "exps3")
    chain = make_exps(info, rows, (0, 1), [far0], (6,), chain, None, 0, "exps4")
    chain = make_exps(info, rows, (0, 1), [far1], (7,), chain, positive, 0, "exps5")
    _, _, exps, units, sums, col_sums = chain

    by_row = sums + get(sums, core=1)
    by_col = col_sums + swap(col_sums, "first", 0)
    by_col = by_col + swap(after(by_col, by_row), "first", 1)
    by_row = by_row + swap(by_row, "z", 0)
    by_col = by_col + swap(by_col, "second", 0)
    by_col = after(by_col, by_row)
    by_row = [by_row, swap(by_row, "z", 1)]
    by_col = [by_col, swap(by_col, "second", 1)]
    arow, acol, loss = make_totals(info, by_row, by_col)

    given = (acol, arow, exps, units)
    (theirs,) = make_grads(((1536, 512), (768, ROWS)), None, (BF16,), info, *given, None, loss, "grads_core")
    core = get(theirs, core=1)
    (far,) = make_grads(((1280, ROWS),), None, (F32,), theirs, *given, None, None, "grads_far")
    far = make_sum(far_kernel, (far, core, loss), "sum_far")
    passed = get(far, z_own=-1)
    free, held = make_grads(
        ((256, ROWS), (1024, ROWS)), (512, 0), (BF16, F32), info, *given, core, far, "grads_near"
    )
    one = get(free, z_own=1)
    (theirs,) = make_grads(((512, ROWS),), None, (BF16,), held, *given, None, None, "grads_core_own")
    core = get(theirs, core=1)
    two = make_sum(two_kernel, (held, passed), "sum_two")
    token = two
    two = get(two, z_own=-1)
    (own,) = make_grads(((0, ROWS),), (0,), (F32,), token, *given, core, None, "grads_own")
    grad, loss = make_final((embeds, mates, own, one, two, far, passed))
    return (loss[0, 0], grad)


def solution(mesh):
    torus = Mesh(mesh.devices.reshape(SIZES), AXES)
    return jax.shard_map(
        per_device,
        mesh=torus,
        in_specs=(P(AXES, None), P(AXES)),
        out_specs=(P(), P(AXES, None)),
        check_vma=False,
    )
```

```python
import functools
import math

import jax
import jax.numpy as jnp
from jax import lax
from jax.experimental import pallas as pl
from jax.experimental.pallas import tpu as pltpu
from jax.sharding import Mesh, PartitionSpec as P

INV_TAU = 10.0
EXP_SCALE = INV_TAU * math.log2(math.e)
AXES = ("zlo", "core", "y", "x", "zhi")
SIZES = (2, 2, 4, 4, 2)
OFFSETS = (0, -1, 1, 2)
NT = (((1,), (1,)), ((), ()))
NN = (((1,), (0,)), ((), ()))
ROWS = 256
ALL_ROWS = 2048
COLS = 4096
TILE = 512
MIB = 1024 * 1024
E = 512
BF16 = jnp.bfloat16
F32 = jnp.float32


def place(x, y, z, core):
    return ((((z % 2) * 2 + core) * 4 + y) * 4 + x) * 2 + z // 2


def get(value, z=0, core=0, first=0, second=0, z_own=0):
    pairs = []
    for px in range(4):
        for py in range(4):
            for pz in range(4):
                for pc in range(2):
                    x, y = (first, second) if pc == 0 else (second, first)
                    away = z + (z_own if pc == 0 else -z_own)
                    source = place((px + x) % 4, (py + y) % 4, (pz + away) % 4, pc ^ core)
                    pairs.append((source, place(px, py, pz, pc)))
    return lax.ppermute(value, AXES, pairs)


def swap(value, way, step):
    pairs = []
    for px in range(4):
        for py in range(4):
            for pz in range(4):
                for pc in range(2):
                    at = [px, py, pz]
                    axis = {"z": 2, "first": pc, "second": 1 - pc}[way]
                    at[axis] = at[axis] ^ 1 if step == 0 else 3 - at[axis]
                    pairs.append((place(*at, pc), place(px, py, pz, pc)))
    return lax.ppermute(value, AXES, pairs)


def ring_sum(own, before, after, far):
    return (own + far) + (before + after)


def after(value, *others):
    return lax.optimization_barrier((value, *others))[0]


def vmem():
    return pl.BlockSpec(memory_space=pltpu.VMEM)


def smem():
    return pl.BlockSpec(memory_space=pltpu.SMEM)


def hbm():
    return pl.BlockSpec(memory_space=pltpu.HBM)


def params(mib):
    return pltpu.CompilerParams(vmem_limit_bytes=mib * MIB)


def block_of(z, core):
    return ((z & 1) * 2 + core) * 2 + lax.shift_right_logical(z, 1)


def row_blocks(info_ref):
    for c in range(2):
        core = info_ref[3] ^ c
        up = 1 - 2 * core
        for k, away in enumerate((0, -up, up, 2)):
            yield (k // 2) * 1024 + c * 512 + (k % 2) * ROWS, block_of((info_ref[2] + away) & 3, core)


def col_blocks(info_ref):
    for two in OFFSETS:
        for one in OFFSETS:
            x = info_ref[0] + jnp.where(info_ref[3] == 0, one, two)
            y = info_ref[1] + jnp.where(info_ref[3] == 0, two, one)
            yield (y & 3) * 4 + (x & 3)


def in_parts(value):
    high = value.astype(BF16)
    rest = value - high.astype(F32)
    middle = rest.astype(BF16)
    low = (rest - middle.astype(F32)).astype(BF16)
    rows = [high.astype(F32), middle.astype(F32), low.astype(F32), jnp.zeros((13, value.shape[1]), F32)]
    return jnp.concatenate(rows, axis=0).astype(BF16)


def of_parts(block):
    rows = block.astype(F32)
    return rows[0:1] + (rows[1:2] + rows[2:3])


def unit_kernel(z_ref, unit_ref, scaled_ref):
    zf = z_ref[...].astype(F32)
    recip = lax.rsqrt(jnp.sum(zf * zf, axis=1, keepdims=True) + 1e-06)
    unit = zf * recip
    unit_ref[...] = unit.astype(BF16)
    scaled_ref[...] = (unit * EXP_SCALE).astype(BF16)


def make_unit(embeds):
    return pl.pallas_call(
        unit_kernel,
        out_shape=(jax.ShapeDtypeStruct((ROWS, E), BF16), jax.ShapeDtypeStruct((ROWS, E), BF16)),
        in_specs=[vmem()],
        out_specs=(vmem(), vmem()),
        compiler_params=params(4),
        name="unit",
    )(embeds)


def mates_kernel(unit_ref, partner_ref, mates_ref, positive_ref):
    unit = unit_ref[...]
    ids = lax.broadcasted_iota(jnp.int32, (ROWS, ROWS), 0)
    pick = (ids == (partner_ref[...] & (ROWS - 1))).astype(F32).astype(BF16)
    mates = lax.dot_general(pick, unit, NN, preferred_element_type=F32)
    mates_ref[...] = mates.astype(BF16)
    products = jnp.sum(unit.astype(F32) * mates, axis=0, keepdims=True)
    total = jnp.sum(products, axis=1, keepdims=True) * INV_TAU
    positive_ref[...] = jnp.broadcast_to(total, (1, 128))


def make_mates(unit, partner):
    return pl.pallas_call(
        mates_kernel,
        out_shape=(
            jax.ShapeDtypeStruct((ROWS, E), BF16),
            jax.ShapeDtypeStruct((1, 128), F32),
        ),
        in_specs=[vmem(), vmem()],
        out_specs=(vmem(), vmem()),
        compiler_params=params(4),
        name="mates",
    )(unit, partner.reshape(1, ROWS))


def exps_kernel(places, rows_here, first, last, *refs):
    count = len(places)
    info_ref, refs = refs[0], refs[1:]
    row_refs, refs = refs[: 2 * len(rows_here)], refs[2 * len(rows_here) :]
    col_refs, refs = refs[:count], refs[count:]
    if not first:
        refs = refs[4:]
    if last:
        positive_ref, refs = refs[0], refs[1:]
    sums_ref, col_sums_ref, exps_ref, unit_ref = refs[:4]
    if first:
        sums_ref[...] = jnp.zeros_like(sums_ref)
        col_sums_ref[...] = jnp.zeros_like(col_sums_ref)
    for n, col_ref in enumerate(col_refs):
        if 0 in rows_here:
            start = places[n] * TILE
            unit_ref[start : start + col_ref.shape[0]] = col_ref[...]

        @pl.loop(0, col_ref.shape[0] // ROWS)
        def _(m):
            here = pl.ds(pl.multiple_of(places[n] * TILE + m * ROWS, ROWS), ROWS)
            cols = col_ref[pl.ds(pl.multiple_of(m * ROWS, ROWS), ROWS), :]
            by_col = col_sums_ref[:, here]
            for k, ref in enumerate(row_refs):
                start = rows_here[k // 2] * 1024 + (k % 2) * 512
                part = slice(start, start + 512)
                e = jnp.exp2(lax.dot_general(ref[...], cols, NT, preferred_element_type=F32))
                if first and n == 0 and k == 0:
                    i = lax.broadcasted_iota(jnp.int32, (ROWS, ROWS), 0)
                    j = lax.broadcasted_iota(jnp.int32, (ROWS, ROWS), 1)
                    own = jnp.where(i == j + m * ROWS, 0.0, e[:ROWS])
                    e = jnp.concatenate([own, e[ROWS:]], axis=0)
                exps_ref[part, here] = e.astype(BF16)
                sums_ref[part] += e[:, :128] + e[:, 128:]
                by_col += jnp.sum(e.reshape(-1, 8, ROWS), axis=0)
            col_sums_ref[:, here] = by_col

    if last:
        line_ref, col_line_ref = refs[4:]
        totals = jnp.sum(sums_ref[...].T, axis=0, keepdims=True)
        for start, at in row_blocks(info_ref):
            line_ref[pl.ds(at, 1), :] = totals[:, start : start + ROWS]
        totals = jnp.sum(col_sums_ref[...], axis=0, keepdims=True)
        col_line_ref[...] = jnp.zeros_like(col_line_ref)
        for n, at in enumerate(col_blocks(info_ref)):
            col_line_ref[pl.ds(at, 1), :] = totals[:, n * ROWS : (n + 1) * ROWS]
        col_line_ref[16:17, 0:128] = positive_ref[...]


def make_exps(info, rows, rows_here, cols, places, chain, positive, weight, name):
    first, last = chain is None, positive is not None
    count = len(cols)
    tiles = sum(c.shape[0] for c in cols) // TILE
    operands = [info, *rows, *cols] + ([] if first else list(chain[:4])) + ([positive] if last else [])
    out_shape = (
        pltpu.VMEM((ALL_ROWS, 128), F32),
        pltpu.VMEM((8, COLS), F32),
        pltpu.VMEM((ALL_ROWS, COLS), BF16),
        pltpu.VMEM((COLS, E), BF16),
    )
    if last:
        out_shape += (jax.ShapeDtypeStruct((8, ROWS), F32), jax.ShapeDtypeStruct((24, ROWS), F32))
    start = 1 + len(rows) + count
    return pl.pallas_call(
        functools.partial(exps_kernel, places, rows_here, first, last),
        out_shape=out_shape,
        in_specs=[smem()] + [vmem()] * (len(operands) - 1),
        out_specs=(vmem(),) * len(out_shape),
        input_output_aliases={} if first else {start + n: n for n in range(4)},
        compiler_params=params(12),
        cost_estimate=pl.CostEstimate(
            flops=2 * len(rows) * 512 * tiles * TILE * E * weight,
            bytes_accessed=tiles * TILE * E * 2 * weight,
            transcendentals=len(rows) * 512 * tiles * TILE * weight,
        ),
        name=name,
    )(*operands)


def totals_kernel(info_ref, *refs):
    row_refs, col_refs, (arow_ref, acol_ref, loss_ref, recips, col_recips) = refs[:2], refs[2:4], refs[4:]
    recips[...] = 1.0 / (row_refs[0][...] + row_refs[1][...])
    both = col_refs[0][...] + col_refs[1][...]
    totals = both[:16]
    col_recips[...] = 1.0 / totals
    logs = jnp.sum(jnp.sum(jnp.log(totals), axis=0, keepdims=True), axis=1, keepdims=True)
    loss = jnp.broadcast_to(logs, (1, 128)) - both[16:17, :128]
    loss_ref[...] = in_parts(jnp.concatenate([loss] * (E // 128), axis=1))
    for start, at in row_blocks(info_ref):
        line = recips[pl.ds(at, 1), :]
        arow_ref[start : start + ROWS] = jnp.broadcast_to(line, (128, ROWS)).T.astype(BF16)
    for n, at in enumerate(col_blocks(info_ref)):
        line = col_recips[pl.ds(at, 1), :]
        acol_ref[2 * n : 2 * n + 1] = line[:, :128]
        acol_ref[2 * n + 1 : 2 * n + 2] = line[:, 128:]


def make_totals(info, by_row, by_col):
    return pl.pallas_call(
        totals_kernel,
        out_shape=(
            jax.ShapeDtypeStruct((ALL_ROWS, 128), BF16),
            jax.ShapeDtypeStruct((32, 128), F32),
            jax.ShapeDtypeStruct((16, E), BF16),
        ),
        in_specs=[smem()] + [vmem()] * 4,
        out_specs=(vmem(), vmem(), vmem()),
        scratch_shapes=[pltpu.VMEM((8, ROWS), F32), pltpu.VMEM((16, ROWS), F32)],
        compiler_params=params(4),
        name="totals",
    )(info, *by_row, *by_col)


def grads_kernel(pieces, adds, carries, acol_ref, arow_ref, exps_ref, unit_ref, *refs):
    if adds is not None:
        add_ref, refs = refs[0], refs[1:]
    if carries:
        carry_ref, refs = refs[0], refs[1:]
        end = refs[0].shape[0]
        refs[0][end - 16 : end] = carry_ref[carry_ref.shape[0] - 16 : carry_ref.shape[0]]
    cols = [acol_ref[g : g + 1].astype(BF16) for g in range(COLS // 128)]

    def weights(here):
        a = arow_ref[here]
        return exps_ref[here] * jnp.concatenate([a + col for col in cols], axis=1)

    if adds is None:
        to = 0
        for start, size in pieces:
            w = weights(slice(start, start + size))
            product = lax.dot_general(w, unit_ref[...], NN, preferred_element_type=F32)
            refs[0][to : to + size] = product.astype(refs[0].dtype)
            to += size

    else:
        w = jnp.concatenate([weights(slice(start, start + size)) for start, size in pieces], axis=0)
        product = lax.dot_general(w, unit_ref[...], NN, preferred_element_type=F32)
        start = 0
        for (_, size), add, ref in zip(pieces, adds, refs):
            ref[:size] = (product[start : start + size] + add_ref[add : add + size].astype(F32)).astype(ref.dtype)
            start += size


def make_grads(pieces, adds, dtypes, token, acol, arow, exps, unit, add, carry, name):
    count = sum(size for _, size in pieces)
    sizes = [count] if adds is None else [size for _, size in pieces]
    if carry is not None:
        sizes[0] += 16
    exps = pltpu.with_memory_space_constraint(exps, pltpu.VMEM)
    unit = pltpu.with_memory_space_constraint(unit, pltpu.VMEM)
    operands = [after(acol, token), arow, exps, unit]
    operands += [] if adds is None else [add]
    operands += [] if carry is None else [carry]
    return pl.pallas_call(
        functools.partial(grads_kernel, pieces, adds, carry is not None),
        out_shape=tuple(jax.ShapeDtypeStruct((size, E), dtype) for size, dtype in zip(sizes, dtypes)),
        in_specs=[vmem()] * len(operands),
        out_specs=(vmem(),) * len(sizes),
        compiler_params=params(16),
        cost_estimate=pl.CostEstimate(
            flops=2 * count * COLS * E,
            bytes_accessed=COLS * (count + E) * 2,
            transcendentals=0,
        ),
        name=name,
    )(*operands)


def far_kernel(raw_ref, core_ref, loss_ref, out_ref):
    out_ref[:ROWS] = (raw_ref[...] + core_ref[256:512].astype(F32)).astype(BF16)
    out_ref[ROWS:] = in_parts(of_parts(loss_ref[...]) + of_parts(core_ref[768:]))


def two_kernel(held_ref, far_ref, out_ref):
    out_ref[:ROWS] = (held_ref[...] + far_ref[:ROWS].astype(F32)).astype(BF16)
    out_ref[ROWS:] = far_ref[ROWS:]


def make_sum(kernel, operands, name):
    return pl.pallas_call(
        kernel,
        out_shape=jax.ShapeDtypeStruct((ROWS + 16, E), BF16),
        in_specs=[vmem()] * len(operands),
        out_specs=vmem(),
        compiler_params=params(4),
        name=name,
    )(*operands)


def final_kernel(z_ref, mates_ref, own_ref, one_ref, two_ref, here_ref, passed_ref, grad_ref, loss_ref):
    zf = z_ref[...].astype(F32)
    recip = lax.rsqrt(jnp.sum(zf * zf, axis=1, keepdims=True) + 1e-06)
    unit = zf * recip
    acc = own_ref[...] + one_ref[:ROWS].astype(F32) + two_ref[:ROWS].astype(F32)
    grad_unit = INV_TAU * (acc - 2.0 * mates_ref[...].astype(F32))
    along = jnp.sum(unit * grad_unit, axis=1, keepdims=True)
    grad_ref[...] = recip * (grad_unit - unit * along)
    loss = ring_sum(*[of_parts(ref[ROWS:]) for ref in (here_ref, passed_ref, one_ref, two_ref)])
    loss_ref[...] = loss[:, :1] / (ROWS * 128)


def make_final(operands):
    return pl.pallas_call(
        final_kernel,
        out_shape=(jax.ShapeDtypeStruct((ROWS, E), F32), jax.ShapeDtypeStruct((1, 1), F32)),
        in_specs=[vmem()] * len(operands),
        out_specs=(vmem(), vmem()),
        compiler_params=params(4),
        name="final",
    )(*operands)


def per_device(embeds, partner):
    unit, scaled = make_unit(embeds)
    core_id = lax.axis_index("core")
    z = lax.axis_index("zhi") * 2 + lax.axis_index("zlo")
    info = jnp.stack([lax.axis_index("x"), lax.axis_index("y"), z, core_id]).astype(jnp.int32)

    z_one = get(scaled, z_own=-1)
    before, next_ = get(unit, first=-1), get(unit, first=1)
    before, next_ = lax.optimization_barrier((before, next_))
    far = get(unit, first=2)
    near = jnp.concatenate([scaled, z_one], axis=0)
    line0 = jnp.concatenate([after(unit, near), before], axis=0)
    line1 = jnp.concatenate([next_, far], axis=0)
    before0, after0 = get(line0, second=-1), get(line0, second=1)
    before1, after1 = get(line1, second=-1), get(line1, second=1)
    z_two = get(scaled, z_own=1)
    z_far = get(z_one, z_own=-1)
    near = [near, get(near, core=1)]

    mates, positive = make_mates(unit, partner)
    chain = make_exps(info, near, (0,), [line0, line1], (0, 1), None, None, 8, "exps0")
    rest = jnp.concatenate([z_two, z_far], axis=0)
    rest = [rest, get(rest, core=1)]
    chain = make_exps(info, rest, (1,), [line0, line1], (0, 1), chain, None, 8, "exps1")
    far0 = get(after(before0, after0, chain[0]), second=-1)
    rows = near + rest
    chain = make_exps(info, rows, (0, 1), [before0], (2,), chain, None, 4, "exps2")
    far1 = get(after(after1, before1, chain[0]), second=1)
    chain = make_exps(info, rows, (0, 1), [after0, before1, after1], (4, 3, 5), chain, None, 0, "exps3")
    chain = make_exps(info, rows, (0, 1), [far0], (6,), chain, None, 0, "exps4")
    chain = make_exps(info, rows, (0, 1), [far1], (7,), chain, positive, 0, "exps5")
    _, _, exps, units, sums, col_sums = chain

    by_row = sums + get(sums, core=1)
    by_col = col_sums + swap(col_sums, "first", 0)
    by_col = by_col + swap(after(by_col, by_row), "first", 1)
    by_row = by_row + swap(by_row, "z", 0)
    by_col = by_col + swap(after(by_col, by_row), "second", 0)
    by_row = [by_row, swap(by_row, "z", 1)]
    by_col = after(by_col, by_row[1])
    by_col = [by_col, swap(by_col, "second", 1)]
    arow, acol, loss = make_totals(info, by_row, by_col)

    given = (acol, arow, exps, units)
    (theirs,) = make_grads(((1536, 512), (768, ROWS)), None, (BF16,), info, *given, None, loss, "grads_core")
    core = get(theirs, core=1)
    (far,) = make_grads(((1280, ROWS),), None, (F32,), theirs, *given, None, None, "grads_far")
    far = make_sum(far_kernel, (far, core, loss), "sum_far")
    passed = get(far, z_own=-1)
    free, held = make_grads(
        ((256, ROWS), (1024, ROWS)), (512, 0), (BF16, F32), info, *given, core, far, "grads_near"
    )
    one = get(free, z_own=1)
    (theirs,) = make_grads(((512, ROWS),), None, (BF16,), held, *given, None, None, "grads_core_own")
    core = get(theirs, core=1)
    two = make_sum(two_kernel, (held, passed), "sum_two")
    token = two
    two = get(two, z_own=-1)
    (own,) = make_grads(((0, ROWS),), (0,), (F32,), token, *given, core, None, "grads_own")
    grad, loss = make_final((embeds, mates, own, one, two, far, passed))
    return (loss[0, 0], grad)


def solution(mesh):
    torus = Mesh(mesh.devices.reshape(SIZES), AXES)
    return jax.shard_map(
        per_device,
        mesh=torus,
        in_specs=(P(AXES, None), P(AXES)),
        out_specs=(P(), P(AXES, None)),
        check_vma=False,
    )
```

```python
import functools
import math

import jax
import jax.numpy as jnp
from jax import lax
from jax.experimental import pallas as pl
from jax.experimental.pallas import tpu as pltpu
from jax.sharding import Mesh, PartitionSpec as P

INV_TAU = 10.0
EXP_SCALE = INV_TAU * math.log2(math.e)
AXES = ("zlo", "core", "y", "x", "zhi")
SIZES = (2, 2, 4, 4, 2)
OFFSETS = (0, -1, 1, 2)
NT = (((1,), (1,)), ((), ()))
NN = (((1,), (0,)), ((), ()))
ROWS = 256
ALL_ROWS = 2048
COLS = 4096
TILE = 512
MIB = 1024 * 1024
E = 512
BF16 = jnp.bfloat16
F32 = jnp.float32


def place(x, y, z, core):
    return ((((z % 2) * 2 + core) * 4 + y) * 4 + x) * 2 + z // 2


def get(value, z=0, core=0, first=0, second=0, z_own=0):
    pairs = []
    for px in range(4):
        for py in range(4):
            for pz in range(4):
                for pc in range(2):
                    x, y = (first, second) if pc == 0 else (second, first)
                    away = z + (z_own if pc == 0 else -z_own)
                    source = place((px + x) % 4, (py + y) % 4, (pz + away) % 4, pc ^ core)
                    pairs.append((source, place(px, py, pz, pc)))
    return lax.ppermute(value, AXES, pairs)


def swap(value, way, step):
    pairs = []
    for px in range(4):
        for py in range(4):
            for pz in range(4):
                for pc in range(2):
                    at = [px, py, pz]
                    axis = {"z": 2, "first": pc, "second": 1 - pc}[way]
                    at[axis] = at[axis] ^ 1 if step == 0 else 3 - at[axis]
                    pairs.append((place(*at, pc), place(px, py, pz, pc)))
    return lax.ppermute(value, AXES, pairs)


def ring_sum(own, before, after, far):
    return (own + far) + (before + after)


def after(value, *others):
    return lax.optimization_barrier((value, *others))[0]


def vmem():
    return pl.BlockSpec(memory_space=pltpu.VMEM)


def smem():
    return pl.BlockSpec(memory_space=pltpu.SMEM)


def hbm():
    return pl.BlockSpec(memory_space=pltpu.HBM)


def params(mib):
    return pltpu.CompilerParams(vmem_limit_bytes=mib * MIB)


def block_of(z, core):
    return ((z & 1) * 2 + core) * 2 + lax.shift_right_logical(z, 1)


def row_blocks(info_ref):
    for c in range(2):
        core = info_ref[3] ^ c
        up = 1 - 2 * core
        for k, away in enumerate((0, -up, up, 2)):
            yield (k // 2) * 1024 + c * 512 + (k % 2) * ROWS, block_of((info_ref[2] + away) & 3, core)


def col_blocks(info_ref):
    for two in OFFSETS:
        for one in OFFSETS:
            x = info_ref[0] + jnp.where(info_ref[3] == 0, one, two)
            y = info_ref[1] + jnp.where(info_ref[3] == 0, two, one)
            yield (y & 3) * 4 + (x & 3)


def in_parts(value):
    high = value.astype(BF16)
    rest = value - high.astype(F32)
    middle = rest.astype(BF16)
    low = (rest - middle.astype(F32)).astype(BF16)
    rows = [high.astype(F32), middle.astype(F32), low.astype(F32), jnp.zeros((13, value.shape[1]), F32)]
    return jnp.concatenate(rows, axis=0).astype(BF16)


def of_parts(block):
    rows = block.astype(F32)
    return rows[0:1] + (rows[1:2] + rows[2:3])


def unit_kernel(z_ref, unit_ref, scaled_ref):
    zf = z_ref[...].astype(F32)
    recip = lax.rsqrt(jnp.sum(zf * zf, axis=1, keepdims=True) + 1e-06)
    unit = zf * recip
    unit_ref[...] = unit.astype(BF16)
    scaled_ref[...] = (unit * EXP_SCALE).astype(BF16)


def make_unit(embeds):
    return pl.pallas_call(
        unit_kernel,
        out_shape=(jax.ShapeDtypeStruct((ROWS, E), BF16), jax.ShapeDtypeStruct((ROWS, E), BF16)),
        in_specs=[vmem()],
        out_specs=(vmem(), vmem()),
        compiler_params=params(4),
        name="unit",
    )(embeds)


def mates_kernel(unit_ref, partner_ref, mates_ref, positive_ref):
    unit = unit_ref[...]
    ids = lax.broadcasted_iota(jnp.int32, (ROWS, ROWS), 0)
    pick = (ids == (partner_ref[...] & (ROWS - 1))).astype(F32).astype(BF16)
    mates = lax.dot_general(pick, unit, NN, preferred_element_type=F32)
    mates_ref[...] = mates.astype(BF16)
    products = jnp.sum(unit.astype(F32) * mates, axis=0, keepdims=True)
    total = jnp.sum(products, axis=1, keepdims=True) * INV_TAU
    positive_ref[...] = jnp.broadcast_to(total, (1, 128))


def make_mates(unit, partner):
    return pl.pallas_call(
        mates_kernel,
        out_shape=(
            jax.ShapeDtypeStruct((ROWS, E), BF16),
            jax.ShapeDtypeStruct((1, 128), F32),
        ),
        in_specs=[vmem(), vmem()],
        out_specs=(vmem(), vmem()),
        compiler_params=params(4),
        name="mates",
    )(unit, partner.reshape(1, ROWS))


def exps_kernel(places, rows_here, olds, first, last, *refs):
    count = len(places)
    info_ref, refs = refs[0], refs[1:]
    row_refs, refs = refs[: 2 * len(rows_here)], refs[2 * len(rows_here) :]
    col_refs, refs = refs[:count], refs[count:]
    if not first:
        refs = refs[4:]
    if last:
        positive_ref, refs = refs[0], refs[1:]
    sums_ref, col_sums_ref, exps_ref, unit_ref = refs[:4]
    if first:
        sums_ref[...] = jnp.zeros_like(sums_ref)
        col_sums_ref[...] = jnp.zeros_like(col_sums_ref)
    for n, col_ref in enumerate(col_refs):
        if 0 in rows_here and n not in olds:
            start = places[n] * TILE
            unit_ref[start : start + col_ref.shape[0]] = col_ref[...]

        @pl.loop(0, col_ref.shape[0] // ROWS)
        def _(m):
            here = pl.ds(pl.multiple_of(places[n] * TILE + m * ROWS, ROWS), ROWS)
            cols = col_ref[pl.ds(pl.multiple_of(m * ROWS, ROWS), ROWS), :]
            by_col = col_sums_ref[:, here]
            for k, ref in enumerate(row_refs):
                if n in olds and rows_here[k // 2] == 0:
                    continue
                start = rows_here[k // 2] * 1024 + (k % 2) * 512
                part = slice(start, start + 512)
                e = jnp.exp2(lax.dot_general(ref[...], cols, NT, preferred_element_type=F32))
                if first and n == 0 and k == 0:
                    i = lax.broadcasted_iota(jnp.int32, (ROWS, ROWS), 0)
                    j = lax.broadcasted_iota(jnp.int32, (ROWS, ROWS), 1)
                    own = jnp.where(i == j + m * ROWS, 0.0, e[:ROWS])
                    e = jnp.concatenate([own, e[ROWS:]], axis=0)
                exps_ref[part, here] = e.astype(BF16)
                sums_ref[part] += e[:, :128] + e[:, 128:]
                by_col += jnp.sum(e.reshape(-1, 8, ROWS), axis=0)
            col_sums_ref[:, here] = by_col

    if last:
        line_ref, col_line_ref = refs[4:]
        totals = jnp.sum(sums_ref[...].T, axis=0, keepdims=True)
        for start, at in row_blocks(info_ref):
            line_ref[pl.ds(at, 1), :] = totals[:, start : start + ROWS]
        totals = jnp.sum(col_sums_ref[...], axis=0, keepdims=True)
        col_line_ref[...] = jnp.zeros_like(col_line_ref)
        for n, at in enumerate(col_blocks(info_ref)):
            col_line_ref[pl.ds(at, 1), :] = totals[:, n * ROWS : (n + 1) * ROWS]
        col_line_ref[16:17, 0:128] = positive_ref[...]


def make_exps(info, rows, rows_here, cols, places, olds, chain, positive, weight, name):
    first, last = chain is None, positive is not None
    count = len(cols)
    tiles = sum(c.shape[0] for c in cols) // TILE
    operands = [info, *rows, *cols] + ([] if first else list(chain[:4])) + ([positive] if last else [])
    out_shape = (
        pltpu.VMEM((ALL_ROWS, 128), F32),
        pltpu.VMEM((8, COLS), F32),
        pltpu.VMEM((ALL_ROWS, COLS), BF16),
        pltpu.VMEM((COLS, E), BF16),
    )
    if last:
        out_shape += (jax.ShapeDtypeStruct((8, ROWS), F32), jax.ShapeDtypeStruct((24, ROWS), F32))
    start = 1 + len(rows) + count
    return pl.pallas_call(
        functools.partial(exps_kernel, places, rows_here, olds, first, last),
        out_shape=out_shape,
        in_specs=[smem()] + [vmem()] * (len(operands) - 1),
        out_specs=(vmem(),) * len(out_shape),
        input_output_aliases={} if first else {start + n: n for n in range(4)},
        compiler_params=params(12),
        cost_estimate=pl.CostEstimate(
            flops=2 * len(rows) * 512 * tiles * TILE * E * weight,
            bytes_accessed=tiles * TILE * E * 2 * weight,
            transcendentals=len(rows) * 512 * tiles * TILE * weight,
        ),
        name=name,
    )(*operands)


def totals_kernel(info_ref, *refs):
    row_refs, col_refs, (arow_ref, acol_ref, loss_ref, recips, col_recips) = refs[:2], refs[2:4], refs[4:]
    recips[...] = 1.0 / (row_refs[0][...] + row_refs[1][...])
    both = col_refs[0][...] + col_refs[1][...]
    totals = both[:16]
    col_recips[...] = 1.0 / totals
    logs = jnp.sum(jnp.sum(jnp.log(totals), axis=0, keepdims=True), axis=1, keepdims=True)
    loss = jnp.broadcast_to(logs, (1, 128)) - both[16:17, :128]
    loss_ref[...] = in_parts(jnp.concatenate([loss] * (E // 128), axis=1))
    for start, at in row_blocks(info_ref):
        line = recips[pl.ds(at, 1), :]
        arow_ref[start : start + ROWS] = jnp.broadcast_to(line, (128, ROWS)).T.astype(BF16)
    for n, at in enumerate(col_blocks(info_ref)):
        line = col_recips[pl.ds(at, 1), :]
        acol_ref[2 * n : 2 * n + 1] = line[:, :128]
        acol_ref[2 * n + 1 : 2 * n + 2] = line[:, 128:]


def make_totals(info, by_row, by_col):
    return pl.pallas_call(
        totals_kernel,
        out_shape=(
            jax.ShapeDtypeStruct((ALL_ROWS, 128), BF16),
            jax.ShapeDtypeStruct((32, 128), F32),
            jax.ShapeDtypeStruct((16, E), BF16),
        ),
        in_specs=[smem()] + [vmem()] * 4,
        out_specs=(vmem(), vmem(), vmem()),
        scratch_shapes=[pltpu.VMEM((8, ROWS), F32), pltpu.VMEM((16, ROWS), F32)],
        compiler_params=params(4),
        name="totals",
    )(info, *by_row, *by_col)


def grads_kernel(pieces, adds, carries, acol_ref, arow_ref, exps_ref, unit_ref, *refs):
    if adds is not None:
        add_ref, refs = refs[0], refs[1:]
    if carries:
        carry_ref, refs = refs[0], refs[1:]
        end = refs[0].shape[0]
        refs[0][end - 16 : end] = carry_ref[carry_ref.shape[0] - 16 : carry_ref.shape[0]]
    cols = [acol_ref[g : g + 1].astype(BF16) for g in range(COLS // 128)]

    def weights(here):
        a = arow_ref[here]
        return exps_ref[here] * jnp.concatenate([a + col for col in cols], axis=1)

    if adds is None:
        to = 0
        for start, size in pieces:
            w = weights(slice(start, start + size))
            product = lax.dot_general(w, unit_ref[...], NN, preferred_element_type=F32)
            refs[0][to : to + size] = product.astype(refs[0].dtype)
            to += size

    else:
        w = jnp.concatenate([weights(slice(start, start + size)) for start, size in pieces], axis=0)
        product = lax.dot_general(w, unit_ref[...], NN, preferred_element_type=F32)
        start = 0
        for (_, size), add, ref in zip(pieces, adds, refs):
            ref[:size] = (product[start : start + size] + add_ref[add : add + size].astype(F32)).astype(ref.dtype)
            start += size


def make_grads(pieces, adds, dtypes, token, acol, arow, exps, unit, add, carry, name):
    count = sum(size for _, size in pieces)
    sizes = [count] if adds is None else [size for _, size in pieces]
    if carry is not None:
        sizes[0] += 16
    exps = pltpu.with_memory_space_constraint(exps, pltpu.VMEM)
    unit = pltpu.with_memory_space_constraint(unit, pltpu.VMEM)
    operands = [after(acol, token), arow, exps, unit]
    operands += [] if adds is None else [add]
    operands += [] if carry is None else [carry]
    return pl.pallas_call(
        functools.partial(grads_kernel, pieces, adds, carry is not None),
        out_shape=tuple(jax.ShapeDtypeStruct((size, E), dtype) for size, dtype in zip(sizes, dtypes)),
        in_specs=[vmem()] * len(operands),
        out_specs=(vmem(),) * len(sizes),
        compiler_params=params(16),
        cost_estimate=pl.CostEstimate(
            flops=2 * count * COLS * E,
            bytes_accessed=COLS * (count + E) * 2,
            transcendentals=0,
        ),
        name=name,
    )(*operands)


def far_kernel(raw_ref, core_ref, loss_ref, out_ref):
    out_ref[:ROWS] = (raw_ref[...] + core_ref[256:512].astype(F32)).astype(BF16)
    out_ref[ROWS:] = in_parts(of_parts(loss_ref[...]) + of_parts(core_ref[768:]))


def two_kernel(held_ref, far_ref, out_ref):
    out_ref[:ROWS] = (held_ref[...] + far_ref[:ROWS].astype(F32)).astype(BF16)
    out_ref[ROWS:] = far_ref[ROWS:]


def make_sum(kernel, operands, name):
    return pl.pallas_call(
        kernel,
        out_shape=jax.ShapeDtypeStruct((ROWS + 16, E), BF16),
        in_specs=[vmem()] * len(operands),
        out_specs=vmem(),
        compiler_params=params(4),
        name=name,
    )(*operands)


def final_kernel(z_ref, mates_ref, own_ref, one_ref, two_ref, here_ref, passed_ref, grad_ref, loss_ref):
    zf = z_ref[...].astype(F32)
    recip = lax.rsqrt(jnp.sum(zf * zf, axis=1, keepdims=True) + 1e-06)
    unit = zf * recip
    acc = own_ref[...] + one_ref[:ROWS].astype(F32) + two_ref[:ROWS].astype(F32)
    grad_unit = INV_TAU * (acc - 2.0 * mates_ref[...].astype(F32))
    along = jnp.sum(unit * grad_unit, axis=1, keepdims=True)
    grad_ref[...] = recip * (grad_unit - unit * along)
    loss = ring_sum(*[of_parts(ref[ROWS:]) for ref in (here_ref, passed_ref, one_ref, two_ref)])
    loss_ref[...] = loss[:, :1] / (ROWS * 128)


def make_final(operands):
    return pl.pallas_call(
        final_kernel,
        out_shape=(jax.ShapeDtypeStruct((ROWS, E), F32), jax.ShapeDtypeStruct((1, 1), F32)),
        in_specs=[vmem()] * len(operands),
        out_specs=(vmem(), vmem()),
        compiler_params=params(4),
        name="final",
    )(*operands)


def per_device(embeds, partner):
    unit, scaled = make_unit(embeds)
    core_id = lax.axis_index("core")
    z = lax.axis_index("zhi") * 2 + lax.axis_index("zlo")
    info = jnp.stack([lax.axis_index("x"), lax.axis_index("y"), z, core_id]).astype(jnp.int32)

    z_one = get(scaled, z_own=-1)
    before, next_ = get(unit, first=-1), get(unit, first=1)
    before, next_ = lax.optimization_barrier((before, next_))
    far = get(unit, first=2)
    near = jnp.concatenate([scaled, z_one], axis=0)
    line0 = jnp.concatenate([after(unit, near), before], axis=0)
    line1 = jnp.concatenate([next_, far], axis=0)
    before0, after0 = get(line0, second=-1), get(line0, second=1)
    before1, after1 = get(line1, second=-1), get(line1, second=1)
    z_two = get(scaled, z_own=1)
    z_far = get(z_one, z_own=-1)
    near = [near, get(near, core=1)]

    mates, positive = make_mates(unit, partner)
    chain = make_exps(info, near, (0,), [line0, line1], (0, 1), (), None, None, 16, "exps0")
    rest = jnp.concatenate([z_two, z_far], axis=0)
    rest = [rest, get(after(rest, chain[0]), core=1)]
    chain = make_exps(info, near, (0,), [before0, after0], (2, 4), (), chain, None, 16, "exps1")
    far0 = get(after(before0, after0, chain[0]), second=-1)
    chain = make_exps(info, rest, (1,), [line0, line1], (0, 1), (), chain, None, 16, "exps2")
    far1 = get(after(after1, before1, chain[0]), second=1)
    rows = near + rest
    cols = [before0, after0, before1, after1]
    chain = make_exps(info, rows, (0, 1), cols, (2, 4, 3, 5), (0, 1), chain, None, 8, "exps3")
    chain = make_exps(info, rows, (0, 1), [far0], (6,), (), chain, None, 4, "exps4")
    chain = make_exps(info, rows, (0, 1), [far1], (7,), (), chain, positive, 4, "exps5")
    _, _, exps, units, sums, col_sums = chain

    by_row = sums + get(sums, core=1)
    by_col = col_sums + swap(col_sums, "first", 0)
    by_col = by_col + swap(after(by_col, by_row), "first", 1)
    by_row = by_row + swap(by_row, "z", 0)
    by_col = by_col + swap(by_col, "second", 0)
    by_col = after(by_col, by_row)
    by_row = [by_row, swap(by_row, "z", 1)]
    by_col = [by_col, swap(by_col, "second", 1)]
    arow, acol, loss = make_totals(info, by_row, by_col)

    given = (acol, arow, exps, units)
    (theirs,) = make_grads(((1536, 512), (768, ROWS)), None, (BF16,), info, *given, None, loss, "grads_core")
    core = get(theirs, core=1)
    (far,) = make_grads(((1280, ROWS),), None, (F32,), theirs, *given, None, None, "grads_far")
    far = make_sum(far_kernel, (far, core, loss), "sum_far")
    passed = get(far, z_own=-1)
    free, held = make_grads(
        ((256, ROWS), (1024, ROWS)), (512, 0), (BF16, F32), info, *given, core, far, "grads_near"
    )
    one = get(free, z_own=1)
    (theirs,) = make_grads(((512, ROWS),), None, (BF16,), held, *given, None, None, "grads_core_own")
    core = get(theirs, core=1)
    two = make_sum(two_kernel, (held, passed), "sum_two")
    token = two
    two = get(two, z_own=-1)
    (own,) = make_grads(((0, ROWS),), (0,), (F32,), token, *given, core, None, "grads_own")
    grad, loss = make_final((embeds, mates, own, one, two, far, passed))
    return (loss[0, 0], grad)


def solution(mesh):
    torus = Mesh(mesh.devices.reshape(SIZES), AXES)
    return jax.shard_map(
        per_device,
        mesh=torus,
        in_specs=(P(AXES, None), P(AXES)),
        out_specs=(P(), P(AXES, None)),
        check_vma=False,
    )
```

```python
import functools
import math

import jax
import jax.numpy as jnp
from jax import lax
from jax.experimental import pallas as pl
from jax.experimental.pallas import tpu as pltpu
from jax.sharding import Mesh, PartitionSpec as P

INV_TAU = 10.0
EXP_SCALE = INV_TAU * math.log2(math.e)
AXES = ("zlo", "core", "y", "x", "zhi")
SIZES = (2, 2, 4, 4, 2)
OFFSETS = (0, -1, 1, 2)
NT = (((1,), (1,)), ((), ()))
NN = (((1,), (0,)), ((), ()))
ROWS = 256
ALL_ROWS = 2048
COLS = 4096
TILE = 512
MIB = 1024 * 1024
E = 512
BF16 = jnp.bfloat16
F32 = jnp.float32


def place(x, y, z, core):
    return ((((z % 2) * 2 + core) * 4 + y) * 4 + x) * 2 + z // 2


def get(value, z=0, core=0, first=0, second=0, z_own=0):
    pairs = []
    for px in range(4):
        for py in range(4):
            for pz in range(4):
                for pc in range(2):
                    x, y = (first, second) if pc == 0 else (second, first)
                    away = z + (z_own if pc == 0 else -z_own)
                    source = place((px + x) % 4, (py + y) % 4, (pz + away) % 4, pc ^ core)
                    pairs.append((source, place(px, py, pz, pc)))
    return lax.ppermute(value, AXES, pairs)


def swap(value, way, step):
    pairs = []
    for px in range(4):
        for py in range(4):
            for pz in range(4):
                for pc in range(2):
                    at = [px, py, pz]
                    axis = {"z": 2, "first": pc, "second": 1 - pc}[way]
                    at[axis] = at[axis] ^ 1 if step == 0 else 3 - at[axis]
                    pairs.append((place(*at, pc), place(px, py, pz, pc)))
    return lax.ppermute(value, AXES, pairs)


def ring_sum(own, before, after, far):
    return (own + far) + (before + after)


def after(value, *others):
    return lax.optimization_barrier((value, *others))[0]


def vmem():
    return pl.BlockSpec(memory_space=pltpu.VMEM)


def smem():
    return pl.BlockSpec(memory_space=pltpu.SMEM)


def hbm():
    return pl.BlockSpec(memory_space=pltpu.HBM)


def params(mib):
    return pltpu.CompilerParams(vmem_limit_bytes=mib * MIB)


def block_of(z, core):
    return ((z & 1) * 2 + core) * 2 + lax.shift_right_logical(z, 1)


def row_blocks(info_ref):
    for c in range(2):
        core = info_ref[3] ^ c
        up = 1 - 2 * core
        for k, away in enumerate((0, -up, up, 2)):
            yield (k // 2) * 1024 + c * 512 + (k % 2) * ROWS, block_of((info_ref[2] + away) & 3, core)


def col_blocks(info_ref):
    for two in OFFSETS:
        for one in OFFSETS:
            x = info_ref[0] + jnp.where(info_ref[3] == 0, one, two)
            y = info_ref[1] + jnp.where(info_ref[3] == 0, two, one)
            yield (y & 3) * 4 + (x & 3)


def in_parts(value):
    high = value.astype(BF16)
    rest = value - high.astype(F32)
    middle = rest.astype(BF16)
    low = (rest - middle.astype(F32)).astype(BF16)
    rows = [high.astype(F32), middle.astype(F32), low.astype(F32), jnp.zeros((13, value.shape[1]), F32)]
    return jnp.concatenate(rows, axis=0).astype(BF16)


def of_parts(block):
    rows = block.astype(F32)
    return rows[0:1] + (rows[1:2] + rows[2:3])


def unit_kernel(z_ref, unit_ref, scaled_ref):
    zf = z_ref[...].astype(F32)
    recip = lax.rsqrt(jnp.sum(zf * zf, axis=1, keepdims=True) + 1e-06)
    unit = zf * recip
    unit_ref[...] = unit.astype(BF16)
    scaled_ref[...] = (unit * EXP_SCALE).astype(BF16)


def make_unit(embeds):
    return pl.pallas_call(
        unit_kernel,
        out_shape=(jax.ShapeDtypeStruct((ROWS, E), BF16), jax.ShapeDtypeStruct((ROWS, E), BF16)),
        in_specs=[vmem()],
        out_specs=(vmem(), vmem()),
        compiler_params=params(4),
        name="unit",
    )(embeds)


def mates_kernel(unit_ref, partner_ref, mates_ref, positive_ref):
    unit = unit_ref[...]
    ids = lax.broadcasted_iota(jnp.int32, (ROWS, ROWS), 0)
    pick = (ids == (partner_ref[...] & (ROWS - 1))).astype(F32).astype(BF16)
    mates = lax.dot_general(pick, unit, NN, preferred_element_type=F32)
    mates_ref[...] = mates.astype(BF16)
    products = jnp.sum(unit.astype(F32) * mates, axis=0, keepdims=True)
    total = jnp.sum(products, axis=1, keepdims=True) * INV_TAU
    positive_ref[...] = jnp.broadcast_to(total, (1, 128))


def make_mates(unit, partner):
    return pl.pallas_call(
        mates_kernel,
        out_shape=(
            jax.ShapeDtypeStruct((ROWS, E), BF16),
            jax.ShapeDtypeStruct((1, 128), F32),
        ),
        in_specs=[vmem(), vmem()],
        out_specs=(vmem(), vmem()),
        compiler_params=params(4),
        name="mates",
    )(unit, partner.reshape(1, ROWS))


def exps_kernel(places, rows_here, first, last, *refs):
    count = len(places)
    info_ref, refs = refs[0], refs[1:]
    row_refs, refs = refs[: 2 * len(rows_here)], refs[2 * len(rows_here) :]
    col_refs, refs = refs[:count], refs[count:]
    if not first:
        refs = refs[4:]
    if last:
        positive_ref, refs = refs[0], refs[1:]
    sums_ref, col_sums_ref, exps_ref, unit_ref = refs[:4]
    if first:
        sums_ref[...] = jnp.zeros_like(sums_ref)
        col_sums_ref[...] = jnp.zeros_like(col_sums_ref)
    for n, col_ref in enumerate(col_refs):
        if 0 in rows_here:
            start = places[n] * TILE
            unit_ref[start : start + col_ref.shape[0]] = col_ref[...]

        here = slice(places[n] * TILE, places[n] * TILE + TILE)
        by_col = col_sums_ref[:, here]
        for k, ref in enumerate(row_refs):
            start = rows_here[k // 2] * 1024 + (k % 2) * 512
            part = slice(start, start + 512)
            e = jnp.exp2(lax.dot_general(ref[...], col_ref[...], NT, preferred_element_type=F32))
            if first and n == 0 and k == 0:
                i = lax.broadcasted_iota(jnp.int32, (ROWS, TILE), 0)
                j = lax.broadcasted_iota(jnp.int32, (ROWS, TILE), 1)
                e = jnp.concatenate([jnp.where(i == j, 0.0, e[:ROWS]), e[ROWS:]], axis=0)
            exps_ref[part, here] = e.astype(BF16)
            sums_ref[part] += (e[:, :128] + e[:, 128:256]) + (e[:, 256:384] + e[:, 384:])
            by_col += jnp.sum(e.reshape(-1, 8, TILE), axis=0)
        col_sums_ref[:, here] = by_col

    if last:
        line_ref, col_line_ref = refs[4:]
        totals = jnp.sum(sums_ref[...].T, axis=0, keepdims=True)
        for start, at in row_blocks(info_ref):
            line_ref[pl.ds(at, 1), :] = totals[:, start : start + ROWS]
        totals = jnp.sum(col_sums_ref[...], axis=0, keepdims=True)
        col_line_ref[...] = jnp.zeros_like(col_line_ref)
        for n, at in enumerate(col_blocks(info_ref)):
            col_line_ref[pl.ds(at, 1), :] = totals[:, n * ROWS : (n + 1) * ROWS]
        col_line_ref[16:17, 0:128] = positive_ref[...]


def make_exps(info, rows, rows_here, cols, places, chain, positive, weight, name):
    first, last = chain is None, positive is not None
    count = len(cols)
    tiles = sum(c.shape[0] for c in cols) // TILE
    operands = [info, *rows, *cols] + ([] if first else list(chain[:4])) + ([positive] if last else [])
    out_shape = (
        pltpu.VMEM((ALL_ROWS, 128), F32),
        pltpu.VMEM((8, COLS), F32),
        pltpu.VMEM((ALL_ROWS, COLS), BF16),
        pltpu.VMEM((COLS, E), BF16),
    )
    if last:
        out_shape += (jax.ShapeDtypeStruct((8, ROWS), F32), jax.ShapeDtypeStruct((24, ROWS), F32))
    start = 1 + len(rows) + count
    return pl.pallas_call(
        functools.partial(exps_kernel, places, rows_here, first, last),
        out_shape=out_shape,
        in_specs=[smem()] + [vmem()] * (len(operands) - 1),
        out_specs=(vmem(),) * len(out_shape),
        input_output_aliases={} if first else {start + n: n for n in range(4)},
        compiler_params=params(12),
        cost_estimate=pl.CostEstimate(
            flops=2 * len(rows) * 512 * tiles * TILE * E * weight,
            bytes_accessed=tiles * TILE * E * 2 * weight,
            transcendentals=len(rows) * 512 * tiles * TILE * weight,
        ),
        name=name,
    )(*operands)


def totals_kernel(info_ref, *refs):
    row_refs, col_refs, (arow_ref, acol_ref, loss_ref, recips, col_recips) = refs[:2], refs[2:4], refs[4:]
    recips[...] = 1.0 / (row_refs[0][...] + row_refs[1][...])
    both = col_refs[0][...] + col_refs[1][...]
    totals = both[:16]
    col_recips[...] = 1.0 / totals
    logs = jnp.sum(jnp.sum(jnp.log(totals), axis=0, keepdims=True), axis=1, keepdims=True)
    loss = jnp.broadcast_to(logs, (1, 128)) - both[16:17, :128]
    loss_ref[...] = in_parts(jnp.concatenate([loss] * (E // 128), axis=1))
    for start, at in row_blocks(info_ref):
        line = recips[pl.ds(at, 1), :]
        arow_ref[start : start + ROWS] = jnp.broadcast_to(line, (128, ROWS)).T.astype(BF16)
    for n, at in enumerate(col_blocks(info_ref)):
        line = col_recips[pl.ds(at, 1), :]
        acol_ref[2 * n : 2 * n + 1] = line[:, :128]
        acol_ref[2 * n + 1 : 2 * n + 2] = line[:, 128:]


def make_totals(info, by_row, by_col):
    return pl.pallas_call(
        totals_kernel,
        out_shape=(
            jax.ShapeDtypeStruct((ALL_ROWS, 128), BF16),
            jax.ShapeDtypeStruct((32, 128), F32),
            jax.ShapeDtypeStruct((16, E), BF16),
        ),
        in_specs=[smem()] + [vmem()] * 4,
        out_specs=(vmem(), vmem(), vmem()),
        scratch_shapes=[pltpu.VMEM((8, ROWS), F32), pltpu.VMEM((16, ROWS), F32)],
        compiler_params=params(4),
        name="totals",
    )(info, *by_row, *by_col)


def grads_kernel(pieces, adds, carries, acol_ref, arow_ref, exps_ref, unit_ref, *refs):
    if adds is not None:
        add_ref, refs = refs[0], refs[1:]
    if carries:
        carry_ref, refs = refs[0], refs[1:]
        end = refs[0].shape[0]
        refs[0][end - 16 : end] = carry_ref[carry_ref.shape[0] - 16 : carry_ref.shape[0]]
    cols = [acol_ref[g : g + 1].astype(BF16) for g in range(COLS // 128)]

    def weights(here):
        a = arow_ref[here]
        return exps_ref[here] * jnp.concatenate([a + col for col in cols], axis=1)

    if adds is None:
        to = 0
        for start, size in pieces:
            w = weights(slice(start, start + size))
            product = lax.dot_general(w, unit_ref[...], NN, preferred_element_type=F32)
            refs[0][to : to + size] = product.astype(refs[0].dtype)
            to += size

    else:
        w = jnp.concatenate([weights(slice(start, start + size)) for start, size in pieces], axis=0)
        product = lax.dot_general(w, unit_ref[...], NN, preferred_element_type=F32)
        start = 0
        for (_, size), add, ref in zip(pieces, adds, refs):
            ref[:size] = (product[start : start + size] + add_ref[add : add + size].astype(F32)).astype(ref.dtype)
            start += size


def make_grads(pieces, adds, dtypes, token, acol, arow, exps, unit, add, carry, name):
    count = sum(size for _, size in pieces)
    sizes = [count] if adds is None else [size for _, size in pieces]
    if carry is not None:
        sizes[0] += 16
    exps = pltpu.with_memory_space_constraint(exps, pltpu.VMEM)
    unit = pltpu.with_memory_space_constraint(unit, pltpu.VMEM)
    operands = [after(acol, token), arow, exps, unit]
    operands += [] if adds is None else [add]
    operands += [] if carry is None else [carry]
    return pl.pallas_call(
        functools.partial(grads_kernel, pieces, adds, carry is not None),
        out_shape=tuple(jax.ShapeDtypeStruct((size, E), dtype) for size, dtype in zip(sizes, dtypes)),
        in_specs=[vmem()] * len(operands),
        out_specs=(vmem(),) * len(sizes),
        compiler_params=params(16),
        cost_estimate=pl.CostEstimate(
            flops=2 * count * COLS * E,
            bytes_accessed=COLS * (count + E) * 2,
            transcendentals=0,
        ),
        name=name,
    )(*operands)


def far_kernel(raw_ref, core_ref, loss_ref, out_ref):
    out_ref[:ROWS] = (raw_ref[...] + core_ref[256:512].astype(F32)).astype(BF16)
    out_ref[ROWS:] = in_parts(of_parts(loss_ref[...]) + of_parts(core_ref[768:]))


def two_kernel(held_ref, far_ref, out_ref):
    out_ref[:ROWS] = (held_ref[...] + far_ref[:ROWS].astype(F32)).astype(BF16)
    out_ref[ROWS:] = far_ref[ROWS:]


def make_sum(kernel, operands, name):
    return pl.pallas_call(
        kernel,
        out_shape=jax.ShapeDtypeStruct((ROWS + 16, E), BF16),
        in_specs=[vmem()] * len(operands),
        out_specs=vmem(),
        compiler_params=params(4),
        name=name,
    )(*operands)


def final_kernel(z_ref, mates_ref, own_ref, one_ref, two_ref, here_ref, passed_ref, grad_ref, loss_ref):
    zf = z_ref[...].astype(F32)
    recip = lax.rsqrt(jnp.sum(zf * zf, axis=1, keepdims=True) + 1e-06)
    unit = zf * recip
    acc = own_ref[...] + one_ref[:ROWS].astype(F32) + two_ref[:ROWS].astype(F32)
    grad_unit = INV_TAU * (acc - 2.0 * mates_ref[...].astype(F32))
    along = jnp.sum(unit * grad_unit, axis=1, keepdims=True)
    grad_ref[...] = recip * (grad_unit - unit * along)
    loss = ring_sum(*[of_parts(ref[ROWS:]) for ref in (here_ref, passed_ref, one_ref, two_ref)])
    loss_ref[...] = loss[:, :1] / (ROWS * 128)


def make_final(operands):
    return pl.pallas_call(
        final_kernel,
        out_shape=(jax.ShapeDtypeStruct((ROWS, E), F32), jax.ShapeDtypeStruct((1, 1), F32)),
        in_specs=[vmem()] * len(operands),
        out_specs=(vmem(), vmem()),
        compiler_params=params(4),
        name="final",
    )(*operands)


def per_device(embeds, partner):
    unit, scaled = make_unit(embeds)
    core_id = lax.axis_index("core")
    z = lax.axis_index("zhi") * 2 + lax.axis_index("zlo")
    info = jnp.stack([lax.axis_index("x"), lax.axis_index("y"), z, core_id]).astype(jnp.int32)

    z_one = get(scaled, z_own=-1)
    before, next_ = get(unit, first=-1), get(unit, first=1)
    before, next_ = lax.optimization_barrier((before, next_))
    far = get(unit, first=2)
    near = jnp.concatenate([scaled, z_one], axis=0)
    line0 = jnp.concatenate([after(unit, near), before], axis=0)
    line1 = jnp.concatenate([next_, far], axis=0)
    before0, after0 = get(line0, second=-1), get(line0, second=1)
    before1, after1 = get(line1, second=-1), get(line1, second=1)
    z_two = get(scaled, z_own=1)
    z_far = get(z_one, z_own=-1)
    near = [near, get(near, core=1)]

    mates, positive = make_mates(unit, partner)
    chain = make_exps(info, near, (0,), [line0, line1], (0, 1), None, None, 8, "exps0")
    rest = jnp.concatenate([z_two, z_far], axis=0)
    rest = [rest, get(rest, core=1)]
    chain = make_exps(info, rest, (1,), [line0, line1], (0, 1), chain, None, 8, "exps1")
    far0 = get(after(before0, after0, chain[0]), second=-1)
    rows = near + rest
    chain = make_exps(info, rows, (0, 1), [before0], (2,), chain, None, 4, "exps2")
    far1 = get(after(after1, before1, chain[0]), second=1)
    chain = make_exps(info, rows, (0, 1), [after0, before1, after1], (4, 3, 5), chain, None, 0, "exps3")
    chain = make_exps(info, rows, (0, 1), [far0], (6,), chain, None, 0, "exps4")
    chain = make_exps(info, rows, (0, 1), [far1], (7,), chain, positive, 0, "exps5")
    _, _, exps, units, sums, col_sums = chain

    by_row = sums + get(sums, core=1)
    by_col = col_sums + swap(col_sums, "first", 0)
    by_col = by_col + swap(after(by_col, by_row), "first", 1)
    by_row = by_row + swap(by_row, "z", 0)
    by_col = by_col + swap(by_col, "second", 0)
    by_col = after(by_col, by_row)
    by_row = [by_row, swap(by_row, "z", 1)]
    by_col = [by_col, swap(by_col, "second", 1)]
    arow, acol, loss = make_totals(info, by_row, by_col)

    given = (acol, arow, exps, units)
    (theirs,) = make_grads(((1536, 512), (768, ROWS)), None, (BF16,), info, *given, None, loss, "grads_core")
    core = get(theirs, core=1)
    (far,) = make_grads(((1280, ROWS),), None, (F32,), theirs, *given, None, None, "grads_far")
    far = make_sum(far_kernel, (far, core, loss), "sum_far")
    passed = get(far, z_own=-1)
    free, held = make_grads(
        ((256, ROWS), (1024, ROWS)), (512, 0), (BF16, F32), info, *given, core, far, "grads_near"
    )
    one = get(free, z_own=1)
    (theirs,) = make_grads(((512, ROWS),), None, (BF16,), held, *given, None, None, "grads_core_own")
    core = get(theirs, core=1)
    two = make_sum(two_kernel, (held, passed), "sum_two")
    token = two
    two = get(two, z_own=-1)
    (own,) = make_grads(((0, ROWS),), (0,), (F32,), token, *given, core, None, "grads_own")
    grad, loss = make_final((embeds, mates, own, one, two, far, passed))
    return (loss[0, 0], grad)


def solution(mesh):
    torus = Mesh(mesh.devices.reshape(SIZES), AXES)
    return jax.shard_map(
        per_device,
        mesh=torus,
        in_specs=(P(AXES, None), P(AXES)),
        out_specs=(P(), P(AXES, None)),
        check_vma=False,
    )
```

```python
import functools
import math

import jax
import jax.numpy as jnp
from jax import lax
from jax.experimental import pallas as pl
from jax.experimental.pallas import tpu as pltpu
from jax.sharding import Mesh, PartitionSpec as P

INV_TAU = 10.0
EXP_SCALE = INV_TAU * math.log2(math.e)
AXES = ("zlo", "core", "y", "x", "zhi")
SIZES = (2, 2, 4, 4, 2)
OFFSETS = (0, -1, 1, 2)
NT = (((1,), (1,)), ((), ()))
NN = (((1,), (0,)), ((), ()))
ROWS = 256
ALL_ROWS = 2048
COLS = 4096
TILE = 512
MIB = 1024 * 1024
E = 512
BF16 = jnp.bfloat16
F32 = jnp.float32


def place(x, y, z, core):
    return ((((z % 2) * 2 + core) * 4 + y) * 4 + x) * 2 + z // 2


def get(value, z=0, core=0, first=0, second=0, z_own=0):
    pairs = []
    for px in range(4):
        for py in range(4):
            for pz in range(4):
                for pc in range(2):
                    x, y = (first, second) if pc == 0 else (second, first)
                    away = z + (z_own if pc == 0 else -z_own)
                    source = place((px + x) % 4, (py + y) % 4, (pz + away) % 4, pc ^ core)
                    pairs.append((source, place(px, py, pz, pc)))
    return lax.ppermute(value, AXES, pairs)


def swap(value, way, step):
    pairs = []
    for px in range(4):
        for py in range(4):
            for pz in range(4):
                for pc in range(2):
                    at = [px, py, pz]
                    axis = {"z": 2, "first": pc, "second": 1 - pc}[way]
                    at[axis] = at[axis] ^ 1 if step == 0 else 3 - at[axis]
                    pairs.append((place(*at, pc), place(px, py, pz, pc)))
    return lax.ppermute(value, AXES, pairs)


def ring_sum(own, before, after, far):
    return (own + far) + (before + after)


def after(value, *others):
    return lax.optimization_barrier((value, *others))[0]


def vmem():
    return pl.BlockSpec(memory_space=pltpu.VMEM)


def smem():
    return pl.BlockSpec(memory_space=pltpu.SMEM)


def hbm():
    return pl.BlockSpec(memory_space=pltpu.HBM)


def params(mib):
    return pltpu.CompilerParams(vmem_limit_bytes=mib * MIB)


def block_of(z, core):
    return ((z & 1) * 2 + core) * 2 + lax.shift_right_logical(z, 1)


def row_blocks(info_ref):
    for c in range(2):
        core = info_ref[3] ^ c
        up = 1 - 2 * core
        for k, away in enumerate((0, -up, up, 2)):
            yield (k // 2) * 1024 + c * 512 + (k % 2) * ROWS, block_of((info_ref[2] + away) & 3, core)


def col_blocks(info_ref):
    for two in OFFSETS:
        for one in OFFSETS:
            x = info_ref[0] + jnp.where(info_ref[3] == 0, one, two)
            y = info_ref[1] + jnp.where(info_ref[3] == 0, two, one)
            yield (y & 3) * 4 + (x & 3)


def in_parts(value):
    high = value.astype(BF16)
    rest = value - high.astype(F32)
    middle = rest.astype(BF16)
    low = (rest - middle.astype(F32)).astype(BF16)
    rows = [high.astype(F32), middle.astype(F32), low.astype(F32), jnp.zeros((13, value.shape[1]), F32)]
    return jnp.concatenate(rows, axis=0).astype(BF16)


def of_parts(block):
    rows = block.astype(F32)
    return rows[0:1] + (rows[1:2] + rows[2:3])


def unit_kernel(z_ref, unit_ref, scaled_ref):
    zf = z_ref[...].astype(F32)
    recip = lax.rsqrt(jnp.sum(zf * zf, axis=1, keepdims=True) + 1e-06)
    unit = zf * recip
    unit_ref[...] = unit.astype(BF16)
    scaled_ref[...] = (unit * EXP_SCALE).astype(BF16)


def make_unit(embeds):
    return pl.pallas_call(
        unit_kernel,
        out_shape=(jax.ShapeDtypeStruct((ROWS, E), BF16), jax.ShapeDtypeStruct((ROWS, E), BF16)),
        in_specs=[vmem()],
        out_specs=(vmem(), vmem()),
        compiler_params=params(4),
        name="unit",
    )(embeds)


def mates_kernel(unit_ref, partner_ref, mates_ref, positive_ref):
    unit = unit_ref[...]
    ids = lax.broadcasted_iota(jnp.int32, (ROWS, ROWS), 0)
    pick = (ids == (partner_ref[...] & (ROWS - 1))).astype(F32).astype(BF16)
    mates = lax.dot_general(pick, unit, NN, preferred_element_type=F32)
    mates_ref[...] = mates.astype(BF16)
    products = jnp.sum(unit.astype(F32) * mates, axis=0, keepdims=True)
    total = jnp.sum(products, axis=1, keepdims=True) * INV_TAU
    positive_ref[...] = jnp.broadcast_to(total, (1, 128))


def make_mates(unit, partner):
    return pl.pallas_call(
        mates_kernel,
        out_shape=(
            jax.ShapeDtypeStruct((ROWS, E), BF16),
            jax.ShapeDtypeStruct((1, 128), F32),
        ),
        in_specs=[vmem(), vmem()],
        out_specs=(vmem(), vmem()),
        compiler_params=params(4),
        name="mates",
    )(unit, partner.reshape(1, ROWS))


def exps_kernel(places, rows_here, first, last, *refs):
    count = len(places)
    info_ref, refs = refs[0], refs[1:]
    row_refs, refs = refs[: 2 * len(rows_here)], refs[2 * len(rows_here) :]
    col_refs, refs = refs[:count], refs[count:]
    if not first:
        refs = refs[4:]
    if last:
        positive_ref, refs = refs[0], refs[1:]
    sums_ref, col_sums_ref, exps_ref, unit_ref = refs[:4]
    if first:
        sums_ref[...] = jnp.zeros_like(sums_ref)
        col_sums_ref[...] = jnp.zeros_like(col_sums_ref)
    for n, col_ref in enumerate(col_refs):
        if 0 in rows_here:
            start = places[n] * TILE
            unit_ref[start : start + col_ref.shape[0]] = col_ref[...]

        here = slice(places[n] * TILE, places[n] * TILE + TILE)
        by_col = col_sums_ref[:, here]
        for k, ref in enumerate(row_refs):
            start = rows_here[k // 2] * 1024 + (k % 2) * 512
            part = slice(start, start + 512)
            e = jnp.exp2(lax.dot_general(ref[...], col_ref[...], NT, preferred_element_type=F32))
            if first and n == 0 and k == 0:
                i = lax.broadcasted_iota(jnp.int32, (ROWS, TILE), 0)
                j = lax.broadcasted_iota(jnp.int32, (ROWS, TILE), 1)
                e = jnp.concatenate([jnp.where(i == j, 0.0, e[:ROWS]), e[ROWS:]], axis=0)
            exps_ref[part, here] = e.astype(BF16)
            sums_ref[part] += (e[:, :128] + e[:, 128:256]) + (e[:, 256:384] + e[:, 384:])
            by_col += jnp.sum(e.reshape(-1, 8, TILE), axis=0)
        col_sums_ref[:, here] = by_col

    if last:
        line_ref, col_line_ref = refs[4:]
        totals = jnp.sum(sums_ref[...].T, axis=0, keepdims=True)
        for start, at in row_blocks(info_ref):
            line_ref[pl.ds(at, 1), :] = totals[:, start : start + ROWS]
        totals = jnp.sum(col_sums_ref[...], axis=0, keepdims=True)
        col_line_ref[...] = jnp.zeros_like(col_line_ref)
        for n, at in enumerate(col_blocks(info_ref)):
            col_line_ref[pl.ds(at, 1), :] = totals[:, n * ROWS : (n + 1) * ROWS]
        col_line_ref[16:17, 0:128] = positive_ref[...]


def make_exps(info, rows, rows_here, cols, places, chain, positive, weight, name):
    first, last = chain is None, positive is not None
    count = len(cols)
    tiles = sum(c.shape[0] for c in cols) // TILE
    operands = [info, *rows, *cols] + ([] if first else list(chain[:4])) + ([positive] if last else [])
    out_shape = (
        pltpu.VMEM((ALL_ROWS, 128), F32),
        pltpu.VMEM((8, COLS), F32),
        pltpu.VMEM((ALL_ROWS, COLS), BF16),
        pltpu.VMEM((COLS, E), BF16),
    )
    if last:
        out_shape += (jax.ShapeDtypeStruct((8, ROWS), F32), jax.ShapeDtypeStruct((24, ROWS), F32))
    start = 1 + len(rows) + count
    return pl.pallas_call(
        functools.partial(exps_kernel, places, rows_here, first, last),
        out_shape=out_shape,
        in_specs=[smem()] + [vmem()] * (len(operands) - 1),
        out_specs=(vmem(),) * len(out_shape),
        input_output_aliases={} if first else {start + n: n for n in range(4)},
        compiler_params=params(12),
        cost_estimate=pl.CostEstimate(
            flops=2 * len(rows) * 512 * tiles * TILE * E * weight,
            bytes_accessed=tiles * TILE * E * 2 * weight,
            transcendentals=len(rows) * 512 * tiles * TILE * weight,
        ),
        name=name,
    )(*operands)


def totals_kernel(info_ref, *refs):
    row_refs, col_refs, (arow_ref, acol_ref, loss_ref, recips, col_recips) = refs[:2], refs[2:4], refs[4:]
    recips[...] = 1.0 / (row_refs[0][...] + row_refs[1][...])
    both = col_refs[0][...] + col_refs[1][...]
    totals = both[:16]
    col_recips[...] = 1.0 / totals
    logs = jnp.sum(jnp.sum(jnp.log(totals), axis=0, keepdims=True), axis=1, keepdims=True)
    loss = jnp.broadcast_to(logs, (1, 128)) - both[16:17, :128]
    loss_ref[...] = in_parts(jnp.concatenate([loss] * (E // 128), axis=1))
    for start, at in row_blocks(info_ref):
        line = recips[pl.ds(at, 1), :]
        arow_ref[start : start + ROWS] = jnp.broadcast_to(line, (128, ROWS)).T.astype(BF16)
    for n, at in enumerate(col_blocks(info_ref)):
        line = col_recips[pl.ds(at, 1), :]
        acol_ref[2 * n : 2 * n + 1] = line[:, :128]
        acol_ref[2 * n + 1 : 2 * n + 2] = line[:, 128:]


def make_totals(info, by_row, by_col):
    return pl.pallas_call(
        totals_kernel,
        out_shape=(
            jax.ShapeDtypeStruct((ALL_ROWS, 128), BF16),
            jax.ShapeDtypeStruct((32, 128), F32),
            jax.ShapeDtypeStruct((16, E), BF16),
        ),
        in_specs=[smem()] + [vmem()] * 4,
        out_specs=(vmem(), vmem(), vmem()),
        scratch_shapes=[pltpu.VMEM((8, ROWS), F32), pltpu.VMEM((16, ROWS), F32)],
        compiler_params=params(4),
        name="totals",
    )(info, *by_row, *by_col)


def grads_kernel(pieces, adds, carries, acol_ref, arow_ref, exps_ref, unit_ref, *refs):
    if adds is not None:
        add_ref, refs = refs[0], refs[1:]
    if carries:
        carry_ref, refs = refs[0], refs[1:]
        end = refs[0].shape[0]
        refs[0][end - 16 : end] = carry_ref[carry_ref.shape[0] - 16 : carry_ref.shape[0]]
    cols = [acol_ref[g : g + 1].astype(BF16) for g in range(COLS // 128)]

    def weights(here):
        a = arow_ref[here]
        return exps_ref[here] * jnp.concatenate([a + col for col in cols], axis=1)

    if adds is None:
        to = 0
        for start, size in pieces:
            w = weights(slice(start, start + size))
            product = lax.dot_general(w, unit_ref[...], NN, preferred_element_type=F32)
            refs[0][to : to + size] = product.astype(refs[0].dtype)
            to += size

    else:
        w = jnp.concatenate([weights(slice(start, start + size)) for start, size in pieces], axis=0)
        product = lax.dot_general(w, unit_ref[...], NN, preferred_element_type=F32)
        start = 0
        for (_, size), add, ref in zip(pieces, adds, refs):
            ref[:size] = (product[start : start + size] + add_ref[add : add + size].astype(F32)).astype(ref.dtype)
            start += size


def make_grads(pieces, adds, dtypes, token, acol, arow, exps, unit, add, carry, name):
    count = sum(size for _, size in pieces)
    sizes = [count] if adds is None else [size for _, size in pieces]
    if carry is not None:
        sizes[0] += 16
    exps = pltpu.with_memory_space_constraint(exps, pltpu.VMEM)
    unit = pltpu.with_memory_space_constraint(unit, pltpu.VMEM)
    operands = [after(acol, token), arow, exps, unit]
    operands += [] if adds is None else [add]
    operands += [] if carry is None else [carry]
    return pl.pallas_call(
        functools.partial(grads_kernel, pieces, adds, carry is not None),
        out_shape=tuple(jax.ShapeDtypeStruct((size, E), dtype) for size, dtype in zip(sizes, dtypes)),
        in_specs=[vmem()] * len(operands),
        out_specs=(vmem(),) * len(sizes),
        compiler_params=params(16),
        cost_estimate=pl.CostEstimate(
            flops=2 * count * COLS * E,
            bytes_accessed=COLS * (count + E) * 2,
            transcendentals=0,
        ),
        name=name,
    )(*operands)


def far_kernel(raw_ref, core_ref, loss_ref, out_ref):
    out_ref[:ROWS] = (raw_ref[...] + core_ref[256:512].astype(F32)).astype(BF16)
    out_ref[ROWS:] = in_parts(of_parts(loss_ref[...]) + of_parts(core_ref[768:]))


def two_kernel(held_ref, far_ref, out_ref):
    out_ref[:ROWS] = (held_ref[...] + far_ref[:ROWS].astype(F32)).astype(BF16)
    out_ref[ROWS:] = far_ref[ROWS:]


def make_sum(kernel, operands, name):
    return pl.pallas_call(
        kernel,
        out_shape=jax.ShapeDtypeStruct((ROWS + 16, E), BF16),
        in_specs=[vmem()] * len(operands),
        out_specs=vmem(),
        compiler_params=params(4),
        name=name,
    )(*operands)


def final_kernel(z_ref, mates_ref, own_ref, one_ref, two_ref, here_ref, passed_ref, grad_ref, loss_ref):
    zf = z_ref[...].astype(F32)
    recip = lax.rsqrt(jnp.sum(zf * zf, axis=1, keepdims=True) + 1e-06)
    unit = zf * recip
    acc = own_ref[...] + one_ref[:ROWS].astype(F32) + two_ref[:ROWS].astype(F32)
    grad_unit = INV_TAU * (acc - 2.0 * mates_ref[...].astype(F32))
    along = jnp.sum(unit * grad_unit, axis=1, keepdims=True)
    grad_ref[...] = recip * (grad_unit - unit * along)
    loss = ring_sum(*[of_parts(ref[ROWS:]) for ref in (here_ref, passed_ref, one_ref, two_ref)])
    loss_ref[...] = loss[:, :1] / (ROWS * 128)


def make_final(operands):
    return pl.pallas_call(
        final_kernel,
        out_shape=(jax.ShapeDtypeStruct((ROWS, E), F32), jax.ShapeDtypeStruct((1, 1), F32)),
        in_specs=[vmem()] * len(operands),
        out_specs=(vmem(), vmem()),
        compiler_params=params(4),
        name="final",
    )(*operands)


def per_device(embeds, partner):
    unit, scaled = make_unit(embeds)
    core_id = lax.axis_index("core")
    z = lax.axis_index("zhi") * 2 + lax.axis_index("zlo")
    info = jnp.stack([lax.axis_index("x"), lax.axis_index("y"), z, core_id]).astype(jnp.int32)

    z_one = get(scaled, z_own=-1)
    before, next_ = get(unit, first=-1), get(unit, first=1)
    before, next_ = lax.optimization_barrier((before, next_))
    far = get(unit, first=2)
    near = jnp.concatenate([scaled, z_one], axis=0)
    line0 = jnp.concatenate([after(unit, near), before], axis=0)
    line1 = jnp.concatenate([next_, far], axis=0)
    before0 = get(line0, second=-1)
    before1, after1 = get(line1, second=-1), get(line1, second=1)
    z_two = get(scaled, z_own=1)
    z_far = get(z_one, z_own=-1)
    near = [near, get(near, core=1)]

    mates, positive = make_mates(unit, partner)
    chain = make_exps(info, near, (0,), [line0, line1], (0, 1), None, None, 8, "exps0")
    after0 = get(after(line0, line1), second=1)
    far1 = get(after(after1, chain[0]), second=1)
    rest = jnp.concatenate([z_two, z_far], axis=0)
    rest = [rest, get(rest, core=1)]
    chain = make_exps(info, rest, (1,), [line0, line1], (0, 1), chain, None, 8, "exps1")
    far0 = get(after(before0, chain[0]), second=-1)
    rows = near + rest
    chain = make_exps(info, rows, (0, 1), [before0, after1], (2, 5), chain, None, 4, "exps2")
    chain = make_exps(info, rows, (0, 1), [before1, after0], (3, 4), chain, None, 0, "exps3")
    chain = make_exps(info, rows, (0, 1), [far0], (6,), chain, None, 0, "exps4")
    chain = make_exps(info, rows, (0, 1), [far1], (7,), chain, positive, 0, "exps5")
    _, _, exps, units, sums, col_sums = chain

    by_row = sums + get(sums, core=1)
    by_col = col_sums + swap(col_sums, "first", 0)
    by_col = by_col + swap(after(by_col, by_row), "first", 1)
    by_row = by_row + swap(by_row, "z", 0)
    by_col = by_col + swap(by_col, "second", 0)
    by_col = after(by_col, by_row)
    by_row = [by_row, swap(by_row, "z", 1)]
    by_col = [by_col, swap(by_col, "second", 1)]
    arow, acol, loss = make_totals(info, by_row, by_col)

    given = (acol, arow, exps, units)
    (theirs,) = make_grads(((1536, 512), (768, ROWS)), None, (BF16,), info, *given, None, loss, "grads_core")
    core = get(theirs, core=1)
    (far,) = make_grads(((1280, ROWS),), None, (F32,), theirs, *given, None, None, "grads_far")
    far = make_sum(far_kernel, (far, core, loss), "sum_far")
    passed = get(far, z_own=-1)
    free, held = make_grads(
        ((256, ROWS), (1024, ROWS)), (512, 0), (BF16, F32), info, *given, core, far, "grads_near"
    )
    one = get(free, z_own=1)
    (theirs,) = make_grads(((512, ROWS),), None, (BF16,), held, *given, None, None, "grads_core_own")
    core = get(theirs, core=1)
    two = make_sum(two_kernel, (held, passed), "sum_two")
    token = two
    two = get(two, z_own=-1)
    (own,) = make_grads(((0, ROWS),), (0,), (F32,), token, *given, core, None, "grads_own")
    grad, loss = make_final((embeds, mates, own, one, two, far, passed))
    return (loss[0, 0], grad)


def solution(mesh):
    torus = Mesh(mesh.devices.reshape(SIZES), AXES)
    return jax.shard_map(
        per_device,
        mesh=torus,
        in_specs=(P(AXES, None), P(AXES)),
        out_specs=(P(), P(AXES, None)),
        check_vma=False,
    )
```

```python
import functools
import math

import jax
import jax.numpy as jnp
from jax import lax
from jax.experimental import pallas as pl
from jax.experimental.pallas import tpu as pltpu
from jax.sharding import Mesh, PartitionSpec as P

INV_TAU = 10.0
EXP_SCALE = INV_TAU * math.log2(math.e)
AXES = ("zlo", "core", "y", "x", "zhi")
SIZES = (2, 2, 4, 4, 2)
OFFSETS = (0, -1, 1, 2)
NT = (((1,), (1,)), ((), ()))
NN = (((1,), (0,)), ((), ()))
ROWS = 256
ALL_ROWS = 2048
COLS = 4096
TILE = 512
MIB = 1024 * 1024
E = 512
BF16 = jnp.bfloat16
F32 = jnp.float32


def place(x, y, z, core):
    return ((((z % 2) * 2 + core) * 4 + y) * 4 + x) * 2 + z // 2


def get(value, z=0, core=0, first=0, second=0, z_own=0):
    pairs = []
    for px in range(4):
        for py in range(4):
            for pz in range(4):
                for pc in range(2):
                    x, y = (first, second) if pc == 0 else (second, first)
                    away = z + (z_own if pc == 0 else -z_own)
                    source = place((px + x) % 4, (py + y) % 4, (pz + away) % 4, pc ^ core)
                    pairs.append((source, place(px, py, pz, pc)))
    return lax.ppermute(value, AXES, pairs)


def swap(value, way, step):
    pairs = []
    for px in range(4):
        for py in range(4):
            for pz in range(4):
                for pc in range(2):
                    at = [px, py, pz]
                    axis = {"z": 2, "first": pc, "second": 1 - pc}[way]
                    at[axis] = at[axis] ^ 1 if step == 0 else 3 - at[axis]
                    pairs.append((place(*at, pc), place(px, py, pz, pc)))
    return lax.ppermute(value, AXES, pairs)


def ring_sum(own, before, after, far):
    return (own + far) + (before + after)


def after(value, *others):
    return lax.optimization_barrier((value, *others))[0]


def vmem():
    return pl.BlockSpec(memory_space=pltpu.VMEM)


def smem():
    return pl.BlockSpec(memory_space=pltpu.SMEM)


def hbm():
    return pl.BlockSpec(memory_space=pltpu.HBM)


def params(mib):
    return pltpu.CompilerParams(vmem_limit_bytes=mib * MIB)


def block_of(z, core):
    return ((z & 1) * 2 + core) * 2 + lax.shift_right_logical(z, 1)


def row_blocks(info_ref):
    for c in range(2):
        core = info_ref[3] ^ c
        up = 1 - 2 * core
        for k, away in enumerate((0, -up, up, 2)):
            yield (k // 2) * 1024 + c * 512 + (k % 2) * ROWS, block_of((info_ref[2] + away) & 3, core)


def col_blocks(info_ref):
    for two in OFFSETS:
        for one in OFFSETS:
            x = info_ref[0] + jnp.where(info_ref[3] == 0, one, two)
            y = info_ref[1] + jnp.where(info_ref[3] == 0, two, one)
            yield (y & 3) * 4 + (x & 3)


def in_parts(value):
    high = value.astype(BF16)
    rest = value - high.astype(F32)
    middle = rest.astype(BF16)
    low = (rest - middle.astype(F32)).astype(BF16)
    rows = [high.astype(F32), middle.astype(F32), low.astype(F32), jnp.zeros((13, value.shape[1]), F32)]
    return jnp.concatenate(rows, axis=0).astype(BF16)


def of_parts(block):
    rows = block.astype(F32)
    return rows[0:1] + (rows[1:2] + rows[2:3])


def unit_kernel(z_ref, unit_ref, scaled_ref):
    zf = z_ref[...].astype(F32)
    recip = lax.rsqrt(jnp.sum(zf * zf, axis=1, keepdims=True) + 1e-06)
    unit = zf * recip
    unit_ref[...] = unit.astype(BF16)
    scaled_ref[...] = (unit * EXP_SCALE).astype(BF16)


def make_unit(embeds):
    return pl.pallas_call(
        unit_kernel,
        out_shape=(jax.ShapeDtypeStruct((ROWS, E), BF16), jax.ShapeDtypeStruct((ROWS, E), BF16)),
        in_specs=[vmem()],
        out_specs=(vmem(), vmem()),
        compiler_params=params(4),
        name="unit",
    )(embeds)


def mates_kernel(unit_ref, partner_ref, mates_ref, positive_ref):
    unit = unit_ref[...]
    ids = lax.broadcasted_iota(jnp.int32, (ROWS, ROWS), 0)
    pick = (ids == (partner_ref[...] & (ROWS - 1))).astype(F32).astype(BF16)
    mates = lax.dot_general(pick, unit, NN, preferred_element_type=F32)
    mates_ref[...] = mates.astype(BF16)
    products = jnp.sum(unit.astype(F32) * mates, axis=0, keepdims=True)
    total = jnp.sum(products, axis=1, keepdims=True) * INV_TAU
    positive_ref[...] = jnp.broadcast_to(total, (1, 128))


def make_mates(unit, partner):
    return pl.pallas_call(
        mates_kernel,
        out_shape=(
            jax.ShapeDtypeStruct((ROWS, E), BF16),
            jax.ShapeDtypeStruct((1, 128), F32),
        ),
        in_specs=[vmem(), vmem()],
        out_specs=(vmem(), vmem()),
        compiler_params=params(4),
        name="mates",
    )(unit, partner.reshape(1, ROWS))


def exps_kernel(places, rows_here, first, last, *refs):
    count = len(places)
    info_ref, refs = refs[0], refs[1:]
    row_refs, refs = refs[: 2 * len(rows_here)], refs[2 * len(rows_here) :]
    col_refs, refs = refs[:count], refs[count:]
    if not first:
        refs = refs[4:]
    if last:
        positive_ref, refs = refs[0], refs[1:]
    sums_ref, col_sums_ref, exps_ref, unit_ref = refs[:4]
    if first:
        sums_ref[...] = jnp.zeros_like(sums_ref)
        col_sums_ref[...] = jnp.zeros_like(col_sums_ref)
    for n, col_ref in enumerate(col_refs):
        if 0 in rows_here:
            start = places[n] * TILE
            unit_ref[start : start + col_ref.shape[0]] = col_ref[...]

        here = slice(places[n] * TILE, places[n] * TILE + TILE)
        by_col = col_sums_ref[:, here]
        for k, ref in enumerate(row_refs):
            start = rows_here[k // 2] * 1024 + (k % 2) * 512
            part = slice(start, start + 512)
            e = jnp.exp2(lax.dot_general(ref[...], col_ref[...], NT, preferred_element_type=F32))
            if first and n == 0 and k == 0:
                i = lax.broadcasted_iota(jnp.int32, (ROWS, TILE), 0)
                j = lax.broadcasted_iota(jnp.int32, (ROWS, TILE), 1)
                e = jnp.concatenate([jnp.where(i == j, 0.0, e[:ROWS]), e[ROWS:]], axis=0)
            exps_ref[part, here] = e.astype(BF16)
            sums_ref[part] += (e[:, :128] + e[:, 128:256]) + (e[:, 256:384] + e[:, 384:])
            by_col += jnp.sum(e.reshape(-1, 8, TILE), axis=0)
        col_sums_ref[:, here] = by_col

    if last:
        line_ref, col_line_ref = refs[4:]
        totals = jnp.sum(sums_ref[...].T, axis=0, keepdims=True)
        for start, at in row_blocks(info_ref):
            line_ref[pl.ds(at, 1), :] = totals[:, start : start + ROWS]
        totals = jnp.sum(col_sums_ref[...], axis=0, keepdims=True)
        col_line_ref[...] = jnp.zeros_like(col_line_ref)
        for n, at in enumerate(col_blocks(info_ref)):
            col_line_ref[pl.ds(at, 1), :] = totals[:, n * ROWS : (n + 1) * ROWS]
        col_line_ref[16:17, 0:128] = positive_ref[...]


def make_exps(info, rows, rows_here, cols, places, chain, positive, weight, name):
    first, last = chain is None, positive is not None
    count = len(cols)
    tiles = sum(c.shape[0] for c in cols) // TILE
    operands = [info, *rows, *cols] + ([] if first else list(chain[:4])) + ([positive] if last else [])
    out_shape = (
        pltpu.VMEM((ALL_ROWS, 128), F32),
        pltpu.VMEM((8, COLS), F32),
        pltpu.VMEM((ALL_ROWS, COLS), BF16),
        pltpu.VMEM((COLS, E), BF16),
    )
    if last:
        out_shape += (jax.ShapeDtypeStruct((8, ROWS), F32), jax.ShapeDtypeStruct((24, ROWS), F32))
    start = 1 + len(rows) + count
    return pl.pallas_call(
        functools.partial(exps_kernel, places, rows_here, first, last),
        out_shape=out_shape,
        in_specs=[smem()] + [vmem()] * (len(operands) - 1),
        out_specs=(vmem(),) * len(out_shape),
        input_output_aliases={} if first else {start + n: n for n in range(4)},
        compiler_params=params(12),
        cost_estimate=pl.CostEstimate(
            flops=2 * len(rows) * 512 * tiles * TILE * E * weight,
            bytes_accessed=tiles * TILE * E * 2 * weight,
            transcendentals=len(rows) * 512 * tiles * TILE * weight,
        ),
        name=name,
    )(*operands)


def totals_kernel(info_ref, *refs):
    row_refs, col_refs, (arow_ref, acol_ref, loss_ref, recips, col_recips) = refs[:2], refs[2:4], refs[4:]
    recips[...] = 1.0 / (row_refs[0][...] + row_refs[1][...])
    both = col_refs[0][...] + col_refs[1][...]
    totals = both[:16]
    col_recips[...] = 1.0 / totals
    logs = jnp.sum(jnp.sum(jnp.log(totals), axis=0, keepdims=True), axis=1, keepdims=True)
    loss = jnp.broadcast_to(logs, (1, 128)) - both[16:17, :128]
    loss_ref[...] = in_parts(jnp.concatenate([loss] * (E // 128), axis=1))
    for start, at in row_blocks(info_ref):
        line = recips[pl.ds(at, 1), :]
        arow_ref[start : start + ROWS] = jnp.broadcast_to(line, (128, ROWS)).T.astype(BF16)
    for n, at in enumerate(col_blocks(info_ref)):
        line = col_recips[pl.ds(at, 1), :]
        acol_ref[2 * n : 2 * n + 1] = line[:, :128]
        acol_ref[2 * n + 1 : 2 * n + 2] = line[:, 128:]


def make_totals(info, by_row, by_col):
    return pl.pallas_call(
        totals_kernel,
        out_shape=(
            jax.ShapeDtypeStruct((ALL_ROWS, 128), BF16),
            jax.ShapeDtypeStruct((32, 128), F32),
            jax.ShapeDtypeStruct((16, E), BF16),
        ),
        in_specs=[smem()] + [vmem()] * 4,
        out_specs=(vmem(), vmem(), vmem()),
        scratch_shapes=[pltpu.VMEM((8, ROWS), F32), pltpu.VMEM((16, ROWS), F32)],
        compiler_params=params(4),
        name="totals",
    )(info, *by_row, *by_col)


def grads_kernel(pieces, adds, carries, acol_ref, arow_ref, exps_ref, unit_ref, *refs):
    if adds is not None:
        add_ref, refs = refs[0], refs[1:]
    if carries:
        carry_ref, refs = refs[0], refs[1:]
        end = refs[0].shape[0]
        refs[0][end - 16 : end] = carry_ref[carry_ref.shape[0] - 16 : carry_ref.shape[0]]
    cols = [acol_ref[g : g + 1].astype(BF16) for g in range(COLS // 128)]

    def weights(here):
        a = arow_ref[here]
        return exps_ref[here] * jnp.concatenate([a + col for col in cols], axis=1)

    if adds is None:
        to = 0
        for start, size in pieces:
            w = weights(slice(start, start + size))
            product = lax.dot_general(w, unit_ref[...], NN, preferred_element_type=F32)
            refs[0][to : to + size] = product.astype(refs[0].dtype)
            to += size

    else:
        w = jnp.concatenate([weights(slice(start, start + size)) for start, size in pieces], axis=0)
        product = lax.dot_general(w, unit_ref[...], NN, preferred_element_type=F32)
        start = 0
        for (_, size), add, ref in zip(pieces, adds, refs):
            ref[:size] = (product[start : start + size] + add_ref[add : add + size].astype(F32)).astype(ref.dtype)
            start += size


def make_grads(pieces, adds, dtypes, token, acol, arow, exps, unit, add, carry, name):
    count = sum(size for _, size in pieces)
    sizes = [count] if adds is None else [size for _, size in pieces]
    if carry is not None:
        sizes[0] += 16
    exps = pltpu.with_memory_space_constraint(exps, pltpu.VMEM)
    unit = pltpu.with_memory_space_constraint(unit, pltpu.VMEM)
    operands = [after(acol, token), arow, exps, unit]
    operands += [] if adds is None else [add]
    operands += [] if carry is None else [carry]
    return pl.pallas_call(
        functools.partial(grads_kernel, pieces, adds, carry is not None),
        out_shape=tuple(jax.ShapeDtypeStruct((size, E), dtype) for size, dtype in zip(sizes, dtypes)),
        in_specs=[vmem()] * len(operands),
        out_specs=(vmem(),) * len(sizes),
        compiler_params=params(16),
        cost_estimate=pl.CostEstimate(
            flops=2 * count * COLS * E,
            bytes_accessed=COLS * (count + E) * 2,
            transcendentals=0,
        ),
        name=name,
    )(*operands)


def far_kernel(raw_ref, core_ref, loss_ref, out_ref):
    out_ref[:ROWS] = (raw_ref[...] + core_ref[256:512].astype(F32)).astype(BF16)
    out_ref[ROWS:] = in_parts(of_parts(loss_ref[...]) + of_parts(core_ref[768:]))


def two_kernel(held_ref, far_ref, out_ref):
    out_ref[:ROWS] = (held_ref[...] + far_ref[:ROWS].astype(F32)).astype(BF16)
    out_ref[ROWS:] = far_ref[ROWS:]


def make_sum(kernel, operands, name):
    return pl.pallas_call(
        kernel,
        out_shape=jax.ShapeDtypeStruct((ROWS + 16, E), BF16),
        in_specs=[vmem()] * len(operands),
        out_specs=vmem(),
        compiler_params=params(4),
        name=name,
    )(*operands)


def final_kernel(z_ref, mates_ref, own_ref, one_ref, two_ref, here_ref, passed_ref, grad_ref, loss_ref):
    zf = z_ref[...].astype(F32)
    recip = lax.rsqrt(jnp.sum(zf * zf, axis=1, keepdims=True) + 1e-06)
    unit = zf * recip
    acc = own_ref[...] + one_ref[:ROWS].astype(F32) + two_ref[:ROWS].astype(F32)
    grad_unit = INV_TAU * (acc - 2.0 * mates_ref[...].astype(F32))
    along = jnp.sum(unit * grad_unit, axis=1, keepdims=True)
    grad_ref[...] = recip * (grad_unit - unit * along)
    loss = ring_sum(*[of_parts(ref[ROWS:]) for ref in (here_ref, passed_ref, one_ref, two_ref)])
    loss_ref[...] = loss[:, :1] / (ROWS * 128)


def make_final(operands):
    return pl.pallas_call(
        final_kernel,
        out_shape=(jax.ShapeDtypeStruct((ROWS, E), F32), jax.ShapeDtypeStruct((1, 1), F32)),
        in_specs=[vmem()] * len(operands),
        out_specs=(vmem(), vmem()),
        compiler_params=params(4),
        name="final",
    )(*operands)


def per_device(embeds, partner):
    unit, scaled = make_unit(embeds)
    core_id = lax.axis_index("core")
    z = lax.axis_index("zhi") * 2 + lax.axis_index("zlo")
    info = jnp.stack([lax.axis_index("x"), lax.axis_index("y"), z, core_id]).astype(jnp.int32)

    z_one = get(scaled, z_own=-1)
    before, next_ = get(unit, first=-1), get(unit, first=1)
    before, next_ = lax.optimization_barrier((before, next_))
    far = get(unit, first=2)
    near = jnp.concatenate([scaled, z_one], axis=0)
    line0 = jnp.concatenate([after(unit, near), before], axis=0)
    line1 = jnp.concatenate([next_, far], axis=0)
    before0 = get(line0, second=-1)
    before1, after1 = get(line1, second=-1), get(line1, second=1)
    z_two = get(scaled, z_own=1)
    z_far = get(z_one, z_own=-1)
    near = [near, get(near, core=1)]

    mates, positive = make_mates(unit, partner)
    chain = make_exps(info, near, (0,), [line0, line1], (0, 1), None, None, 8, "exps0")
    after0 = get(after(line0, line1), second=1)
    far0 = get(after(before0, chain[0]), second=-1)
    far1 = get(after(after1, chain[0]), second=1)
    rest = jnp.concatenate([z_two, z_far], axis=0)
    rest = [rest, get(rest, core=1)]
    chain = make_exps(info, rest, (1,), [line0, line1], (0, 1), chain, None, 8, "exps1")
    rows = near + rest
    chain = make_exps(info, rows, (0, 1), [before0, after1], (2, 5), chain, None, 4, "exps2")
    chain = make_exps(info, rows, (0, 1), [before1, after0], (3, 4), chain, None, 0, "exps3")
    chain = make_exps(info, rows, (0, 1), [far0], (6,), chain, None, 0, "exps4")
    chain = make_exps(info, rows, (0, 1), [far1], (7,), chain, positive, 0, "exps5")
    _, _, exps, units, sums, col_sums = chain

    by_row = sums + get(sums, core=1)
    by_col = col_sums + swap(col_sums, "first", 0)
    by_col = by_col + swap(after(by_col, by_row), "first", 1)
    by_row = by_row + swap(by_row, "z", 0)
    by_col = by_col + swap(by_col, "second", 0)
    by_col = after(by_col, by_row)
    by_row = [by_row, swap(by_row, "z", 1)]
    by_col = [by_col, swap(by_col, "second", 1)]
    arow, acol, loss = make_totals(info, by_row, by_col)

    given = (acol, arow, exps, units)
    (theirs,) = make_grads(((1536, 512), (768, ROWS)), None, (BF16,), info, *given, None, loss, "grads_core")
    core = get(theirs, core=1)
    (far,) = make_grads(((1280, ROWS),), None, (F32,), theirs, *given, None, None, "grads_far")
    far = make_sum(far_kernel, (far, core, loss), "sum_far")
    passed = get(far, z_own=-1)
    free, held = make_grads(
        ((256, ROWS), (1024, ROWS)), (512, 0), (BF16, F32), info, *given, core, far, "grads_near"
    )
    one = get(free, z_own=1)
    (theirs,) = make_grads(((512, ROWS),), None, (BF16,), held, *given, None, None, "grads_core_own")
    core = get(theirs, core=1)
    two = make_sum(two_kernel, (held, passed), "sum_two")
    token = two
    two = get(two, z_own=-1)
    (own,) = make_grads(((0, ROWS),), (0,), (F32,), token, *given, core, None, "grads_own")
    grad, loss = make_final((embeds, mates, own, one, two, far, passed))
    return (loss[0, 0], grad)


def solution(mesh):
    torus = Mesh(mesh.devices.reshape(SIZES), AXES)
    return jax.shard_map(
        per_device,
        mesh=torus,
        in_specs=(P(AXES, None), P(AXES)),
        out_specs=(P(), P(AXES, None)),
        check_vma=False,
    )
```

```python
import functools
import math

import jax
import jax.numpy as jnp
from jax import lax
from jax.experimental import pallas as pl
from jax.experimental.pallas import tpu as pltpu
from jax.sharding import Mesh, PartitionSpec as P

INV_TAU = 10.0
EXP_SCALE = INV_TAU * math.log2(math.e)
AXES = ("zlo", "core", "y", "x", "zhi")
SIZES = (2, 2, 4, 4, 2)
OFFSETS = (0, -1, 1, 2)
NT = (((1,), (1,)), ((), ()))
NN = (((1,), (0,)), ((), ()))
ROWS = 256
ALL_ROWS = 2048
COLS = 4096
TILE = 512
MIB = 1024 * 1024
E = 512
BF16 = jnp.bfloat16
F32 = jnp.float32


def place(x, y, z, core):
    return ((((z % 2) * 2 + core) * 4 + y) * 4 + x) * 2 + z // 2


def get(value, z=0, core=0, first=0, second=0, z_own=0):
    pairs = []
    for px in range(4):
        for py in range(4):
            for pz in range(4):
                for pc in range(2):
                    x, y = (first, second) if pc == 0 else (second, first)
                    away = z + (z_own if pc == 0 else -z_own)
                    source = place((px + x) % 4, (py + y) % 4, (pz + away) % 4, pc ^ core)
                    pairs.append((source, place(px, py, pz, pc)))
    return lax.ppermute(value, AXES, pairs)


def swap(value, way, step):
    pairs = []
    for px in range(4):
        for py in range(4):
            for pz in range(4):
                for pc in range(2):
                    at = [px, py, pz]
                    axis = {"z": 2, "first": pc, "second": 1 - pc}[way]
                    at[axis] = at[axis] ^ 1 if step == 0 else 3 - at[axis]
                    pairs.append((place(*at, pc), place(px, py, pz, pc)))
    return lax.ppermute(value, AXES, pairs)


def ring_sum(own, before, after, far):
    return (own + far) + (before + after)


def after(value, *others):
    return lax.optimization_barrier((value, *others))[0]


def vmem():
    return pl.BlockSpec(memory_space=pltpu.VMEM)


def smem():
    return pl.BlockSpec(memory_space=pltpu.SMEM)


def hbm():
    return pl.BlockSpec(memory_space=pltpu.HBM)


def params(mib):
    return pltpu.CompilerParams(vmem_limit_bytes=mib * MIB)


def block_of(z, core):
    return ((z & 1) * 2 + core) * 2 + lax.shift_right_logical(z, 1)


def row_blocks(info_ref):
    for c in range(2):
        core = info_ref[3] ^ c
        up = 1 - 2 * core
        for k, away in enumerate((0, -up, up, 2)):
            yield (k // 2) * 1024 + c * 512 + (k % 2) * ROWS, block_of((info_ref[2] + away) & 3, core)


def col_blocks(info_ref):
    for two in OFFSETS:
        for one in OFFSETS:
            x = info_ref[0] + jnp.where(info_ref[3] == 0, one, two)
            y = info_ref[1] + jnp.where(info_ref[3] == 0, two, one)
            yield (y & 3) * 4 + (x & 3)


def in_parts(value):
    high = value.astype(BF16)
    rest = value - high.astype(F32)
    middle = rest.astype(BF16)
    low = (rest - middle.astype(F32)).astype(BF16)
    rows = [high.astype(F32), middle.astype(F32), low.astype(F32), jnp.zeros((13, value.shape[1]), F32)]
    return jnp.concatenate(rows, axis=0).astype(BF16)


def of_parts(block):
    rows = block.astype(F32)
    return rows[0:1] + (rows[1:2] + rows[2:3])


def unit_kernel(z_ref, unit_ref, scaled_ref):
    zf = z_ref[...].astype(F32)
    recip = lax.rsqrt(jnp.sum(zf * zf, axis=1, keepdims=True) + 1e-06)
    unit = zf * recip
    unit_ref[...] = unit.astype(BF16)
    scaled_ref[...] = (unit * EXP_SCALE).astype(BF16)


def make_unit(embeds):
    return pl.pallas_call(
        unit_kernel,
        out_shape=(jax.ShapeDtypeStruct((ROWS, E), BF16), jax.ShapeDtypeStruct((ROWS, E), BF16)),
        in_specs=[vmem()],
        out_specs=(vmem(), vmem()),
        compiler_params=params(4),
        name="unit",
    )(embeds)


def mates_kernel(unit_ref, partner_ref, mates_ref, positive_ref):
    unit = unit_ref[...]
    ids = lax.broadcasted_iota(jnp.int32, (ROWS, ROWS), 0)
    pick = (ids == (partner_ref[...] & (ROWS - 1))).astype(F32).astype(BF16)
    mates = lax.dot_general(pick, unit, NN, preferred_element_type=F32)
    mates_ref[...] = mates.astype(BF16)
    products = jnp.sum(unit.astype(F32) * mates, axis=0, keepdims=True)
    total = jnp.sum(products, axis=1, keepdims=True) * INV_TAU
    positive_ref[...] = jnp.broadcast_to(total, (1, 128))


def make_mates(unit, partner):
    return pl.pallas_call(
        mates_kernel,
        out_shape=(
            jax.ShapeDtypeStruct((ROWS, E), BF16),
            jax.ShapeDtypeStruct((1, 128), F32),
        ),
        in_specs=[vmem(), vmem()],
        out_specs=(vmem(), vmem()),
        compiler_params=params(4),
        name="mates",
    )(unit, partner.reshape(1, ROWS))


def exps_kernel(places, rows_here, first, last, *refs):
    count = len(places)
    info_ref, refs = refs[0], refs[1:]
    row_refs, refs = refs[: 2 * len(rows_here)], refs[2 * len(rows_here) :]
    col_refs, refs = refs[:count], refs[count:]
    if not first:
        refs = refs[4:]
    if last:
        positive_ref, refs = refs[0], refs[1:]
    sums_ref, col_sums_ref, exps_ref, unit_ref = refs[:4]
    if first:
        sums_ref[...] = jnp.zeros_like(sums_ref)
        col_sums_ref[...] = jnp.zeros_like(col_sums_ref)
    for n, col_ref in enumerate(col_refs):
        if 0 in rows_here:
            start = places[n] * TILE
            unit_ref[start : start + col_ref.shape[0]] = col_ref[...]

        here = slice(places[n] * TILE, places[n] * TILE + TILE)
        by_col = col_sums_ref[:, here]
        for k, ref in enumerate(row_refs):
            start = rows_here[k // 2] * 1024 + (k % 2) * 512
            part = slice(start, start + 512)
            e = jnp.exp2(lax.dot_general(ref[...], col_ref[...], NT, preferred_element_type=F32))
            if first and n == 0 and k == 0:
                i = lax.broadcasted_iota(jnp.int32, (ROWS, TILE), 0)
                j = lax.broadcasted_iota(jnp.int32, (ROWS, TILE), 1)
                e = jnp.concatenate([jnp.where(i == j, 0.0, e[:ROWS]), e[ROWS:]], axis=0)
            exps_ref[part, here] = e.astype(BF16)
            sums_ref[part] += (e[:, :128] + e[:, 128:256]) + (e[:, 256:384] + e[:, 384:])
            by_col += jnp.sum(e.reshape(-1, 8, TILE), axis=0)
        col_sums_ref[:, here] = by_col

    if last:
        line_ref, col_line_ref = refs[4:]
        totals = jnp.sum(sums_ref[...].T, axis=0, keepdims=True)
        for start, at in row_blocks(info_ref):
            line_ref[pl.ds(at, 1), :] = totals[:, start : start + ROWS]
        totals = jnp.sum(col_sums_ref[...], axis=0, keepdims=True)
        col_line_ref[...] = jnp.zeros_like(col_line_ref)
        for n, at in enumerate(col_blocks(info_ref)):
            col_line_ref[pl.ds(at, 1), :] = totals[:, n * ROWS : (n + 1) * ROWS]
        col_line_ref[16:17, 0:128] = positive_ref[...]


def make_exps(info, rows, rows_here, cols, places, chain, positive, weight, name):
    first, last = chain is None, positive is not None
    count = len(cols)
    tiles = sum(c.shape[0] for c in cols) // TILE
    operands = [info, *rows, *cols] + ([] if first else list(chain[:4])) + ([positive] if last else [])
    out_shape = (
        pltpu.VMEM((ALL_ROWS, 128), F32),
        pltpu.VMEM((8, COLS), F32),
        pltpu.VMEM((ALL_ROWS, COLS), BF16),
        pltpu.VMEM((COLS, E), BF16),
    )
    if last:
        out_shape += (jax.ShapeDtypeStruct((8, ROWS), F32), jax.ShapeDtypeStruct((24, ROWS), F32))
    start = 1 + len(rows) + count
    return pl.pallas_call(
        functools.partial(exps_kernel, places, rows_here, first, last),
        out_shape=out_shape,
        in_specs=[smem()] + [vmem()] * (len(operands) - 1),
        out_specs=(vmem(),) * len(out_shape),
        input_output_aliases={} if first else {start + n: n for n in range(4)},
        compiler_params=params(12),
        cost_estimate=pl.CostEstimate(
            flops=2 * len(rows) * 512 * tiles * TILE * E * weight,
            bytes_accessed=tiles * TILE * E * 2 * weight,
            transcendentals=len(rows) * 512 * tiles * TILE * weight,
        ),
        name=name,
    )(*operands)


def totals_kernel(info_ref, *refs):
    row_refs, col_refs, (arow_ref, acol_ref, loss_ref, recips, col_recips) = refs[:2], refs[2:4], refs[4:]
    recips[...] = 1.0 / (row_refs[0][...] + row_refs[1][...])
    both = col_refs[0][...] + col_refs[1][...]
    totals = both[:16]
    col_recips[...] = 1.0 / totals
    logs = jnp.sum(jnp.sum(jnp.log(totals), axis=0, keepdims=True), axis=1, keepdims=True)
    loss = jnp.broadcast_to(logs, (1, 128)) - both[16:17, :128]
    loss_ref[...] = in_parts(jnp.concatenate([loss] * (E // 128), axis=1))
    for start, at in row_blocks(info_ref):
        line = recips[pl.ds(at, 1), :]
        arow_ref[start : start + ROWS] = jnp.broadcast_to(line, (128, ROWS)).T.astype(BF16)
    for n, at in enumerate(col_blocks(info_ref)):
        line = col_recips[pl.ds(at, 1), :]
        acol_ref[2 * n : 2 * n + 1] = line[:, :128]
        acol_ref[2 * n + 1 : 2 * n + 2] = line[:, 128:]


def make_totals(info, by_row, by_col):
    return pl.pallas_call(
        totals_kernel,
        out_shape=(
            jax.ShapeDtypeStruct((ALL_ROWS, 128), BF16),
            jax.ShapeDtypeStruct((32, 128), F32),
            jax.ShapeDtypeStruct((16, E), BF16),
        ),
        in_specs=[smem()] + [vmem()] * 4,
        out_specs=(vmem(), vmem(), vmem()),
        scratch_shapes=[pltpu.VMEM((8, ROWS), F32), pltpu.VMEM((16, ROWS), F32)],
        compiler_params=params(4),
        name="totals",
    )(info, *by_row, *by_col)


def grads_kernel(pieces, adds, carries, acol_ref, arow_ref, exps_ref, unit_ref, *refs):
    if adds is not None:
        add_ref, refs = refs[0], refs[1:]
    if carries:
        carry_ref, refs = refs[0], refs[1:]
        end = refs[0].shape[0]
        refs[0][end - 16 : end] = carry_ref[carry_ref.shape[0] - 16 : carry_ref.shape[0]]
    cols = [acol_ref[g : g + 1].astype(BF16) for g in range(COLS // 128)]

    def weights(here):
        a = arow_ref[here]
        return exps_ref[here] * jnp.concatenate([a + col for col in cols], axis=1)

    if adds is None:
        to = 0
        for start, size in pieces:
            w = weights(slice(start, start + size))
            product = lax.dot_general(w, unit_ref[...], NN, preferred_element_type=F32)
            refs[0][to : to + size] = product.astype(refs[0].dtype)
            to += size

    else:
        w = jnp.concatenate([weights(slice(start, start + size)) for start, size in pieces], axis=0)
        product = lax.dot_general(w, unit_ref[...], NN, preferred_element_type=F32)
        start = 0
        for (_, size), add, ref in zip(pieces, adds, refs):
            ref[:size] = (product[start : start + size] + add_ref[add : add + size].astype(F32)).astype(ref.dtype)
            start += size


def make_grads(pieces, adds, dtypes, token, acol, arow, exps, unit, add, carry, name):
    count = sum(size for _, size in pieces)
    sizes = [count] if adds is None else [size for _, size in pieces]
    if carry is not None:
        sizes[0] += 16
    exps = pltpu.with_memory_space_constraint(exps, pltpu.VMEM)
    unit = pltpu.with_memory_space_constraint(unit, pltpu.VMEM)
    operands = [after(acol, token), arow, exps, unit]
    operands += [] if adds is None else [add]
    operands += [] if carry is None else [carry]
    return pl.pallas_call(
        functools.partial(grads_kernel, pieces, adds, carry is not None),
        out_shape=tuple(jax.ShapeDtypeStruct((size, E), dtype) for size, dtype in zip(sizes, dtypes)),
        in_specs=[vmem()] * len(operands),
        out_specs=(vmem(),) * len(sizes),
        compiler_params=params(16),
        cost_estimate=pl.CostEstimate(
            flops=2 * count * COLS * E,
            bytes_accessed=COLS * (count + E) * 2,
            transcendentals=0,
        ),
        name=name,
    )(*operands)


def far_kernel(raw_ref, core_ref, loss_ref, out_ref):
    out_ref[:ROWS] = (raw_ref[...] + core_ref[256:512].astype(F32)).astype(BF16)
    out_ref[ROWS:] = in_parts(of_parts(loss_ref[...]) + of_parts(core_ref[768:]))


def two_kernel(held_ref, far_ref, out_ref):
    out_ref[:ROWS] = (held_ref[...] + far_ref[:ROWS].astype(F32)).astype(BF16)
    out_ref[ROWS:] = far_ref[ROWS:]


def make_sum(kernel, operands, name):
    return pl.pallas_call(
        kernel,
        out_shape=jax.ShapeDtypeStruct((ROWS + 16, E), BF16),
        in_specs=[vmem()] * len(operands),
        out_specs=vmem(),
        compiler_params=params(4),
        name=name,
    )(*operands)


def final_kernel(z_ref, mates_ref, own_ref, one_ref, two_ref, here_ref, passed_ref, grad_ref, loss_ref):
    zf = z_ref[...].astype(F32)
    recip = lax.rsqrt(jnp.sum(zf * zf, axis=1, keepdims=True) + 1e-06)
    unit = zf * recip
    acc = own_ref[...] + one_ref[:ROWS].astype(F32) + two_ref[:ROWS].astype(F32)
    grad_unit = INV_TAU * (acc - 2.0 * mates_ref[...].astype(F32))
    along = jnp.sum(unit * grad_unit, axis=1, keepdims=True)
    grad_ref[...] = recip * (grad_unit - unit * along)
    loss = ring_sum(*[of_parts(ref[ROWS:]) for ref in (here_ref, passed_ref, one_ref, two_ref)])
    loss_ref[...] = loss[:, :1] / (ROWS * 128)


def make_final(operands):
    return pl.pallas_call(
        final_kernel,
        out_shape=(jax.ShapeDtypeStruct((ROWS, E), F32), jax.ShapeDtypeStruct((1, 1), F32)),
        in_specs=[vmem()] * len(operands),
        out_specs=(vmem(), vmem()),
        compiler_params=params(4),
        name="final",
    )(*operands)


def per_device(embeds, partner):
    unit, scaled = make_unit(embeds)
    core_id = lax.axis_index("core")
    z = lax.axis_index("zhi") * 2 + lax.axis_index("zlo")
    info = jnp.stack([lax.axis_index("x"), lax.axis_index("y"), z, core_id]).astype(jnp.int32)

    z_one = get(scaled, z_own=-1)
    before, next_ = get(unit, first=-1), get(unit, first=1)
    before, next_ = lax.optimization_barrier((before, next_))
    far = get(unit, first=2)
    near = jnp.concatenate([scaled, z_one], axis=0)
    line0 = jnp.concatenate([after(unit, near), before], axis=0)
    line1 = jnp.concatenate([next_, far], axis=0)
    before0 = get(line0, second=-1)
    before1, after1 = get(line1, second=-1), get(line1, second=1)
    z_two = get(scaled, z_own=1)
    z_far = get(z_one, z_own=-1)
    near = [near, get(near, core=1)]

    mates, positive = make_mates(unit, partner)
    chain = make_exps(info, near, (0,), [line0, line1], (0, 1), None, None, 8, "exps0")
    after0 = get(after(line0, line1), second=1)
    far0 = get(after(before0, chain[0]), second=-1)
    far1 = get(after(after1, chain[0]), second=1)
    rest = jnp.concatenate([z_two, z_far], axis=0)
    rest = [rest, get(rest, core=1)]
    chain = make_exps(info, rest, (1,), [line0, line1], (0, 1), chain, None, 8, "exps1")
    rows = near + rest
    chain = make_exps(info, rows, (0, 1), [before0, after1], (2, 5), chain, None, 4, "exps2")
    chain = make_exps(info, rows, (0, 1), [before1, after0], (3, 4), chain, None, 0, "exps3")
    chain = make_exps(info, rows, (0, 1), [far0, far1], (6, 7), chain, positive, 0, "exps4")
    _, _, exps, units, sums, col_sums = chain

    by_row = sums + get(sums, core=1)
    by_col = col_sums + swap(col_sums, "first", 0)
    by_col = by_col + swap(after(by_col, by_row), "first", 1)
    by_row = by_row + swap(by_row, "z", 0)
    by_col = by_col + swap(by_col, "second", 0)
    by_col = after(by_col, by_row)
    by_row = [by_row, swap(by_row, "z", 1)]
    by_col = [by_col, swap(by_col, "second", 1)]
    arow, acol, loss = make_totals(info, by_row, by_col)

    given = (acol, arow, exps, units)
    (theirs,) = make_grads(((1536, 512), (768, ROWS)), None, (BF16,), info, *given, None, loss, "grads_core")
    core = get(theirs, core=1)
    (far,) = make_grads(((1280, ROWS),), None, (F32,), theirs, *given, None, None, "grads_far")
    far = make_sum(far_kernel, (far, core, loss), "sum_far")
    passed = get(far, z_own=-1)
    free, held = make_grads(
        ((256, ROWS), (1024, ROWS)), (512, 0), (BF16, F32), info, *given, core, far, "grads_near"
    )
    one = get(free, z_own=1)
    (theirs,) = make_grads(((512, ROWS),), None, (BF16,), held, *given, None, None, "grads_core_own")
    core = get(theirs, core=1)
    two = make_sum(two_kernel, (held, passed), "sum_two")
    token = two
    two = get(two, z_own=-1)
    (own,) = make_grads(((0, ROWS),), (0,), (F32,), token, *given, core, None, "grads_own")
    grad, loss = make_final((embeds, mates, own, one, two, far, passed))
    return (loss[0, 0], grad)


def solution(mesh):
    torus = Mesh(mesh.devices.reshape(SIZES), AXES)
    return jax.shard_map(
        per_device,
        mesh=torus,
        in_specs=(P(AXES, None), P(AXES)),
        out_specs=(P(), P(AXES, None)),
        check_vma=False,
    )
```
